512 devices in a mesh: grp: 8 (over y), dev: 64 (over z, x, core).
Axes of the slice: x: 4, y: 8, z: 8, core: 2. Of those that a mesh axis runs over, the one named last changes fastest.
Arguments:
- queries: bfloat16 [512, 64, 576], P(('grp', 'dev')), may hold values from -30 to 30
- lengths: int32 [512], P(('grp', 'dev')), may hold values from 1 to 768, as said below
- pages: bfloat16 [2048, 64, 576], P(('grp', 'dev')), may hold values from -7 to 7
- slot_owner: int32 [2048], P(('grp', 'dev')), may hold values from 0 to 7, as said below
- slot_page: int32 [2048], P(('grp', 'dev')), may hold values from 0 to 11, as said below
- value_up: bfloat16 [64, 512, 128], P('dev'), may hold values from -2 to 2
- out_proj: bfloat16 [8192, 7168], P('dev'), may hold values from -0.0625 to 0.0625
Outputs:
- hidden: bfloat16 [512, 7168], P(('grp', 'dev'))
The draws below stay inside these ranges and needn't reach their ends.
Inputs may be any that keep to these rules, and one draw needn't show every extreme that they name: Request R's pages number ceil(lengths[R] / 64); in every column one request is exactly 768 tokens long. `slot_owner`: every slot holds a page; every page of every request lies in exactly one slot of the request's column, on any of its 8 devices. `slot_page`: page numbers of one request are 0 to its page count - 1, each once.
All inputs are finite; a program needn't handle non-finite values.
Results may differ from the reference program's by a relative error of at most 0.02.
Values may be sent and summed in bfloat16 or wider, within the bound.
A program may use at most 64 MiB of HBM per device.

```python
import jax
import jax.numpy as jnp
from jax import lax

D = 7168
LAT = 512
ROPE = 64
NOPE = 128
VDIM = 128
HEADS = 64
PAGE = 64
POOL = 4
REQ_DEV = 1
CACHE = 576
COLREQ = 8
MAXPG = 12
REQUESTS = 512
SLOTS = 2048
N_GRP = 8
N_DEV = 64


def page_layout(key):
    key = jax.random.fold_in(key, 101)
    column_keys = jax.random.split(key, N_DEV)

    def one_column(column_key):
        key_long, key_weight, key_order, key_tail, key_shuffle = jax.random.split(column_key, 5)
        request_index = jnp.arange(COLREQ, dtype=jnp.int32)
        longest = jax.random.randint(key_long, (), 0, COLREQ, dtype=jnp.int32)
        weight = jax.random.randint(key_weight, (COLREQ,), 1, 5, dtype=jnp.int32)
        weight = jnp.where(request_index == longest, 0, weight)
        spare_pages = N_GRP * POOL - MAXPG - (COLREQ - 1)
        base_part = spare_pages * weight // jnp.maximum(jnp.sum(weight), 1)
        leftover = spare_pages - jnp.sum(base_part)
        priority = jax.random.permutation(key_order, COLREQ).astype(jnp.int32)
        priority = jnp.where(request_index == longest, COLREQ, priority)
        rank_order = jnp.sum((priority[None, :] < priority[:, None]).astype(jnp.int32), axis=1)
        counts = 1 + base_part + (rank_order < leftover).astype(jnp.int32)
        counts = jnp.where(request_index == longest, MAXPG, counts).astype(jnp.int32)
        tail_tokens = jax.random.randint(key_tail, (COLREQ,), 1, PAGE + 1, dtype=jnp.int32)
        tail_tokens = jnp.where(request_index == longest, PAGE, tail_tokens)
        length_col = ((counts - 1) * PAGE + tail_tokens).astype(jnp.int32)
        page_ends = jnp.cumsum(counts).astype(jnp.int32)
        item_index = jnp.arange(N_GRP * POOL, dtype=jnp.int32)
        owner_item = jnp.sum((page_ends[None, :] <= item_index[:, None]).astype(jnp.int32), axis=1)
        page_item = item_index - jnp.take(page_ends - counts, owner_item)
        shuffle = jax.random.permutation(key_shuffle, N_GRP * POOL).astype(jnp.int32)
        return (length_col, jnp.take(owner_item, shuffle), jnp.take(page_item, shuffle))
    length_all, owner_all, page_all = jax.vmap(one_column)(column_keys)
    length_all = length_all.reshape(N_DEV, N_GRP, REQ_DEV).transpose(1, 0, 2).reshape(REQUESTS)
    owner_all = owner_all.reshape(N_DEV, N_GRP, POOL).transpose(1, 0, 2).reshape(SLOTS)
    page_all = page_all.reshape(N_DEV, N_GRP, POOL).transpose(1, 0, 2).reshape(SLOTS)
    return (length_all.astype(jnp.int32), owner_all.astype(jnp.int32), page_all.astype(jnp.int32))


def draw_lengths(key, part):
    return page_layout(key)[0]


def draw_slot_owner(key, part):
    return page_layout(key)[1]


def draw_slot_page(key, part):
    return page_layout(key)[2]


def draw_queries(key, part):
    key = jax.random.fold_in(key, 5)
    key_base = jax.random.fold_in(key, 0)
    full_shape = (REQUESTS, HEADS, CACHE)
    values = jnp.clip(0.9 * jax.random.normal(key_base, full_shape, jnp.float32), -4.5, 4.5)
    return values.astype(jnp.bfloat16)


def draw_pages(key, part):
    key = jax.random.fold_in(key, 6)
    key_base = jax.random.fold_in(key, 0)
    full_shape = (SLOTS, PAGE, CACHE)
    values = jnp.clip(jax.random.normal(key_base, full_shape, jnp.float32), -5.0, 5.0)
    return values.astype(jnp.bfloat16)


def shard_levels(key, dims, shards, least, largest):
    def one(axis_at, shards_of):
        steps = jax.random.uniform(jax.random.fold_in(jax.random.fold_in(key, 6), axis_at), (shards_of,), jnp.float32, least / len(shards), largest / len(shards))
        return jnp.repeat(jnp.exp(steps), dims[axis_at] // shards_of).reshape((-1,) + (1,) * (len(dims) - axis_at - 1))

    loudness = one(*shards[0])
    for cut in shards[1:]:
        loudness = loudness * one(*cut)
    return loudness


def bell_draw(rng, shape, spread, most, cuts=(), kind=jnp.bfloat16):
    values = jax.random.normal(rng, shape, jnp.float32) * spread
    if len(cuts) > 0:
        values = shard_levels(rng, shape, cuts, -0.22, 0.18) * values
    return jnp.clip(values, min=-most, max=most).astype(kind)


def setup_inputs(seed: int = 0) -> dict:
    splits = jax.random.split(jax.random.key(seed), 8)
    return {
        "queries": draw_queries(jax.random.fold_in(splits[7], 71), 0),
        "lengths": draw_lengths(jax.random.fold_in(splits[7], 71), 0),
        "pages": draw_pages(jax.random.fold_in(splits[7], 71), 0),
        "slot_owner": draw_slot_owner(jax.random.fold_in(splits[7], 71), 0),
        "slot_page": draw_slot_page(jax.random.fold_in(splits[7], 71), 0),
        "value_up": bell_draw(splits[5], (HEADS, LAT, VDIM), (max(LAT // 64, 1)) ** -0.5, 2.0, ((0, 64),)),
        "out_proj": bell_draw(splits[6], (HEADS * VDIM, D), (HEADS * VDIM) ** -0.5, 0.0625, ((0, 64),)),
    }


def device_partials(column_queries, column_lengths, dev_pages, owner_ids, page_ids):
    score_scale = (NOPE + ROPE) ** -0.5
    slot_queries = jnp.take(column_queries, owner_ids, axis=0)
    scores = jnp.einsum('shc,spc->shp', slot_queries.astype(jnp.float32), dev_pages.astype(jnp.float32)) * score_scale
    positions = page_ids[:, None] * PAGE + jnp.arange(PAGE, dtype=jnp.int32)[None, :]
    live_tokens = positions < jnp.take(column_lengths, owner_ids, axis=0)[:, None]
    masked = jnp.where(live_tokens[:, None, :], scores, jnp.float32(-1e30))
    slot_max = jnp.max(masked, axis=-1)
    pick_slot = owner_ids[None, :] == jnp.arange(COLREQ, dtype=jnp.int32)[:, None]
    local_max = jnp.max(jnp.where(pick_slot[:, :, None], slot_max[None, :, :], jnp.float32(-1e30)), axis=1)
    shifted = scores - jnp.take(local_max, owner_ids, axis=0)[:, :, None]
    weights = jnp.where(live_tokens[:, None, :], jnp.exp(shifted), jnp.float32(0.0))
    pick_float = pick_slot.astype(jnp.float32)
    local_total = jnp.dot(pick_float, jnp.sum(weights, axis=-1), precision=lax.Precision.HIGHEST)
    weights_bf = weights.astype(jnp.bfloat16)
    slot_value = jnp.einsum('shp,spl->shl', weights_bf.astype(jnp.float32), dev_pages[:, :, :LAT].astype(jnp.float32))
    local_value = jnp.einsum('ks,shl->khl', pick_float, slot_value, precision=lax.Precision.HIGHEST)
    return local_max, local_total, local_value


def reference(queries, lengths, pages, slot_owner, slot_page, value_up, out_proj):
    all_queries = queries.reshape(N_GRP, N_DEV, REQ_DEV, HEADS, CACHE)
    all_lengths = lengths.reshape(N_GRP, N_DEV, REQ_DEV)
    all_pages = pages.reshape(N_GRP, N_DEV, POOL, PAGE, CACHE)
    all_owner = slot_owner.reshape(N_GRP, N_DEV, POOL)
    all_numbers = slot_page.reshape(N_GRP, N_DEV, POOL)

    def one_column(column):
        column_queries = lax.dynamic_index_in_dim(all_queries, column, 1, keepdims=False).reshape(COLREQ, HEADS, CACHE)
        column_lengths = lax.dynamic_index_in_dim(all_lengths, column, 1, keepdims=False).reshape(COLREQ)

        def one_device(storage):
            dev_pages = lax.dynamic_index_in_dim(lax.dynamic_index_in_dim(all_pages, storage, 0, keepdims=False), column, 0, keepdims=False)
            owner_ids = lax.dynamic_index_in_dim(lax.dynamic_index_in_dim(all_owner, storage, 0, keepdims=False), column, 0, keepdims=False)
            page_ids = lax.dynamic_index_in_dim(lax.dynamic_index_in_dim(all_numbers, storage, 0, keepdims=False), column, 0, keepdims=False)
            return device_partials(column_queries, column_lengths, dev_pages, owner_ids, page_ids)

        local_max, local_total, local_value = lax.map(one_device, jnp.arange(N_GRP, dtype=jnp.int32))
        top_score = jnp.max(local_max, axis=0)
        factor = jnp.exp(local_max - top_score[None])
        denominator = jnp.sum(factor * local_total, axis=0)
        weighted = jnp.sum(factor[..., None] * local_value, axis=0)
        return (weighted / denominator[..., None]).astype(jnp.bfloat16)

    latent = lax.map(one_column, jnp.arange(N_DEV, dtype=jnp.int32))
    latent = latent.reshape(N_DEV, N_GRP, REQ_DEV, HEADS, LAT).transpose(1, 0, 2, 3, 4).reshape(REQUESTS, HEADS, LAT)
    head_value = jnp.einsum('rhl,hlv->rhv', latent.astype(jnp.float32), value_up.astype(jnp.float32)).astype(jnp.bfloat16)
    flat_value = head_value.reshape(REQUESTS, HEADS * VDIM)
    return jnp.dot(flat_value, out_proj, preferred_element_type=jnp.float32).astype(jnp.bfloat16)
```

```python
import jax
import jax.numpy as jnp
from jax import lax
from jax.experimental import pallas as pl
from jax.experimental.pallas import tpu as pltpu
from jax.sharding import PartitionSpec as P

MESH = pl.DeviceIdType.MESH
F32 = jnp.float32
BF16 = jnp.bfloat16

ROPE = 64
NOPE = 128
SCALE = (NOPE + ROPE) ** -0.5
NEG = -1e30

GRP = 8
NZ = 8
NS = 8
NX = 4
HEADS = 64
LAT = 512
CACHE = 576
WIDE = 640
PAGE = 64
POOL = 4
TOK = POOL * PAGE
VDIM = 128
D = 7168
HALF = D // 2
TILES = D // 128
CHUNK = 1024
NCH = D // CHUNK


def pieces(value):
    high = value.astype(BF16).astype(F32)
    rest = value - high
    mid = rest.astype(BF16).astype(F32)
    return high, mid, rest - mid


def kernel(q_hbm, len_ref, pages_hbm, owner_ref, page_ref, vup_hbm, oproj_hbm, out_ref,
           q_raw, q_own, q_in, pages, vup, oproj, part_out, part_in,
           c1_out, c1_in, c1_f, c2_out, c2_in,
           own_f, e1_out, e1_in, e2_out, e2_in, e3_f, e3_out, e3_in,
           loc_sem, qs_sem, qr_sem, ps_sem, pr_sem, c1s_sem, c1r_sem, c2s_sem, c2r_sem,
           e1s_sem, e1r_sem, e2s_sem, e2r_sem, e3s_sem, e3r_sem):
    g = lax.axis_index("grp")
    d = lax.axis_index("dev")
    z = d // NS
    s = d % NS
    x = s // 2
    c = s % 2

    def grp_peer(k):
        return (lax.rem(g + k, GRP), d)

    def z_peer(k):
        return (g, lax.rem(z + k, NZ) * NS + s)

    def s_peer(k):
        return (g, z * NS + lax.rem(s + k, NS))

    barrier = pltpu.get_barrier_semaphore()
    for k in range(1, 8):
        for peer in (grp_peer(k), z_peer(k), s_peer(k)):
            pl.semaphore_signal(barrier, inc=1, device_id=peer, device_id_type=MESH)

    q_load = pltpu.make_async_copy(q_hbm.at[0], q_raw, loc_sem.at[0])
    q_load.start()
    pages_load = pltpu.make_async_copy(pages_hbm, pages, loc_sem.at[1])
    pages_load.start()
    vup_load = pltpu.make_async_copy(vup_hbm.at[0], vup, loc_sem.at[2])
    vup_load.start()
    oproj_load = pltpu.make_async_copy(oproj_hbm, oproj, loc_sem.at[3])
    oproj_load.start()

    q_load.wait()
    length = len_ref[0]
    len_high = (length // 32).astype(F32)
    len_low = (length % 32).astype(F32)
    lane64 = lax.broadcasted_iota(jnp.int32, (HEADS, 128), 1)
    tail = jnp.concatenate([q_raw[:, LAT:CACHE].astype(F32), jnp.zeros((HEADS, WIDE - CACHE), F32)], axis=1)
    tail = jnp.where(lane64 == ROPE, len_high, jnp.where(lane64 == ROPE + 1, len_low, tail))
    q_own[:, 0:LAT] = q_raw[:, 0:LAT]
    q_own[:, LAT:WIDE] = tail.astype(BF16)

    pl.semaphore_wait(barrier, 21)

    def remote(src, dst, send, recv, peer):
        copy = pltpu.make_async_remote_copy(
            src_ref=src, dst_ref=dst, send_sem=send, recv_sem=recv,
            device_id=peer, device_id_type=MESH)
        copy.start()
        return copy

    order = (1, 7, 2, 6, 3, 5, 4)
    q_copies = {k: remote(q_own, q_in.at[k], qs_sem.at[k], qr_sem.at[k], grp_peer(k)) for k in order}

    pages_load.wait()
    lane = lax.broadcasted_iota(jnp.int32, (1, TOK), 1)
    slot = lane // PAGE
    owner_v = jnp.zeros((1, TOK), jnp.int32)
    first_v = jnp.zeros((1, TOK), jnp.int32)
    for i in range(POOL):
        owner_v = jnp.where(slot == i, owner_ref[i], owner_v)
        first_v = jnp.where(slot == i, page_ref[i], first_v)
    pos_v = (first_v * PAGE + lane % PAGE).astype(F32)

    def partial(q_ref, request):
        page_all = pages[...].reshape(TOK, CACHE)
        query = q_ref[:, 0:CACHE]
        scores = lax.dot_general(query, page_all, (((1,), (1,)), ((), ())),
                                 preferred_element_type=F32) * SCALE
        side = q_ref[:, LAT:WIDE].astype(F32)
        limit = side[:, ROPE:ROPE + 1] * 32.0 + side[:, ROPE + 1:ROPE + 2]
        live = (pos_v < limit) & (owner_v == request)
        top = jnp.max(jnp.where(live, scores, NEG), axis=1, keepdims=True)
        weights = jnp.where(live, jnp.exp(scores - top), 0.0)
        total = jnp.sum(weights, axis=1, keepdims=True)
        value = jnp.dot(weights.astype(BF16), page_all[:, 0:LAT], preferred_element_type=F32)
        return top, total, value

    part_copies = {}
    for k in order:
        q_copies[k].wait_recv()
        top, total, value = partial(q_in.at[k], lax.rem(g + (GRP - k), GRP))
        part_out[k, :, 0:LAT] = value.astype(BF16)
        top_p = pieces(top)
        total_p = pieces(total)
        stats = jnp.zeros((HEADS, 128), F32)
        for at, piece in enumerate(top_p + total_p):
            stats = jnp.where(lane64 == at, piece, stats)
        part_out[k, :, LAT:WIDE] = stats.astype(BF16)
        part_copies[k] = remote(part_out.at[k], part_in.at[k], ps_sem.at[k], pr_sem.at[k], grp_peer(GRP - k))

    top0, total0, value0 = partial(q_own, g)

    tops, totals = {0: top0}, {0: total0}
    best = top0
    for k in order:
        part_copies[k].wait_recv()
        stats = part_in[k, :, LAT:WIDE].astype(F32)
        tops[k] = (stats[:, 0:1] + stats[:, 1:2]) + stats[:, 2:3]
        totals[k] = (stats[:, 3:4] + stats[:, 4:5]) + stats[:, 5:6]
        best = jnp.maximum(best, tops[k])
    factor = jnp.exp(top0 - best)
    denominator = factor * total0
    merged = factor * value0
    for k in order:
        factor = jnp.exp(tops[k] - best)
        denominator = denominator + factor * totals[k]
        merged = merged + factor * part_in[k, :, 0:LAT].astype(F32)
    latent = merged * (1.0 / denominator)

    for zz in range(NZ):
        rows = latent[zz * NS:(zz + 1) * NS, :]
        c1_out[zz] = jnp.concatenate([rows[:, 0:256], rows[:, 256:512]], axis=0).astype(BF16)
    c1_copies = []
    for k in order:
        to = lax.rem(z + k, NZ)
        c1_copies.append(remote(c1_out.at[to], c1_in.at[z], c1s_sem.at[k], c1r_sem.at[k], z_peer(k)))
    c1_in[z] = c1_out[z]
    for copy in c1_copies:
        copy.wait_recv()
    arrived = c1_in[...].astype(F32).reshape(NZ * 16, 256)
    c1_f[0] = arrived[:, 0:128]
    c1_f[1] = arrived[:, 128:256]
    for ss in range(NS):
        quarters = [[c1_f[col, pl.ds(half * 8 + ss, NZ, stride=16), :] for col in range(2)] for half in range(2)]
        c2_out[ss] = jnp.concatenate([jnp.concatenate(pair, axis=1) for pair in quarters], axis=0).astype(BF16)
    c2_copies = []
    for k in order:
        to = lax.rem(s + k, NS)
        c2_copies.append(remote(c2_out.at[to], c2_in.at[s], c2s_sem.at[k], c2r_sem.at[k], s_peer(k)))
    c2_in[s] = c2_out[s]
    vup_load.wait()
    for copy in c2_copies:
        copy.wait_recv()

    blocks = []
    for dc in (1, 0):
        for dx in range(NX):
            at = lax.rem(x + dx, NX) * 2 + lax.rem(c + dc, 2)
            both = c2_in[at].astype(F32)
            blocks.append(jnp.concatenate([both[0:8, :], both[8:16, :]], axis=1))
    heads_in = jnp.concatenate(blocks, axis=0).astype(BF16)
    head_value = jnp.dot(heads_in, vup[...], preferred_element_type=F32).astype(BF16)

    oproj_load.wait()
    core_peer = (g, z * NS + x * 2 + (1 - c))
    e1_copies = []
    for n in range(NCH):
        cols = slice(n * CHUNK, (n + 1) * CHUNK)
        product = jnp.dot(head_value, oproj[:, cols], preferred_element_type=F32)
        e1_out[n] = product[0:32].astype(BF16)
        e1_copies.append(remote(e1_out.at[n], e1_in.at[n], e1s_sem.at[n], e1r_sem.at[n], core_peer))
        own_f[n] = product[32:64]

    for n in range(NCH):
        e1_copies[n].wait_recv()
        both = own_f[n] + e1_in[n].astype(F32)
        own_f[n] = both
        for t in range(CHUNK // 512):
            tile = n * (CHUNK // 512) + t
            half, col = tile // (HALF // 512), tile % (HALF // 512) * 512
            for dx in range(1, NX):
                e2_out[dx, half * 8:(half + 1) * 8, col:col + 512] = both[dx * 8:(dx + 1) * 8, t * 512:(t + 1) * 512].astype(BF16)
    e2_copies = {}
    for dx in (1, 3, 2):
        peer = (g, z * NS + lax.rem(x + dx, NX) * 2 + c)
        e2_copies[dx] = remote(e2_out.at[dx], e2_in.at[dx], e2s_sem.at[dx], e2r_sem.at[dx], peer)
    for dx in (1, 3, 2):
        e2_copies[dx].wait_recv()
    for tile in range(TILES):
        n, t = tile // (CHUNK // 128), tile % (CHUNK // 128)
        half, col = tile // (TILES // 2), tile % (TILES // 2) * 128
        total = own_f[n, 0:8, t * 128:(t + 1) * 128]
        for dx in (1, 3, 2):
            total = total + e2_in[dx, half * 8:(half + 1) * 8, col:col + 128].astype(F32)
        e3_f[tile * 8:(tile + 1) * 8, :] = total

    for zz in range(NZ):
        e3_out[zz] = jnp.concatenate(
            [e3_f[pl.ds(zz, TILES, stride=8), :], jnp.zeros((8, 128), F32)], axis=0).astype(BF16)
    e3_copies = []
    for k in order:
        to = lax.rem(z + k, NZ)
        e3_copies.append(remote(e3_out.at[to], e3_in.at[k], e3s_sem.at[k], e3r_sem.at[k], z_peer(k)))
    total = e3_out[z].astype(F32)
    for at, k in enumerate(order):
        e3_copies[at].wait_recv()
        total = total + e3_in[k].astype(F32)
    out_ref[...] = total[0:TILES].astype(BF16)

    for copy in list(q_copies.values()) + list(part_copies.values()) + c1_copies + c2_copies + e1_copies + list(e2_copies.values()) + e3_copies:
        copy.wait_send()


def body(queries, lengths, pages, slot_owner, slot_page, value_up, out_proj):
    any_spec = pl.BlockSpec(memory_space=pl.ANY)
    smem = pl.BlockSpec(memory_space=pltpu.SMEM)
    dma = pltpu.SemaphoreType.DMA
    result = pl.pallas_call(
        kernel,
        out_shape=jax.ShapeDtypeStruct((TILES, 128), BF16),
        in_specs=[any_spec, smem, any_spec, smem, smem, any_spec, any_spec],
        out_specs=pl.BlockSpec(memory_space=pltpu.VMEM),
        scratch_shapes=[
            pltpu.VMEM((HEADS, CACHE), BF16),
            pltpu.VMEM((HEADS, WIDE), BF16),
            pltpu.VMEM((GRP, HEADS, WIDE), BF16),
            pltpu.VMEM((POOL, PAGE, CACHE), BF16),
            pltpu.VMEM((LAT, VDIM), BF16),
            pltpu.VMEM((VDIM, D), BF16),
            pltpu.VMEM((GRP, HEADS, WIDE), BF16),
            pltpu.VMEM((GRP, HEADS, WIDE), BF16),
            pltpu.VMEM((NZ, 16, 256), BF16),
            pltpu.VMEM((NZ, 16, 256), BF16),
            pltpu.VMEM((2, NZ * 16, 128), F32),
            pltpu.VMEM((NS, 16, 256), BF16),
            pltpu.VMEM((NS, 16, 256), BF16),
            pltpu.VMEM((NCH, 32, CHUNK), F32),
            pltpu.VMEM((NCH, 32, CHUNK), BF16),
            pltpu.VMEM((NCH, 32, CHUNK), BF16),
            pltpu.VMEM((NX, 16, HALF), BF16),
            pltpu.VMEM((NX, 16, HALF), BF16),
            pltpu.VMEM((TILES * 8, 128), F32),
            pltpu.VMEM((NZ, 64, 128), BF16),
            pltpu.VMEM((NZ, 64, 128), BF16),
            dma((4,)),
            dma((8,)), dma((8,)), dma((8,)), dma((8,)),
            dma((8,)), dma((8,)), dma((8,)), dma((8,)),
            dma((NCH,)), dma((NCH,)), dma((NX,)), dma((NX,)), dma((8,)), dma((8,)),
        ],
        compiler_params=pltpu.CompilerParams(
            collective_id=0, has_side_effects=True, vmem_limit_bytes=60 * 1024 * 1024),
    )(queries, lengths, pages, slot_owner, slot_page, value_up, out_proj)
    return result.reshape(1, D)


def solution(mesh):
    in_specs = (
        P(("grp", "dev"), None, None),
        P(("grp", "dev")),
        P(("grp", "dev"), None, None),
        P(("grp", "dev")),
        P(("grp", "dev")),
        P("dev", None, None),
        P("dev", None),
    )
    out_specs = P(("grp", "dev"), None)
    return jax.shard_map(body, mesh=mesh, in_specs=in_specs, out_specs=out_specs, check_vma=False)
```

```python
import jax
import jax.numpy as jnp
from jax import lax
from jax.experimental import pallas as pl
from jax.experimental.pallas import tpu as pltpu
from jax.sharding import PartitionSpec as P

MESH = pl.DeviceIdType.MESH
F32 = jnp.float32
BF16 = jnp.bfloat16

ROPE = 64
NOPE = 128
SCALE = (NOPE + ROPE) ** -0.5
NEG = -1e30

GRP = 8
NZ = 8
NS = 8
NX = 4
HEADS = 64
LAT = 512
CACHE = 576
HH = HEADS // 2
PACK = 144
PAGE = 64
POOL = 4
TOK = 2 * POOL * PAGE
VDIM = 128
D = 7168
HALF = D // 2
TILES = D // 128
CHUNK = 1024
NCH = D // CHUNK


def pieces(value):
    high = value.astype(BF16).astype(F32)
    rest = value - high
    mid = rest.astype(BF16).astype(F32)
    return high, mid, rest - mid


def kernel(q_hbm, len_ref, pages_hbm, owner_ref, page_ref, vup_hbm, oproj_hbm, out_ref,
           q_raw, q_own, q_in, meta_own, meta_in, pages, vup, oproj, part_out, part_in,
           c1_out, c1_in, c1_f, c2_out, c2_in,
           own_f, e1_out, e1_in, e2_out, e2_in, e3_f, e3_out, e3_in,
           loc_sem, ms_sem, mr_sem, gs_sem, gr_sem, qs_sem, qr_sem, ps_sem, pr_sem, c1s_sem, c1r_sem, c2s_sem, c2r_sem,
           e1s_sem, e1r_sem, e2s_sem, e2r_sem, e3s_sem, e3r_sem):
    g = lax.axis_index("grp")
    d = lax.axis_index("dev")
    z = d // NS
    s = d % NS
    x = s // 2
    c = s % 2

    def grp_peer(k):
        return (lax.rem(g + k, GRP), d)

    def z_peer(k):
        return (g, lax.rem(z + k, NZ) * NS + s)

    def s_peer(k):
        return (g, z * NS + lax.rem(s + k, NS))

    barrier = pltpu.get_barrier_semaphore()
    for k in range(1, 8):
        for peer in (grp_peer(k), z_peer(k), s_peer(k)):
            pl.semaphore_signal(barrier, inc=1, device_id=peer, device_id_type=MESH)

    q_load = pltpu.make_async_copy(q_hbm.at[0], q_raw, loc_sem.at[0])
    q_load.start()
    pages_load = pltpu.make_async_copy(pages_hbm, pages.at[0:POOL], loc_sem.at[1])
    pages_load.start()
    vup_load = pltpu.make_async_copy(vup_hbm.at[0], vup, loc_sem.at[2])
    vup_load.start()
    oproj_load = pltpu.make_async_copy(oproj_hbm, oproj, loc_sem.at[3])
    oproj_load.start()

    lane = lax.broadcasted_iota(jnp.int32, (1, 128), 1)
    meta = jnp.where(lane == 0, len_ref[0], 0)
    for i in range(POOL):
        meta = jnp.where(lane == 1 + i, owner_ref[i], meta)
        meta = jnp.where(lane == 1 + POOL + i, page_ref[i], meta)
    meta_own[...] = meta

    q_load.wait()
    for half in range(2):
        rows = slice(half * HH, (half + 1) * HH)
        for j in range(4):
            q_own[half, j * HH:(j + 1) * HH, :] = q_raw[rows, j * 128:(j + 1) * 128]
        rope = q_raw[rows, LAT:CACHE].astype(F32)
        q_own[half, 4 * HH:PACK, :] = jnp.concatenate([rope[0:16], rope[16:32]], axis=1).astype(BF16)
    pages_load.wait()

    pl.semaphore_wait(barrier, 21)

    def remote(src, dst, send, recv, peer):
        copy = pltpu.make_async_remote_copy(
            src_ref=src, dst_ref=dst, send_sem=send, recv_sem=recv,
            device_id=peer, device_id_type=MESH)
        copy.start()
        return copy

    parity = lax.rem(g, 2)
    order = (4, 3, 5, 2, 6, 1, 7)
    q_copies, meta_copies, page_copies = {}, {}, []
    for k in order:
        meta_copies[k] = remote(meta_own, meta_in.at[k], ms_sem.at[k], mr_sem.at[k], grp_peer(k))
    for k in order:
        if k == 2:
            page_copies.append(remote(pages.at[0:2], pages.at[4:6], gs_sem.at[0], gr_sem.at[0], grp_peer(1)))
            page_copies.append(remote(pages.at[2:4], pages.at[6:8], gs_sem.at[1], gr_sem.at[1], grp_peer(7)))
        q_copies[k] = remote(q_own.at[lax.rem(g + k, 2)], q_in.at[k], qs_sem.at[k], qr_sem.at[k], grp_peer(k))

    for k in order:
        meta_copies[k].wait_recv()
    for copy in page_copies:
        copy.wait_recv()
    token = lax.broadcasted_iota(jnp.int32, (1, TOK), 1)
    slot = token // PAGE
    owner_v = jnp.zeros((1, TOK), jnp.int32)
    first_v = jnp.zeros((1, TOK), jnp.int32)
    rows = [(meta, i) for i in range(POOL)] + [(meta_in[1], 0), (meta_in[1], 1), (meta_in[7], 2), (meta_in[7], 3)]
    for i, (row, at) in enumerate(rows):
        owner_v = jnp.where(slot == i, row[:, 1 + at:2 + at], owner_v)
        first_v = jnp.where(slot == i, row[:, 1 + POOL + at:2 + POOL + at], first_v)
    pos_v = first_v * PAGE + token % PAGE
    lane16 = lax.broadcasted_iota(jnp.int32, (16, 128), 1)

    def partial(packed, length, request):
        page_all = pages[...].reshape(TOK, CACHE)
        rope = packed[4 * HH:PACK, :].astype(F32)
        rope = jnp.concatenate([rope[:, 0:64], rope[:, 64:128]], axis=0).astype(BF16)
        query = jnp.concatenate([packed[j * HH:(j + 1) * HH, :] for j in range(4)] + [rope], axis=1)
        scores = lax.dot_general(query, page_all, (((1,), (1,)), ((), ())),
                                 preferred_element_type=F32) * SCALE
        live = (pos_v < length) & (owner_v == request)
        top = jnp.max(jnp.where(live, scores, NEG), axis=1, keepdims=True)
        weights = jnp.where(live, jnp.exp(scores - top), 0.0)
        total = jnp.sum(weights, axis=1, keepdims=True)
        value = jnp.dot(weights.astype(BF16), page_all[:, 0:LAT], preferred_element_type=F32)
        return top, total, value

    part_copies = {}
    for k in order:
        q_copies[k].wait_recv()
        top, total, value = partial(q_in[k], meta_in[k][:, 0:1], lax.rem(g + (GRP - k), GRP))
        for j in range(4):
            part_out[k, j * HH:(j + 1) * HH, :] = value[:, j * 128:(j + 1) * 128].astype(BF16)
        stats = jnp.zeros((16, 128), F32)
        for at, piece in enumerate(pieces(top) + pieces(total)):
            stats = jnp.where(lane16 == at, piece[0:16], stats)
            stats = jnp.where(lane16 == at + 6, piece[16:32], stats)
        part_out[k, 4 * HH:PACK, :] = stats.astype(BF16)
        part_copies[k] = remote(part_out.at[k], part_in.at[k], ps_sem.at[k], pr_sem.at[k], grp_peer(GRP - k))

    own = partial(q_own[parity], meta[:, 0:1], g)

    def arrived(k):
        if k == 0:
            return own
        part_copies[k].wait_recv()
        stats = part_in[k, 4 * HH:PACK, :].astype(F32)
        stats = jnp.concatenate([stats[:, 0:6], stats[:, 6:12]], axis=0)
        value = jnp.concatenate([part_in[k, j * HH:(j + 1) * HH, :] for j in range(4)], axis=1).astype(F32)
        return ((stats[:, 0:1] + stats[:, 1:2]) + stats[:, 2:3],
                (stats[:, 3:4] + stats[:, 4:5]) + stats[:, 5:6], value)

    for members, half in (((0, 4, 2, 6), parity), ((3, 5, 1, 7), 1 - parity)):
        parts = [arrived(k) for k in members]
        best = parts[0][0]
        for top, _, _ in parts[1:]:
            best = jnp.maximum(best, top)
        denominator, merged = 0.0, 0.0
        for top, total, value in parts:
            factor = jnp.exp(top - best)
            denominator = denominator + factor * total
            merged = merged + factor * value
        latent = merged * (1.0 / denominator)
        for i in range(NZ // 2):
            rows = latent[i * NS:(i + 1) * NS, :]
            c1_out[half * (NZ // 2) + i] = jnp.concatenate([rows[:, 0:256], rows[:, 256:512]], axis=0).astype(BF16)
    c1_copies = []
    for k in order:
        to = lax.rem(z + k, NZ)
        c1_copies.append(remote(c1_out.at[to], c1_in.at[z], c1s_sem.at[k], c1r_sem.at[k], z_peer(k)))
    c1_in[z] = c1_out[z]
    for copy in c1_copies:
        copy.wait_recv()
    latents = c1_in[...].astype(F32).reshape(NZ * 16, 256)
    c1_f[0] = latents[:, 0:128]
    c1_f[1] = latents[:, 128:256]
    for ss in range(NS):
        quarters = [[c1_f[col, pl.ds(half * 8 + ss, NZ, stride=16), :] for col in range(2)] for half in range(2)]
        c2_out[ss] = jnp.concatenate([jnp.concatenate(pair, axis=1) for pair in quarters], axis=0).astype(BF16)
    c2_copies = []
    for k in order:
        to = lax.rem(s + k, NS)
        c2_copies.append(remote(c2_out.at[to], c2_in.at[s], c2s_sem.at[k], c2r_sem.at[k], s_peer(k)))
    c2_in[s] = c2_out[s]
    vup_load.wait()
    for copy in c2_copies:
        copy.wait_recv()

    blocks = []
    for dc in (1, 0):
        for dx in range(NX):
            at = lax.rem(x + dx, NX) * 2 + lax.rem(c + dc, 2)
            both = c2_in[at].astype(F32)
            blocks.append(jnp.concatenate([both[0:8, :], both[8:16, :]], axis=1))
    heads_in = jnp.concatenate(blocks, axis=0).astype(BF16)
    head_value = jnp.dot(heads_in, vup[...], preferred_element_type=F32).astype(BF16)

    oproj_load.wait()
    core_peer = (g, z * NS + x * 2 + (1 - c))
    e1_copies = []
    for n in range(NCH):
        cols = slice(n * CHUNK, (n + 1) * CHUNK)
        product = jnp.dot(head_value, oproj[:, cols], preferred_element_type=F32)
        e1_out[n] = product[0:32].astype(BF16)
        e1_copies.append(remote(e1_out.at[n], e1_in.at[n], e1s_sem.at[n], e1r_sem.at[n], core_peer))
        own_f[n] = product[32:64]

    for n in range(NCH):
        e1_copies[n].wait_recv()
        both = own_f[n] + e1_in[n].astype(F32)
        own_f[n] = both
        for t in range(CHUNK // 512):
            tile = n * (CHUNK // 512) + t
            half, col = tile // (HALF // 512), tile % (HALF // 512) * 512
            for dx in range(1, NX):
                e2_out[dx, half * 8:(half + 1) * 8, col:col + 512] = both[dx * 8:(dx + 1) * 8, t * 512:(t + 1) * 512].astype(BF16)
    e2_copies = {}
    for dx in (1, 3, 2):
        peer = (g, z * NS + lax.rem(x + dx, NX) * 2 + c)
        e2_copies[dx] = remote(e2_out.at[dx], e2_in.at[dx], e2s_sem.at[dx], e2r_sem.at[dx], peer)
    for dx in (1, 3, 2):
        e2_copies[dx].wait_recv()
    for tile in range(TILES):
        n, t = tile // (CHUNK // 128), tile % (CHUNK // 128)
        half, col = tile // (TILES // 2), tile % (TILES // 2) * 128
        total = own_f[n, 0:8, t * 128:(t + 1) * 128]
        for dx in (1, 3, 2):
            total = total + e2_in[dx, half * 8:(half + 1) * 8, col:col + 128].astype(F32)
        e3_f[tile * 8:(tile + 1) * 8, :] = total

    for zz in range(NZ):
        e3_out[zz] = jnp.concatenate(
            [e3_f[pl.ds(zz, TILES, stride=8), :], jnp.zeros((8, 128), F32)], axis=0).astype(BF16)
    e3_copies = []
    for k in order:
        to = lax.rem(z + k, NZ)
        e3_copies.append(remote(e3_out.at[to], e3_in.at[k], e3s_sem.at[k], e3r_sem.at[k], z_peer(k)))
    total = e3_out[z].astype(F32)
    for at, k in enumerate(order):
        e3_copies[at].wait_recv()
        total = total + e3_in[k].astype(F32)
    out_ref[...] = total[0:TILES].astype(BF16)

    for copy in list(q_copies.values()) + list(meta_copies.values()) + page_copies + list(part_copies.values()) + c1_copies + c2_copies + e1_copies + list(e2_copies.values()) + e3_copies:
        copy.wait_send()


def body(queries, lengths, pages, slot_owner, slot_page, value_up, out_proj):
    any_spec = pl.BlockSpec(memory_space=pl.ANY)
    smem = pl.BlockSpec(memory_space=pltpu.SMEM)
    dma = pltpu.SemaphoreType.DMA
    result = pl.pallas_call(
        kernel,
        out_shape=jax.ShapeDtypeStruct((TILES, 128), BF16),
        in_specs=[any_spec, smem, any_spec, smem, smem, any_spec, any_spec],
        out_specs=pl.BlockSpec(memory_space=pltpu.VMEM),
        scratch_shapes=[
            pltpu.VMEM((HEADS, CACHE), BF16),
            pltpu.VMEM((2, PACK, 128), BF16),
            pltpu.VMEM((GRP, PACK, 128), BF16),
            pltpu.VMEM((1, 128), jnp.int32),
            pltpu.VMEM((GRP, 1, 128), jnp.int32),
            pltpu.VMEM((2 * POOL, PAGE, CACHE), BF16),
            pltpu.VMEM((LAT, VDIM), BF16),
            pltpu.VMEM((VDIM, D), BF16),
            pltpu.VMEM((GRP, PACK, 128), BF16),
            pltpu.VMEM((GRP, PACK, 128), BF16),
            pltpu.VMEM((NZ, 16, 256), BF16),
            pltpu.VMEM((NZ, 16, 256), BF16),
            pltpu.VMEM((2, NZ * 16, 128), F32),
            pltpu.VMEM((NS, 16, 256), BF16),
            pltpu.VMEM((NS, 16, 256), BF16),
            pltpu.VMEM((NCH, 32, CHUNK), F32),
            pltpu.VMEM((NCH, 32, CHUNK), BF16),
            pltpu.VMEM((NCH, 32, CHUNK), BF16),
            pltpu.VMEM((NX, 16, HALF), BF16),
            pltpu.VMEM((NX, 16, HALF), BF16),
            pltpu.VMEM((TILES * 8, 128), F32),
            pltpu.VMEM((NZ, 64, 128), BF16),
            pltpu.VMEM((NZ, 64, 128), BF16),
            dma((4,)),
            dma((8,)), dma((8,)), dma((2,)), dma((2,)),
            dma((8,)), dma((8,)), dma((8,)), dma((8,)),
            dma((8,)), dma((8,)), dma((8,)), dma((8,)),
            dma((NCH,)), dma((NCH,)), dma((NX,)), dma((NX,)), dma((8,)), dma((8,)),
        ],
        compiler_params=pltpu.CompilerParams(
            collective_id=0, has_side_effects=True, vmem_limit_bytes=60 * 1024 * 1024),
    )(queries, lengths, pages, slot_owner, slot_page, value_up, out_proj)
    return result.reshape(1, D)


def solution(mesh):
    in_specs = (
        P(("grp", "dev"), None, None),
        P(("grp", "dev")),
        P(("grp", "dev"), None, None),
        P(("grp", "dev")),
        P(("grp", "dev")),
        P("dev", None, None),
        P("dev", None),
    )
    out_specs = P(("grp", "dev"), None)
    return jax.shard_map(body, mesh=mesh, in_specs=in_specs, out_specs=out_specs, check_vma=False)
```

```python
import jax
import jax.numpy as jnp
from jax import lax
from jax.experimental import pallas as pl
from jax.experimental.pallas import tpu as pltpu
from jax.sharding import PartitionSpec as P

MESH = pl.DeviceIdType.MESH
F32 = jnp.float32
BF16 = jnp.bfloat16

ROPE = 64
NOPE = 128
SCALE = (NOPE + ROPE) ** -0.5
NEG = -1e30

GRP = 8
NZ = 8
NS = 8
NX = 4
HEADS = 64
LAT = 512
CACHE = 576
HH = HEADS // 2
PACK = 144
PAGE = 64
POOL = 4
TOK = 2 * POOL * PAGE
VDIM = 128
D = 7168
HALF = D // 2
TILES = D // 128
CHUNK = 1024
NCH = D // CHUNK


def pieces(value):
    high = value.astype(BF16).astype(F32)
    rest = value - high
    mid = rest.astype(BF16).astype(F32)
    return high, mid, rest - mid


def kernel(q_hbm, len_ref, pages_hbm, owner_ref, page_ref, vup_hbm, oproj_hbm, out_ref,
           q_raw, q_own, q_in, meta_own, meta_in, pages, vup, oproj, part_out, part_in,
           c1_out, c1_in, c1_f, c2_out, c2_in,
           own_f, e1_out, e1_in, e2_out, e2_in, e3_f, e3_out, e3_in,
           loc_sem, in_sem, ms_sem, mr_sem, gs_sem, gr_sem, qs_sem, qr_sem, ps_sem, pr_sem, c1s_sem, c1r_sem, c2s_sem, c2r_sem,
           e1s_sem, e1r_sem, e2s_sem, e2r_sem, e3s_sem, e3r_sem):
    g = lax.axis_index("grp")
    d = lax.axis_index("dev")
    z = d // NS
    s = d % NS
    x = s // 2
    c = s % 2

    def grp_peer(k):
        return (lax.rem(g + k, GRP), d)

    def z_peer(k):
        return (g, lax.rem(z + k, NZ) * NS + s)

    def s_peer(k):
        return (g, z * NS + lax.rem(s + k, NS))

    barrier = pltpu.get_barrier_semaphore()
    near = [grp_peer(1), grp_peer(7), z_peer(1), z_peer(7)] + [s_peer(k) for k in range(1, 8)]
    for peer in near:
        pl.semaphore_signal(barrier, inc=1, device_id=peer, device_id_type=MESH)

    q_load = pltpu.make_async_copy(q_hbm.at[0], q_raw, loc_sem.at[0])
    q_load.start()
    pages_load = pltpu.make_async_copy(pages_hbm, pages.at[0:POOL], loc_sem.at[1])
    pages_load.start()
    vup_load = pltpu.make_async_copy(vup_hbm.at[0], vup, loc_sem.at[2])
    vup_load.start()
    oproj_load = pltpu.make_async_copy(oproj_hbm, oproj, loc_sem.at[3])
    oproj_load.start()

    lane = lax.broadcasted_iota(jnp.int32, (1, 128), 1)
    meta = jnp.where(lane == 0, len_ref[0], 0)
    for i in range(POOL):
        meta = jnp.where(lane == 1 + i, owner_ref[i], meta)
        meta = jnp.where(lane == 1 + POOL + i, page_ref[i], meta)
    meta_own[...] = meta

    order = (4, 3, 5, 2, 6, 1, 7)

    q_load.wait()
    for half in range(2):
        rows = slice(half * HH, (half + 1) * HH)
        for j in range(4):
            q_own[half, j * HH:(j + 1) * HH, :] = q_raw[rows, j * 128:(j + 1) * 128]
        rope = q_raw[rows, LAT:CACHE].astype(F32)
        q_own[half, 4 * HH:PACK, :] = jnp.concatenate([rope[0:16], rope[16:32]], axis=1).astype(BF16)
    pages_load.wait()

    def tell(sem, peers):
        for peer in peers:
            pl.semaphore_signal(sem, inc=1, device_id=peer, device_id_type=MESH)

    def remote(src, dst, send, recv, peer):
        copy = pltpu.make_async_remote_copy(
            src_ref=src, dst_ref=dst, send_sem=send, recv_sem=recv,
            device_id=peer, device_id_type=MESH)
        copy.start()
        return copy

    parity = lax.rem(g, 2)
    q_copies, meta_copies, page_copies = {}, {}, []

    def send_query(k):
        meta_copies[k] = remote(meta_own, meta_in.at[k], ms_sem.at[k], mr_sem.at[k], grp_peer(k))
        q_copies[k] = remote(q_own.at[lax.rem(g + k, 2)], q_in.at[k], qs_sem.at[k], qr_sem.at[k], grp_peer(k))

    pl.semaphore_wait(barrier, 11)
    tell(in_sem.at[0], [grp_peer(1), grp_peer(7)])
    tell(in_sem.at[2], [z_peer(1), z_peer(7)])
    send_query(1)
    send_query(7)
    page_copies.append(remote(pages.at[0:2], pages.at[4:6], gs_sem.at[0], gr_sem.at[0], grp_peer(1)))
    page_copies.append(remote(pages.at[2:4], pages.at[6:8], gs_sem.at[1], gr_sem.at[1], grp_peer(7)))
    pl.semaphore_wait(in_sem.at[0], 2)
    tell(in_sem.at[1], [grp_peer(2), grp_peer(6)])
    send_query(2)
    send_query(6)
    pl.semaphore_wait(in_sem.at[1], 2)
    for k in (4, 3, 5):
        send_query(k)
    pl.semaphore_wait(in_sem.at[2], 2)
    tell(in_sem.at[3], [z_peer(2), z_peer(6)])

    for k in (1, 7):
        meta_copies[k].wait_recv()
    for copy in page_copies:
        copy.wait_recv()
    token = lax.broadcasted_iota(jnp.int32, (1, TOK), 1)
    slot = token // PAGE
    owner_v = jnp.zeros((1, TOK), jnp.int32)
    first_v = jnp.zeros((1, TOK), jnp.int32)
    rows = [(meta, i) for i in range(POOL)] + [(meta_in[1], 0), (meta_in[1], 1), (meta_in[7], 2), (meta_in[7], 3)]
    for i, (row, at) in enumerate(rows):
        owner_v = jnp.where(slot == i, row[:, 1 + at:2 + at], owner_v)
        first_v = jnp.where(slot == i, row[:, 1 + POOL + at:2 + POOL + at], first_v)
    pos_v = first_v * PAGE + token % PAGE
    lane16 = lax.broadcasted_iota(jnp.int32, (16, 128), 1)

    def partials(members):
        page_all = pages[...].reshape(TOK, CACHE)
        queries, limits, requests = [], [], []
        for k in members:
            packed = q_own[parity] if k == 0 else q_in[k]
            row = meta if k == 0 else meta_in[k]
            rope = packed[4 * HH:PACK, :].astype(F32)
            rope = jnp.concatenate([rope[:, 0:64], rope[:, 64:128]], axis=0).astype(BF16)
            queries.append(jnp.concatenate([packed[j * HH:(j + 1) * HH, :] for j in range(4)] + [rope], axis=1))
            limits.append(jnp.broadcast_to(row[:, 0:1], (HH, 1)))
            requests.append(jnp.full((HH, 1), lax.rem(g + (GRP - k), GRP), jnp.int32))
        query = jnp.concatenate(queries, axis=0)
        scores = lax.dot_general(query, page_all, (((1,), (1,)), ((), ())),
                                 preferred_element_type=F32) * SCALE
        live = (pos_v < jnp.concatenate(limits, axis=0)) & (owner_v == jnp.concatenate(requests, axis=0))
        top = jnp.max(jnp.where(live, scores, NEG), axis=1, keepdims=True)
        weights = jnp.where(live, jnp.exp(scores - top), 0.0)
        total = jnp.sum(weights, axis=1, keepdims=True)
        value = jnp.dot(weights.astype(BF16), page_all[:, 0:LAT], preferred_element_type=F32)
        return {k: (top[i * HH:(i + 1) * HH], total[i * HH:(i + 1) * HH], value[i * HH:(i + 1) * HH])
                for i, k in enumerate(members)}

    part_copies = {}

    def send_partial(k, part):
        top, total, value = part
        for j in range(4):
            part_out[k, j * HH:(j + 1) * HH, :] = value[:, j * 128:(j + 1) * 128].astype(BF16)
        stats = jnp.zeros((16, 128), F32)
        for at, piece in enumerate(pieces(top) + pieces(total)):
            stats = jnp.where(lane16 == at, piece[0:16], stats)
            stats = jnp.where(lane16 == at + 6, piece[16:32], stats)
        part_out[k, 4 * HH:PACK, :] = stats.astype(BF16)
        part_copies[k] = remote(part_out.at[k], part_in.at[k], ps_sem.at[k], pr_sem.at[k], grp_peer(GRP - k))

    for copy in (q_copies[1], q_copies[7]):
        copy.wait_recv()
    done = partials((1, 7, 0))
    own = done[0]
    for k in (1, 7):
        send_partial(k, done[k])
    for members in ((2, 6), (4, 3, 5)):
        for k in members:
            meta_copies[k].wait_recv()
            q_copies[k].wait_recv()
        done = partials(members)
        for k in members:
            send_partial(k, done[k])

    def arrived(k):
        part_copies[k].wait_recv()
        stats = part_in[k, 4 * HH:PACK, :].astype(F32)
        stats = jnp.concatenate([stats[:, 0:6], stats[:, 6:12]], axis=0)
        value = jnp.concatenate([part_in[k, j * HH:(j + 1) * HH, :] for j in range(4)], axis=1).astype(F32)
        return ((stats[:, 0:1] + stats[:, 1:2]) + stats[:, 2:3],
                (stats[:, 3:4] + stats[:, 4:5]) + stats[:, 5:6], value)

    def merge(left, right):
        top = jnp.maximum(left[0], right[0])
        left_factor = jnp.exp(left[0] - top)
        right_factor = jnp.exp(right[0] - top)
        return (top, left_factor * left[1] + right_factor * right[1], left_factor * left[2] + right_factor * right[2])

    def c1_copy(zz, origin):
        return pltpu.make_async_remote_copy(
            src_ref=c1_out.at[zz], dst_ref=c1_in.at[origin], send_sem=c1s_sem.at[zz], recv_sem=c1r_sem.at[origin],
            device_id=(g, zz * NS + s), device_id_type=MESH)

    def send_latents(state, half):
        latent = state[2] * (1.0 / state[1])
        for i in range(NZ // 2):
            rows = latent[i * NS:(i + 1) * NS, :]
            zz = half * (NZ // 2) + i
            c1_out[zz] = jnp.concatenate([rows[:, 0:256], rows[:, 256:512]], axis=0).astype(BF16)

            @pl.when(zz != z)
            def _():
                c1_copy(zz, z).start()

    odd = merge(arrived(1), arrived(7))
    even = merge(own, arrived(2))
    even = merge(even, arrived(6))
    pl.semaphore_wait(in_sem.at[3], 2)
    odd = merge(merge(odd, arrived(3)), arrived(5))
    send_latents(odd, 1 - parity)
    even = merge(even, arrived(4))
    send_latents(even, parity)
    c1_in[z] = c1_out[z]
    for k in order:
        c1_copy(lax.rem(z + k, NZ), lax.rem(z + k, NZ)).wait_recv()
    latents = c1_in[...].astype(F32).reshape(NZ * 16, 256)
    c1_f[0] = latents[:, 0:128]
    c1_f[1] = latents[:, 128:256]
    for ss in range(NS):
        quarters = [[c1_f[col, pl.ds(half * 8 + ss, NZ, stride=16), :] for col in range(2)] for half in range(2)]
        c2_out[ss] = jnp.concatenate([jnp.concatenate(pair, axis=1) for pair in quarters], axis=0).astype(BF16)
    c2_copies = []
    for k in order:
        to = lax.rem(s + k, NS)
        c2_copies.append(remote(c2_out.at[to], c2_in.at[s], c2s_sem.at[k], c2r_sem.at[k], s_peer(k)))
    c2_in[s] = c2_out[s]
    vup_load.wait()
    for copy in c2_copies:
        copy.wait_recv()

    blocks = []
    for dc in (1, 0):
        for dx in range(NX):
            at = lax.rem(x + dx, NX) * 2 + lax.rem(c + dc, 2)
            both = c2_in[at].astype(F32)
            blocks.append(jnp.concatenate([both[0:8, :], both[8:16, :]], axis=1))
    heads_in = jnp.concatenate(blocks, axis=0).astype(BF16)
    head_value = jnp.dot(heads_in, vup[...], preferred_element_type=F32).astype(BF16)

    oproj_load.wait()
    core_peer = (g, z * NS + x * 2 + (1 - c))
    e1_copies = []
    for n in range(NCH):
        cols = slice(n * CHUNK, (n + 1) * CHUNK)
        product = jnp.dot(head_value, oproj[:, cols], preferred_element_type=F32)
        e1_out[n] = product[0:32].astype(BF16)
        e1_copies.append(remote(e1_out.at[n], e1_in.at[n], e1s_sem.at[n], e1r_sem.at[n], core_peer))
        own_f[n] = product[32:64]

    for n in range(NCH):
        e1_copies[n].wait_recv()
        both = own_f[n] + e1_in[n].astype(F32)
        own_f[n] = both
        for t in range(CHUNK // 512):
            tile = n * (CHUNK // 512) + t
            half, col = tile // (HALF // 512), tile % (HALF // 512) * 512
            for dx in range(1, NX):
                e2_out[dx, half * 8:(half + 1) * 8, col:col + 512] = both[dx * 8:(dx + 1) * 8, t * 512:(t + 1) * 512].astype(BF16)
    e2_copies = {}
    for dx in (1, 3, 2):
        peer = (g, z * NS + lax.rem(x + dx, NX) * 2 + c)
        e2_copies[dx] = remote(e2_out.at[dx], e2_in.at[dx], e2s_sem.at[dx], e2r_sem.at[dx], peer)
    for dx in (1, 3, 2):
        e2_copies[dx].wait_recv()
    for tile in range(TILES):
        n, t = tile // (CHUNK // 128), tile % (CHUNK // 128)
        half, col = tile // (TILES // 2), tile % (TILES // 2) * 128
        total = own_f[n, 0:8, t * 128:(t + 1) * 128]
        for dx in (1, 3, 2):
            total = total + e2_in[dx, half * 8:(half + 1) * 8, col:col + 128].astype(F32)
        e3_f[tile * 8:(tile + 1) * 8, :] = total

    for zz in range(NZ):
        e3_out[zz] = jnp.concatenate(
            [e3_f[pl.ds(zz, TILES, stride=8), :], jnp.zeros((8, 128), F32)], axis=0).astype(BF16)
    e3_copies = []
    for k in order:
        to = lax.rem(z + k, NZ)
        e3_copies.append(remote(e3_out.at[to], e3_in.at[k], e3s_sem.at[k], e3r_sem.at[k], z_peer(k)))
    total = e3_out[z].astype(F32)
    for at, k in enumerate(order):
        e3_copies[at].wait_recv()
        total = total + e3_in[k].astype(F32)
    out_ref[...] = total[0:TILES].astype(BF16)

    for copy in list(q_copies.values()) + list(meta_copies.values()) + page_copies + list(part_copies.values()) + c2_copies + e1_copies + list(e2_copies.values()) + e3_copies:
        copy.wait_send()
    for k in order:
        c1_copy(lax.rem(z + k, NZ), z).wait_send()


def body(queries, lengths, pages, slot_owner, slot_page, value_up, out_proj):
    any_spec = pl.BlockSpec(memory_space=pl.ANY)
    smem = pl.BlockSpec(memory_space=pltpu.SMEM)
    dma = pltpu.SemaphoreType.DMA
    result = pl.pallas_call(
        kernel,
        out_shape=jax.ShapeDtypeStruct((TILES, 128), BF16),
        in_specs=[any_spec, smem, any_spec, smem, smem, any_spec, any_spec],
        out_specs=pl.BlockSpec(memory_space=pltpu.VMEM),
        scratch_shapes=[
            pltpu.VMEM((HEADS, CACHE), BF16),
            pltpu.VMEM((2, PACK, 128), BF16),
            pltpu.VMEM((GRP, PACK, 128), BF16),
            pltpu.VMEM((1, 128), jnp.int32),
            pltpu.VMEM((GRP, 1, 128), jnp.int32),
            pltpu.VMEM((2 * POOL, PAGE, CACHE), BF16),
            pltpu.VMEM((LAT, VDIM), BF16),
            pltpu.VMEM((VDIM, D), BF16),
            pltpu.VMEM((GRP, PACK, 128), BF16),
            pltpu.VMEM((GRP, PACK, 128), BF16),
            pltpu.VMEM((NZ, 16, 256), BF16),
            pltpu.VMEM((NZ, 16, 256), BF16),
            pltpu.VMEM((2, NZ * 16, 128), F32),
            pltpu.VMEM((NS, 16, 256), BF16),
            pltpu.VMEM((NS, 16, 256), BF16),
            pltpu.VMEM((NCH, 32, CHUNK), F32),
            pltpu.VMEM((NCH, 32, CHUNK), BF16),
            pltpu.VMEM((NCH, 32, CHUNK), BF16),
            pltpu.VMEM((NX, 16, HALF), BF16),
            pltpu.VMEM((NX, 16, HALF), BF16),
            pltpu.VMEM((TILES * 8, 128), F32),
            pltpu.VMEM((NZ, 64, 128), BF16),
            pltpu.VMEM((NZ, 64, 128), BF16),
            dma((4,)), pltpu.SemaphoreType.REGULAR((4,)),
            dma((8,)), dma((8,)), dma((2,)), dma((2,)),
            dma((8,)), dma((8,)), dma((8,)), dma((8,)),
            dma((8,)), dma((8,)), dma((8,)), dma((8,)),
            dma((NCH,)), dma((NCH,)), dma((NX,)), dma((NX,)), dma((8,)), dma((8,)),
        ],
        compiler_params=pltpu.CompilerParams(
            collective_id=0, has_side_effects=True, vmem_limit_bytes=60 * 1024 * 1024),
    )(queries, lengths, pages, slot_owner, slot_page, value_up, out_proj)
    return result.reshape(1, D)


def solution(mesh):
    in_specs = (
        P(("grp", "dev"), None, None),
        P(("grp", "dev")),
        P(("grp", "dev"), None, None),
        P(("grp", "dev")),
        P(("grp", "dev")),
        P("dev", None, None),
        P("dev", None),
    )
    out_specs = P(("grp", "dev"), None)
    return jax.shard_map(body, mesh=mesh, in_specs=in_specs, out_specs=out_specs, check_vma=False)
```

```python
import jax
import jax.numpy as jnp
from jax import lax
from jax.experimental import pallas as pl
from jax.experimental.pallas import tpu as pltpu
from jax.sharding import PartitionSpec as P

MESH = pl.DeviceIdType.MESH
F32 = jnp.float32
BF16 = jnp.bfloat16

ROPE = 64
NOPE = 128
SCALE = (NOPE + ROPE) ** -0.5
NEG = -1e30

GRP = 8
NZ = 8
NS = 8
NX = 4
HEADS = 64
LAT = 512
CACHE = 576
HH = HEADS // 2
PAGE = 64
POOL = 4
TOK = 2 * POOL * PAGE
VDIM = 128
D = 7168
HALF = D // 2
TILES = D // 128
NCH = 4
CHUNK = D // NCH
CT = CHUNK // 128


def pieces(value):
    high = value.astype(BF16).astype(F32)
    rest = value - high
    mid = rest.astype(BF16).astype(F32)
    return high, mid, rest - mid


def kernel(q_hbm, len_ref, pages_hbm, owner_ref, page_ref, vup_hbm, oproj_hbm, out_ref,
           q_own, q_in, meta_own, meta_in, pages, vup, oproj, part_out, part_in,
           lat, c2_out, c2_in, own_f, e1_out, e1_in, e2_out, e2_in, e3_f, e3_out, e3_in,
           loc_sem, in_sem, ms_sem, mr_sem, gs_sem, gr_sem, qs_sem, qr_sem, ps_sem, pr_sem, c2s_sem, c2r_sem,
           e1s_sem, e1r_sem, e2s_sem, e2r_sem, e3s_sem, e3r_sem):
    g = lax.axis_index("grp")
    d = lax.axis_index("dev")
    z = d // NS
    s = d % NS
    x = s // 2
    c = s % 2

    def grp_peer(k):
        return (lax.rem(g + k, GRP), d)

    def z_peer(k):
        return (g, lax.rem(z + k, NZ) * NS + s)

    def s_peer(k):
        return (g, z * NS + lax.rem(s + k, NS))

    barrier = pltpu.get_barrier_semaphore()
    near = [grp_peer(1), grp_peer(7), z_peer(1), z_peer(7)] + [s_peer(k) for k in range(1, 8)]
    for peer in near:
        pl.semaphore_signal(barrier, inc=1, device_id=peer, device_id_type=MESH)

    q_loads = [pltpu.make_async_copy(q_hbm.at[0, h * HH:(h + 1) * HH], q_own.at[h], loc_sem.at[4 + h]) for h in range(2)]
    for load in q_loads:
        load.start()
    pages_load = pltpu.make_async_copy(pages_hbm, pages.at[0:POOL], loc_sem.at[1])
    pages_load.start()
    vup_load = pltpu.make_async_copy(vup_hbm.at[0], vup, loc_sem.at[2])
    vup_load.start()
    oproj_load = pltpu.make_async_copy(oproj_hbm, oproj, loc_sem.at[3])
    oproj_load.start()

    lane = lax.broadcasted_iota(jnp.int32, (1, 128), 1)
    meta = jnp.where(lane == 0, len_ref[0], 0)
    for i in range(POOL):
        meta = jnp.where(lane == 1 + i, owner_ref[i], meta)
        meta = jnp.where(lane == 1 + POOL + i, page_ref[i], meta)
    meta_own[...] = meta

    order = (4, 3, 5, 2, 6, 1, 7)

    def tell(sem, peers):
        for peer in peers:
            pl.semaphore_signal(sem, inc=1, device_id=peer, device_id_type=MESH)

    def remote(src, dst, send, recv, peer):
        copy = pltpu.make_async_remote_copy(
            src_ref=src, dst_ref=dst, send_sem=send, recv_sem=recv,
            device_id=peer, device_id_type=MESH)
        copy.start()
        return copy

    parity = lax.rem(g, 2)
    q_copies, meta_copies, page_copies = {}, {}, []

    def send_query(k):
        meta_copies[k] = remote(meta_own, meta_in.at[k], ms_sem.at[k], mr_sem.at[k], grp_peer(k))
        q_copies[k] = remote(q_hbm.at[0, pl.ds(lax.rem(g + k, 2) * HH, HH)], q_in.at[k], qs_sem.at[k], qr_sem.at[k], grp_peer(k))

    pl.semaphore_wait(barrier, 11)
    tell(in_sem.at[0], [grp_peer(1), grp_peer(7)])
    tell(in_sem.at[2], [z_peer(1), z_peer(7)])
    send_query(1)
    send_query(7)
    page_copies.append(remote(pages_hbm.at[0:2], pages.at[4:6], gs_sem.at[0], gr_sem.at[0], grp_peer(1)))
    page_copies.append(remote(pages_hbm.at[2:4], pages.at[6:8], gs_sem.at[1], gr_sem.at[1], grp_peer(7)))
    pl.semaphore_wait(in_sem.at[0], 2)
    tell(in_sem.at[1], [grp_peer(2), grp_peer(6)])
    send_query(2)
    send_query(6)
    pl.semaphore_wait(in_sem.at[2], 2)
    tell(in_sem.at[3], [z_peer(2), z_peer(6)])
    pl.semaphore_wait(in_sem.at[1], 2)
    for k in (4, 3, 5):
        send_query(k)
    pl.semaphore_wait(in_sem.at[3], 2)
    tell(in_sem.at[4], [grp_peer(k) for k in order])

    pages_load.wait()
    for load in q_loads:
        load.wait()
    for k in (1, 7):
        meta_copies[k].wait_recv()
    for copy in page_copies:
        copy.wait_recv()
    token = lax.broadcasted_iota(jnp.int32, (1, TOK), 1)
    slot = token // PAGE
    owner_v = jnp.zeros((1, TOK), jnp.int32)
    first_v = jnp.zeros((1, TOK), jnp.int32)
    rows = [(meta, i) for i in range(POOL)] + [(meta_in[1], 0), (meta_in[1], 1), (meta_in[7], 2), (meta_in[7], 3)]
    for i, (row, at) in enumerate(rows):
        owner_v = jnp.where(slot == i, row[:, 1 + at:2 + at], owner_v)
        first_v = jnp.where(slot == i, row[:, 1 + POOL + at:2 + POOL + at], first_v)
    pos_v = first_v * PAGE + token % PAGE
    lane64 = lax.broadcasted_iota(jnp.int32, (HEADS, 128), 1)
    lane32 = lax.broadcasted_iota(jnp.int32, (HH, 128), 1)

    def partials(members):
        page_all = pages[...].reshape(TOK, CACHE)
        queries, limits, requests = [], [], []
        for k in members:
            row = meta if k == 0 else meta_in[k]
            queries.append(q_own[parity] if k == 0 else q_in[k])
            limits.append(jnp.broadcast_to(row[:, 0:1], (HH, 1)))
            requests.append(jnp.full((HH, 1), lax.rem(g + (GRP - k), GRP), jnp.int32))
        query = jnp.concatenate(queries, axis=0)
        scores = lax.dot_general(query, page_all, (((1,), (1,)), ((), ())),
                                 preferred_element_type=F32) * SCALE
        live = (pos_v < jnp.concatenate(limits, axis=0)) & (owner_v == jnp.concatenate(requests, axis=0))
        top = jnp.max(jnp.where(live, scores, NEG), axis=1, keepdims=True)
        weights = jnp.where(live, jnp.exp(scores - top), 0.0)
        total = jnp.sum(weights, axis=1, keepdims=True)
        value = jnp.dot(weights.astype(BF16), page_all[:, 0:LAT], preferred_element_type=F32)
        return {k: (top[i * HH:(i + 1) * HH], total[i * HH:(i + 1) * HH], value[i * HH:(i + 1) * HH])
                for i, k in enumerate(members)}

    def part_copy(k, i, origin):
        return pltpu.make_async_remote_copy(
            src_ref=part_out.at[k, i], dst_ref=part_in.at[k, origin],
            send_sem=ps_sem.at[k, i], recv_sem=pr_sem.at[k, origin],
            device_id=(lax.rem(g + (GRP - k), GRP), (parity * 4 + i) * NS + s), device_id_type=MESH)

    def send_partial(k, part):
        top, total, value = part
        stats = jnp.zeros((HH, 128), F32)
        for at, piece in enumerate(pieces(top) + pieces(total)):
            stats = jnp.where(lane32 == at, piece, stats)
        for i in range(4):
            rows = slice(i * 8, (i + 1) * 8)
            part_out[k, i, :, 0:256] = jnp.concatenate([value[rows, 0:256], value[rows, 256:512]], axis=0).astype(BF16)
            part_out[k, i, :, 256:384] = jnp.concatenate([stats[rows], jnp.zeros((8, 128), F32)], axis=0).astype(BF16)
        for i in range(4):
            if k == 0:
                @pl.when(parity * 4 + i != z)
                def _():
                    part_copy(k, i, z).start()

                @pl.when(parity * 4 + i == z)
                def _():
                    part_in[k, z] = part_out[k, i]
            else:
                part_copy(k, i, z).start()

    for copy in (q_copies[1], q_copies[7]):
        copy.wait_recv()
    done = partials((1, 7, 0))
    pl.semaphore_wait(in_sem.at[4], 7)
    for k in (1, 7, 0):
        send_partial(k, done[k])
    for members in ((2, 6), (4, 3, 5)):
        for k in members:
            meta_copies[k].wait_recv()
            q_copies[k].wait_recv()
        done = partials(members)
        for k in members:
            send_partial(k, done[k])

    odd = lax.rem(g + z // 4, 2)
    sources = [even_k + odd * (odd_k - even_k) for even_k, odd_k in ((0, 1), (2, 7), (6, 3), (4, 5))]
    tops, totals = [], []
    for k in sources:
        for i in range(NZ):
            @pl.when((k != 0) | (i != z))
            def _():
                part_copy(k, 0, i).wait_recv()
        stats = part_in[k, :, :, 256:384].astype(F32)[:, 0:8].reshape(HEADS, 128)
        tops.append(jnp.sum(jnp.where(lane64 < 3, stats, 0.0), axis=1, keepdims=True))
        totals.append(jnp.sum(jnp.where((lane64 >= 3) & (lane64 < 6), stats, 0.0), axis=1, keepdims=True))
    best = tops[0]
    for top in tops[1:]:
        best = jnp.maximum(best, top)
    factors = [jnp.exp(top - best) for top in tops]
    denominator = 0.0
    for factor, total in zip(factors, totals):
        denominator = denominator + factor * total
    scale = 1.0 / denominator
    factors = [factor * scale for factor in factors]
    for j in range(4):
        block = 0.0
        for k, factor in zip(sources, factors):
            both = part_in[k, :, :, j % 2 * 128:j % 2 * 128 + 128].astype(F32)
            block = block + factor * both[:, j // 2 * 8:j // 2 * 8 + 8].reshape(HEADS, 128)
        lat[j] = block

    for ss in range(NS):
        quarters = [lat[j, pl.ds(ss, NZ, stride=NS), :] for j in range(4)]
        c2_out[ss] = jnp.concatenate([jnp.concatenate(quarters[0:2], axis=1), jnp.concatenate(quarters[2:4], axis=1)], axis=0).astype(BF16)
    c2_copies = []
    for k in order:
        to = lax.rem(s + k, NS)
        c2_copies.append(remote(c2_out.at[to], c2_in.at[s], c2s_sem.at[k], c2r_sem.at[k], s_peer(k)))
    c2_in[s] = c2_out[s]
    vup_load.wait()
    for copy in c2_copies:
        copy.wait_recv()

    blocks = []
    for dc in (1, 0):
        for dx in range(NX):
            at = lax.rem(x + dx, NX) * 2 + lax.rem(c + dc, 2)
            both = c2_in[at].astype(F32)
            blocks.append(jnp.concatenate([both[0:8, :], both[8:16, :]], axis=1))
    heads_in = jnp.concatenate(blocks, axis=0).astype(BF16)
    head_value = jnp.dot(heads_in, vup[...], preferred_element_type=F32).astype(BF16)

    oproj_load.wait()
    core_peer = (g, z * NS + x * 2 + (1 - c))
    e1_copies = []
    for n in range(NCH):
        cols = slice(n * CHUNK, (n + 1) * CHUNK)
        product = jnp.dot(head_value, oproj[:, cols], preferred_element_type=F32)
        e1_out[n] = product[0:32].astype(BF16)
        e1_copies.append(remote(e1_out.at[n], e1_in.at[n], e1s_sem.at[n], e1r_sem.at[n], core_peer))
        own_f[n] = product[32:64]

    e2_copies = []
    for n in range(NCH):
        e1_copies[n].wait_recv()
        both = own_f[n] + e1_in[n].astype(F32)
        own_f[n] = both
        for dx in (2, 1, 3):
            rows = both[dx * 8:(dx + 1) * 8]
            e2_out[n, dx] = jnp.concatenate([rows[:, 0:CHUNK // 2], rows[:, CHUNK // 2:CHUNK]], axis=0).astype(BF16)
            peer = (g, z * NS + lax.rem(x + dx, NX) * 2 + c)
            e2_copies.append(remote(e2_out.at[n, dx], e2_in.at[n, dx], e2s_sem.at[n, dx], e2r_sem.at[n, dx], peer))

    e3_copies = []
    for n in range(NCH):
        for copy in e2_copies[n * 3:n * 3 + 3]:
            copy.wait_recv()
        for t in range(CT):
            half, col = t // (CT // 2), t % (CT // 2) * 128
            total = own_f[n, 0:8, t * 128:(t + 1) * 128]
            for dx in (1, 3, 2):
                total = total + e2_in[n, dx, :, col:col + 128].astype(F32)[half * 8:half * 8 + 8]
            e3_f[n, t * 8:(t + 1) * 8, :] = total
        for zz in range(NZ):
            e3_out[n, zz] = jnp.concatenate(
                [e3_f[n, pl.ds(zz, CT, stride=8), :], jnp.zeros((16 - CT, 128), F32)], axis=0).astype(BF16)
        for k in order:
            to = lax.rem(z + k, NZ)
            e3_copies.append(remote(e3_out.at[n, to], e3_in.at[n, k], e3s_sem.at[n, k], e3r_sem.at[n, k], z_peer(k)))
    for n in range(NCH):
        total = e3_out[n, z].astype(F32)
        for at, k in enumerate(order):
            e3_copies[n * 7 + at].wait_recv()
            total = total + e3_in[n, k].astype(F32)
        out_ref[n] = total.astype(BF16)

    for copy in list(q_copies.values()) + list(meta_copies.values()) + page_copies + c2_copies + e1_copies + e2_copies + e3_copies:
        copy.wait_send()
    for k in range(GRP):
        for i in range(4):
            if k == 0:
                @pl.when(parity * 4 + i != z)
                def _():
                    part_copy(k, i, z).wait_send()
            else:
                part_copy(k, i, z).wait_send()


def body(queries, lengths, pages, slot_owner, slot_page, value_up, out_proj):
    any_spec = pl.BlockSpec(memory_space=pl.ANY)
    smem = pl.BlockSpec(memory_space=pltpu.SMEM)
    dma = pltpu.SemaphoreType.DMA
    result = pl.pallas_call(
        kernel,
        out_shape=jax.ShapeDtypeStruct((NCH, 16, 128), BF16),
        in_specs=[any_spec, smem, any_spec, smem, smem, any_spec, any_spec],
        out_specs=pl.BlockSpec(memory_space=pltpu.VMEM),
        scratch_shapes=[
            pltpu.VMEM((2, HH, CACHE), BF16),
            pltpu.VMEM((GRP, HH, CACHE), BF16),
            pltpu.VMEM((1, 128), jnp.int32),
            pltpu.VMEM((GRP, 1, 128), jnp.int32),
            pltpu.VMEM((2 * POOL, PAGE, CACHE), BF16),
            pltpu.VMEM((LAT, VDIM), BF16),
            pltpu.VMEM((VDIM, D), BF16),
            pltpu.VMEM((GRP, 4, 16, 384), BF16),
            pltpu.VMEM((GRP, NZ, 16, 384), BF16),
            pltpu.VMEM((4, HEADS, 128), F32),
            pltpu.VMEM((NS, 16, 256), BF16),
            pltpu.VMEM((NS, 16, 256), BF16),
            pltpu.VMEM((NCH, 32, CHUNK), F32),
            pltpu.VMEM((NCH, 32, CHUNK), BF16),
            pltpu.VMEM((NCH, 32, CHUNK), BF16),
            pltpu.VMEM((NCH, NX, 16, CHUNK // 2), BF16),
            pltpu.VMEM((NCH, NX, 16, CHUNK // 2), BF16),
            pltpu.VMEM((NCH, CT * 8, 128), F32),
            pltpu.VMEM((NCH, NZ, 16, 128), BF16),
            pltpu.VMEM((NCH, NZ, 16, 128), BF16),
            dma((6,)), pltpu.SemaphoreType.REGULAR((5,)),
            dma((GRP,)), dma((GRP,)), dma((2,)), dma((2,)), dma((GRP,)), dma((GRP,)),
            dma((GRP, 4)), dma((GRP, NZ)), dma((NS,)), dma((NS,)),
            dma((NCH,)), dma((NCH,)), dma((NCH, NX)), dma((NCH, NX)), dma((NCH, NZ)), dma((NCH, NZ)),
        ],
        compiler_params=pltpu.CompilerParams(
            collective_id=0, has_side_effects=True, vmem_limit_bytes=60 * 1024 * 1024),
    )(queries, lengths, pages, slot_owner, slot_page, value_up, out_proj)
    return result[:, 0:CT].reshape(1, D)


def solution(mesh):
    in_specs = (
        P(("grp", "dev"), None, None),
        P(("grp", "dev")),
        P(("grp", "dev"), None, None),
        P(("grp", "dev")),
        P(("grp", "dev")),
        P("dev", None, None),
        P("dev", None),
    )
    out_specs = P(("grp", "dev"), None)
    return jax.shard_map(body, mesh=mesh, in_specs=in_specs, out_specs=out_specs, check_vma=False)
```

```python
import jax
import jax.numpy as jnp
from jax import lax
from jax.experimental import pallas as pl
from jax.experimental.pallas import tpu as pltpu
from jax.sharding import PartitionSpec as P

MESH = pl.DeviceIdType.MESH
F32 = jnp.float32
BF16 = jnp.bfloat16

ROPE = 64
NOPE = 128
SCALE = (NOPE + ROPE) ** -0.5
NEG = -1e30

GRP = 8
NZ = 8
NS = 8
NX = 4
HEADS = 64
LAT = 512
CACHE = 576
HH = HEADS // 2
PAGE = 64
POOL = 4
TOK = 2 * POOL * PAGE
VDIM = 128
D = 7168
HALF = D // 2
TILES = D // 128
NCH = 4
CHUNK = D // NCH
CT = CHUNK // 128


def pieces(value):
    high = value.astype(BF16).astype(F32)
    rest = value - high
    mid = rest.astype(BF16).astype(F32)
    return high, mid, rest - mid


def kernel(q_hbm, len_ref, pages_hbm, owner_ref, page_ref, vup_hbm, oproj_hbm, out_ref,
           q_own, q_in, meta_own, meta_in, pages, vup, oproj, part_out, part_in, stat_out, stat_in,
           lat, c2_out, c2_in, own_f, e1_out, e1_in, e2_out, e2_in, e3_f, e3_out, e3_in,
           loc_sem, in_sem, ms_sem, mr_sem, gs_sem, gr_sem, qs_sem, qr_sem, ps_sem, pr_sem, ts_sem, tr_sem,
           c2s_sem, c2r_sem, e1s_sem, e1r_sem, e2s_sem, e2r_sem, e3s_sem, e3r_sem):
    g = lax.axis_index("grp")
    d = lax.axis_index("dev")
    z = d // NS
    s = d % NS
    x = s // 2
    c = s % 2

    def grp_peer(k):
        return (lax.rem(g + k, GRP), d)

    def z_peer(k):
        return (g, lax.rem(z + k, NZ) * NS + s)

    def s_peer(k):
        return (g, z * NS + lax.rem(s + k, NS))

    barrier = pltpu.get_barrier_semaphore()
    near = [f(k) for f in (grp_peer, z_peer) for k in (1, 7, 2, 6)] + [s_peer(k) for k in range(1, 8)]
    for peer in near:
        pl.semaphore_signal(barrier, inc=1, device_id=peer, device_id_type=MESH)

    q_load = pltpu.make_async_copy(q_hbm.at[0], q_own, loc_sem.at[0])
    q_load.start()
    pages_load = pltpu.make_async_copy(pages_hbm, pages.at[0:POOL], loc_sem.at[1])
    pages_load.start()
    vup_load = pltpu.make_async_copy(vup_hbm.at[0], vup, loc_sem.at[2])
    vup_load.start()
    oproj_load = pltpu.make_async_copy(oproj_hbm, oproj, loc_sem.at[3])
    oproj_load.start()

    lane = lax.broadcasted_iota(jnp.int32, (1, 128), 1)
    meta = jnp.where(lane == 0, len_ref[0], 0)
    for i in range(POOL):
        meta = jnp.where(lane == 1 + i, owner_ref[i], meta)
        meta = jnp.where(lane == 1 + POOL + i, page_ref[i], meta)
    meta_own[...] = meta

    order = (4, 3, 5, 2, 6, 1, 7)

    def tell(sem, peers):
        for peer in peers:
            pl.semaphore_signal(sem, inc=1, device_id=peer, device_id_type=MESH)

    def remote(src, dst, send, recv, peer):
        copy = pltpu.make_async_remote_copy(
            src_ref=src, dst_ref=dst, send_sem=send, recv_sem=recv,
            device_id=peer, device_id_type=MESH)
        copy.start()
        return copy

    def take(ref, sem):
        pltpu.make_async_copy(ref, ref, sem).wait()

    parity = lax.rem(g, 2)
    slots = {1: 0, 7: 1, 2: 2, 6: 3, 4: 4, 3: 5, 5: 6}
    groups = ((1, 7), (2, 6), (4, 3, 5))

    def send_queries(at):
        for k in groups[at]:
            remote(meta_own, meta_in.at[slots[k]], ms_sem.at[0], mr_sem.at[at], grp_peer(k))
            remote(q_hbm.at[0, pl.ds(lax.rem(g + k, 2) * HH, HH)], q_in.at[slots[k]], qs_sem.at[0], qr_sem.at[at], grp_peer(k))

    def take_queries(at):
        first, count = slots[groups[at][0]], len(groups[at])
        take(q_in.at[first:first + count], qr_sem.at[at])

    def take_meta(at):
        first, count = slots[groups[at][0]], len(groups[at])
        take(meta_in.at[first:first + count], mr_sem.at[at])

    pl.semaphore_wait(barrier, 15)
    tell(in_sem.at[0], [grp_peer(2), grp_peer(6)])
    tell(in_sem.at[1], [z_peer(2), z_peer(6)])
    send_queries(0)
    remote(pages_hbm.at[0:2], pages.at[4:6], gs_sem.at[0], gr_sem.at[0], grp_peer(1))
    remote(pages_hbm.at[2:4], pages.at[6:8], gs_sem.at[0], gr_sem.at[0], grp_peer(7))
    send_queries(1)
    pl.semaphore_wait(in_sem.at[0], 2)
    send_queries(2)
    pl.semaphore_wait(in_sem.at[1], 2)
    for at in range(3):
        tell(in_sem.at[2 + at], [grp_peer(k) for k in groups[at]])

    pages_load.wait()
    q_load.wait()
    take_meta(0)
    take(pages.at[4:8], gr_sem.at[0])
    token = lax.broadcasted_iota(jnp.int32, (1, TOK), 1)
    slot = token // PAGE
    owner_v = jnp.zeros((1, TOK), jnp.int32)
    first_v = jnp.zeros((1, TOK), jnp.int32)
    rows = [(meta, i) for i in range(POOL)] + [(meta_in[0], 0), (meta_in[0], 1), (meta_in[1], 2), (meta_in[1], 3)]
    for i, (row, at) in enumerate(rows):
        owner_v = jnp.where(slot == i, row[:, 1 + at:2 + at], owner_v)
        first_v = jnp.where(slot == i, row[:, 1 + POOL + at:2 + POOL + at], first_v)
    pos_v = first_v * PAGE + token % PAGE
    lane64 = lax.broadcasted_iota(jnp.int32, (HEADS, 128), 1)
    lane32 = lax.broadcasted_iota(jnp.int32, (HH, 128), 1)
    row32 = lax.broadcasted_iota(jnp.int32, (HH, 128), 0)

    def partials(members):
        page_all = pages[...].reshape(TOK, CACHE)
        queries, limits, requests = [], [], []
        for k in members:
            row = meta if k == 0 else meta_in[slots[k]]
            queries.append(q_own[pl.ds(parity * HH, HH), :] if k == 0 else q_in[slots[k]])
            limits.append(jnp.broadcast_to(row[:, 0:1], (HH, 1)))
            requests.append(jnp.full((HH, 1), lax.rem(g + (GRP - k), GRP), jnp.int32))
        query = jnp.concatenate(queries, axis=0)
        scores = lax.dot_general(query, page_all, (((1,), (1,)), ((), ())),
                                 preferred_element_type=F32) * SCALE
        live = (pos_v < jnp.concatenate(limits, axis=0)) & (owner_v == jnp.concatenate(requests, axis=0))
        top = jnp.max(jnp.where(live, scores, NEG), axis=1, keepdims=True)
        weights = jnp.where(live, jnp.exp(scores - top), 0.0)
        total = jnp.sum(weights, axis=1, keepdims=True)
        value = jnp.dot(weights.astype(BF16), page_all[:, 0:LAT], preferred_element_type=F32)
        return {k: (top[i * HH:(i + 1) * HH], total[i * HH:(i + 1) * HH], value[i * HH:(i + 1) * HH])
                for i, k in enumerate(members)}

    def send_partial(k, part):
        top, total, value = part
        stat_out[k] = jnp.concatenate(
            [jnp.sum(jnp.where(lane32 == row32, column, 0.0), axis=0, keepdims=True) for column in (top, total)], axis=0)
        for i in range(4):
            rows = slice(i * 8, (i + 1) * 8)
            part_out[k, i] = jnp.concatenate([value[rows, 0:256], value[rows, 256:512]], axis=0).astype(BF16)
        at = min(k, 1)
        for i in range(4):
            zz = parity * 4 + i

            def away():
                peer = (lax.rem(g + (GRP - k), GRP), zz * NS + s)
                remote(stat_out.at[k], stat_in.at[k, z], ts_sem.at[at], tr_sem.at[k], peer)
                remote(part_out.at[k, i], part_in.at[k, z], ps_sem.at[at], pr_sem.at[k], peer)

            if k == 0:
                pl.when(zz != z)(away)

                @pl.when(zz == z)
                def _():
                    pltpu.make_async_copy(stat_out.at[k], stat_in.at[k, z], tr_sem.at[k]).start()
                    pltpu.make_async_copy(part_out.at[k, i], part_in.at[k, z], pr_sem.at[k]).start()
            else:
                away()

    for at, members in enumerate(((1, 7, 0), (2, 6), (4, 3, 5))):
        if at:
            take_meta(at)
        take_queries(at)
        done = partials(members)
        pl.semaphore_wait(in_sem.at[2 + at], len(groups[at]))
        for k in members:
            send_partial(k, done[k])

    odd = lax.rem(g + z // 4, 2)
    sources = [even_k + odd * (odd_k - even_k) for even_k, odd_k in ((0, 1), (2, 7), (6, 3), (4, 5))]
    mine = lane64 == lax.rem(z, 4) * 8 + lax.broadcasted_iota(jnp.int32, (HEADS, 128), 0) % 8
    tops, totals = [], []
    for k in sources:
        take(stat_in.at[k], tr_sem.at[k])
        take(part_in.at[k], pr_sem.at[k])
        for at, columns in enumerate((tops, totals)):
            spread = jnp.broadcast_to(stat_in[k, :, at:at + 1, :], (NZ, 8, 128)).reshape(HEADS, 128)
            columns.append(jnp.sum(jnp.where(mine, spread, 0.0), axis=1, keepdims=True))
    best = tops[0]
    for top in tops[1:]:
        best = jnp.maximum(best, top)
    factors = [jnp.exp(top - best) for top in tops]
    denominator = 0.0
    for factor, total in zip(factors, totals):
        denominator = denominator + factor * total
    scale = 1.0 / denominator
    factors = [factor * scale for factor in factors]
    for j in range(4):
        block = 0.0
        for k, factor in zip(sources, factors):
            both = part_in[k, :, :, j % 2 * 128:j % 2 * 128 + 128].astype(F32)
            block = block + factor * both[:, j // 2 * 8:j // 2 * 8 + 8].reshape(HEADS, 128)
        lat[j] = block

    for ss in range(NS):
        quarters = [lat[j, pl.ds(ss, NZ, stride=NS), :] for j in range(4)]
        c2_out[ss] = jnp.concatenate([jnp.concatenate(quarters[0:2], axis=1), jnp.concatenate(quarters[2:4], axis=1)], axis=0).astype(BF16)
    for k in order:
        remote(c2_out.at[lax.rem(s + k, NS)], c2_in.at[s], c2s_sem.at[0], c2r_sem.at[0], s_peer(k))
    pltpu.make_async_copy(c2_out.at[s], c2_in.at[s], c2r_sem.at[0]).start()
    vup_load.wait()
    take(c2_in, c2r_sem.at[0])

    blocks = []
    for dc in (1, 0):
        for dx in range(NX):
            at = lax.rem(x + dx, NX) * 2 + lax.rem(c + dc, 2)
            both = c2_in[at].astype(F32)
            blocks.append(jnp.concatenate([both[0:8, :], both[8:16, :]], axis=1))
    heads_in = jnp.concatenate(blocks, axis=0).astype(BF16)
    head_value = jnp.dot(heads_in, vup[...], preferred_element_type=F32).astype(BF16)

    oproj_load.wait()
    core_peer = (g, z * NS + x * 2 + (1 - c))
    for n in range(NCH):
        cols = slice(n * CHUNK, (n + 1) * CHUNK)
        product = jnp.dot(head_value, oproj[:, cols], preferred_element_type=F32)
        e1_out[n] = product[0:32].astype(BF16)
        remote(e1_out.at[n], e1_in.at[n], e1s_sem.at[0], e1r_sem.at[n], core_peer)
        own_f[n] = product[32:64]

    for n in range(NCH):
        take(e1_in.at[n], e1r_sem.at[n])
        both = own_f[n] + e1_in[n].astype(F32)
        own_f[n] = both
        for dx in (2, 1, 3):
            rows = both[dx * 8:(dx + 1) * 8]
            e2_out[n, dx] = jnp.concatenate([rows[:, 0:CHUNK // 2], rows[:, CHUNK // 2:CHUNK]], axis=0).astype(BF16)
            peer = (g, z * NS + lax.rem(x + dx, NX) * 2 + c)
            remote(e2_out.at[n, dx], e2_in.at[n, dx], e2s_sem.at[0], e2r_sem.at[n], peer)

    for n in range(NCH):
        take(e2_in.at[n, 1:NX], e2r_sem.at[n])
        for t in range(CT):
            half, col = t // (CT // 2), t % (CT // 2) * 128
            total = own_f[n, 0:8, t * 128:(t + 1) * 128]
            for dx in (1, 3, 2):
                total = total + e2_in[n, dx, :, col:col + 128].astype(F32)[half * 8:half * 8 + 8]
            e3_f[n, t * 8:(t + 1) * 8, :] = total
        for zz in range(NZ):
            e3_out[n, zz] = jnp.concatenate(
                [e3_f[n, pl.ds(zz, CT, stride=8), :], jnp.zeros((16 - CT, 128), F32)], axis=0).astype(BF16)
        for k in order:
            to = lax.rem(z + k, NZ)
            remote(e3_out.at[n, to], e3_in.at[n, k], e3s_sem.at[0], e3r_sem.at[n], z_peer(k))
    for n in range(NCH):
        take(e3_in.at[n, 1:NZ], e3r_sem.at[n])
        total = e3_out[n, z].astype(F32)
        for k in order:
            total = total + e3_in[n, k].astype(F32)
        out_ref[n] = total.astype(BF16)

    take(q_in.at[0:7], qs_sem.at[0])
    take(meta_in.at[0:7], ms_sem.at[0])
    take(pages.at[4:8], gs_sem.at[0])
    take(part_out.at[1:GRP], ps_sem.at[1])
    take(stat_in.at[1:GRP, 0:4], ts_sem.at[1])

    @pl.when(z // 4 == parity)
    def _():
        take(part_out.at[0, 0:3], ps_sem.at[0])
        take(stat_in.at[0, 0:3], ts_sem.at[0])

    @pl.when(z // 4 != parity)
    def _():
        take(part_out.at[0], ps_sem.at[0])
        take(stat_in.at[0, 0:4], ts_sem.at[0])

    take(c2_out.at[1:NS], c2s_sem.at[0])
    take(e1_out, e1s_sem.at[0])
    take(e2_out.at[:, 1:NX], e2s_sem.at[0])
    take(e3_out.at[:, 1:NZ], e3s_sem.at[0])


def body(queries, lengths, pages, slot_owner, slot_page, value_up, out_proj):
    any_spec = pl.BlockSpec(memory_space=pl.ANY)
    smem = pl.BlockSpec(memory_space=pltpu.SMEM)
    dma = pltpu.SemaphoreType.DMA
    result = pl.pallas_call(
        kernel,
        out_shape=jax.ShapeDtypeStruct((NCH, 16, 128), BF16),
        in_specs=[any_spec, smem, any_spec, smem, smem, any_spec, any_spec],
        out_specs=pl.BlockSpec(memory_space=pltpu.VMEM),
        scratch_shapes=[
            pltpu.VMEM((HEADS, CACHE), BF16),
            pltpu.VMEM((GRP, HH, CACHE), BF16),
            pltpu.VMEM((1, 128), jnp.int32),
            pltpu.VMEM((GRP, 1, 128), jnp.int32),
            pltpu.VMEM((2 * POOL, PAGE, CACHE), BF16),
            pltpu.VMEM((LAT, VDIM), BF16),
            pltpu.VMEM((VDIM, D), BF16),
            pltpu.VMEM((GRP, 4, 16, 256), BF16),
            pltpu.VMEM((GRP, NZ, 16, 256), BF16),
            pltpu.VMEM((GRP, 2, 128), F32),
            pltpu.VMEM((GRP, NZ, 2, 128), F32),
            pltpu.VMEM((4, HEADS, 128), F32),
            pltpu.VMEM((NS, 16, 256), BF16),
            pltpu.VMEM((NS, 16, 256), BF16),
            pltpu.VMEM((NCH, 32, CHUNK), F32),
            pltpu.VMEM((NCH, 32, CHUNK), BF16),
            pltpu.VMEM((NCH, 32, CHUNK), BF16),
            pltpu.VMEM((NCH, NX, 16, CHUNK // 2), BF16),
            pltpu.VMEM((NCH, NX, 16, CHUNK // 2), BF16),
            pltpu.VMEM((NCH, CT * 8, 128), F32),
            pltpu.VMEM((NCH, NZ, 16, 128), BF16),
            pltpu.VMEM((NCH, NZ, 16, 128), BF16),
            dma((4,)), pltpu.SemaphoreType.REGULAR((5,)),
            dma((1,)), dma((3,)), dma((1,)), dma((1,)), dma((1,)), dma((3,)),
            dma((2,)), dma((GRP,)), dma((2,)), dma((GRP,)), dma((1,)), dma((1,)),
            dma((1,)), dma((NCH,)), dma((1,)), dma((NCH,)), dma((1,)), dma((NCH,)),
        ],
        compiler_params=pltpu.CompilerParams(
            collective_id=0, has_side_effects=True, vmem_limit_bytes=60 * 1024 * 1024),
    )(queries, lengths, pages, slot_owner, slot_page, value_up, out_proj)
    return result[:, 0:CT].reshape(1, D)


def solution(mesh):
    in_specs = (
        P(("grp", "dev"), None, None),
        P(("grp", "dev")),
        P(("grp", "dev"), None, None),
        P(("grp", "dev")),
        P(("grp", "dev")),
        P("dev", None, None),
        P("dev", None),
    )
    out_specs = P(("grp", "dev"), None)
    return jax.shard_map(body, mesh=mesh, in_specs=in_specs, out_specs=out_specs, check_vma=False)
```

```python
import jax
import jax.numpy as jnp
from jax import lax
from jax.experimental import pallas as pl
from jax.experimental.pallas import tpu as pltpu
from jax.sharding import PartitionSpec as P

MESH = pl.DeviceIdType.MESH
F32 = jnp.float32
BF16 = jnp.bfloat16

ROPE = 64
NOPE = 128
SCALE = (NOPE + ROPE) ** -0.5
NEG = -1e30

GRP = 8
NZ = 8
NS = 8
NX = 4
HEADS = 64
LAT = 512
CACHE = 576
HH = HEADS // 2
PAGE = 64
POOL = 4
TOK = 2 * POOL * PAGE
VDIM = 128
D = 7168
HALF = D // 2
TILES = D // 128
NCH = 4
CHUNK = D // NCH
CT = CHUNK // 128


def pieces(value):
    high = value.astype(BF16).astype(F32)
    rest = value - high
    mid = rest.astype(BF16).astype(F32)
    return high, mid, rest - mid


def kernel(q_hbm, len_hbm, pages_hbm, owner_hbm, page_hbm, vup_hbm, oproj_hbm, out_ref,
           len_ref, owner_ref, page_ref, q_own, q_in, rope_own, rope_in, prope_out, prope_in, meta_own, meta_in, pages, vup, oproj, part_out, part_in, stat_out, stat_in,
           row_f, lat, c2_out, c2_in, own_f, e1_out, e1_in, e2_out, e2_in, e3_f, e3_out, e3_in,
           loc_sem, in_sem, ms_sem, mr_sem, gs_sem, gr_sem, qs_sem, qr_sem, rs_sem, rr_sem, ps_sem, pr_sem, ts_sem, tr_sem,
           c2s_sem, c2r_sem, e1s_sem, e1r_sem, e2s_sem, e2r_sem, e3s_sem, e3r_sem):
    g = lax.axis_index("grp")
    d = lax.axis_index("dev")
    z = d // NS
    s = d % NS
    x = s // 2
    c = s % 2

    def grp_peer(k):
        return (lax.rem(g + k, GRP), d)

    def z_peer(k):
        return (g, lax.rem(z + k, NZ) * NS + s)

    def s_peer(k):
        return (g, z * NS + lax.rem(s + k, NS))

    barrier = pltpu.get_barrier_semaphore()
    near = [f(k) for f in (grp_peer, z_peer) for k in (1, 7, 2, 6)] + [s_peer(k) for k in range(1, 8)]
    for peer in near:
        pl.semaphore_signal(barrier, inc=1, device_id=peer, device_id_type=MESH)

    q_load = pltpu.make_async_copy(q_hbm.at[0], q_own, loc_sem.at[0])
    q_load.start()
    number_loads = [pltpu.make_async_copy(src, dst, loc_sem.at[4 + at]) for at, (src, dst) in
                    enumerate(((len_hbm, len_ref), (owner_hbm, owner_ref), (page_hbm, page_ref)))]
    for load in number_loads:
        load.start()
    pages_load = pltpu.make_async_copy(pages_hbm, pages.at[0:POOL], loc_sem.at[1])
    pages_load.start()
    vup_load = pltpu.make_async_copy(vup_hbm.at[0], vup, loc_sem.at[2])
    vup_load.start()
    oproj_load = pltpu.make_async_copy(oproj_hbm, oproj, loc_sem.at[3])
    oproj_load.start()

    def tell(sem, peers):
        for peer in peers:
            pl.semaphore_signal(sem, inc=1, device_id=peer, device_id_type=MESH)

    def remote(src, dst, send, recv, peer):
        copy = pltpu.make_async_remote_copy(
            src_ref=src, dst_ref=dst, send_sem=send, recv_sem=recv,
            device_id=peer, device_id_type=MESH)
        copy.start()
        return copy

    def take(ref, sem):
        pltpu.make_async_copy(ref, ref, sem).wait()

    parity = lax.rem(g, 2)
    slots = {1: 0, 7: 1, 2: 2, 6: 3, 4: 4, 3: 5, 5: 6}
    groups = ((1, 7), (2, 6), (4, 3, 5))

    def send_queries(at):
        for k in groups[at]:
            remote(q_hbm.at[0, pl.ds(lax.rem(g + k, 2) * HH, HH), 0:LAT], q_in.at[slots[k]], qs_sem.at[0], qr_sem.at[at], grp_peer(k))

    def send_sides(at):
        for k in groups[at]:
            remote(meta_own, meta_in.at[slots[k]], ms_sem.at[0], mr_sem.at[at], grp_peer(k))
            remote(rope_own.at[lax.rem(g + k, 2)], rope_in.at[slots[k]], rs_sem.at[0], rr_sem.at[at], grp_peer(k))

    def take_queries(at):
        first, count = slots[groups[at][0]], len(groups[at])
        take(rope_in.at[first:first + count], rr_sem.at[at])
        take(q_in.at[first:first + count], qr_sem.at[at])

    def take_meta(at):
        first, count = slots[groups[at][0]], len(groups[at])
        take(meta_in.at[first:first + count], mr_sem.at[at])

    pl.semaphore_wait(barrier, 15)
    tell(in_sem.at[0], [grp_peer(2), grp_peer(6)])
    tell(in_sem.at[1], [z_peer(2), z_peer(6)])
    send_queries(0)
    send_queries(1)
    remote(pages_hbm.at[0:2, :, 0:LAT], pages.at[4:6, :, 0:LAT], gs_sem.at[0], gr_sem.at[0], grp_peer(1))
    remote(pages_hbm.at[2:4, :, 0:LAT], pages.at[6:8, :, 0:LAT], gs_sem.at[0], gr_sem.at[0], grp_peer(7))

    for load in number_loads:
        load.wait()
    lane = lax.broadcasted_iota(jnp.int32, (1, 128), 1)
    meta = jnp.where(lane == 0, len_ref[0], 0)
    for i in range(POOL):
        meta = jnp.where(lane == 1 + i, owner_ref[i], meta)
        meta = jnp.where(lane == 1 + POOL + i, page_ref[i], meta)
    meta_own[...] = meta
    q_load.wait()
    for half in range(2):
        rope = q_own[half * HH:(half + 1) * HH, LAT:CACHE].astype(F32)
        rope_own[half] = jnp.concatenate([rope[0:16], rope[16:32]], axis=1).astype(BF16)
    send_sides(0)
    pages_load.wait()
    for side in range(2):
        rope = [pages[2 * side + i, :, LAT:CACHE].astype(F32) for i in range(2)]
        prope_out[side] = jnp.concatenate(rope, axis=1).astype(BF16)
    remote(prope_out.at[0], prope_in.at[0], gs_sem.at[1], gr_sem.at[1], grp_peer(1))
    remote(prope_out.at[1], prope_in.at[1], gs_sem.at[1], gr_sem.at[1], grp_peer(7))
    send_sides(1)
    pl.semaphore_wait(in_sem.at[0], 2)
    send_queries(2)
    send_sides(2)
    pl.semaphore_wait(in_sem.at[1], 2)
    for at in range(3):
        tell(in_sem.at[2 + at], [grp_peer(k) for k in groups[at]])

    order = (4, 3, 5, 2, 6, 1, 7)
    take_meta(0)
    take(prope_in, gr_sem.at[1])
    take(pages.at[4:8, :, 0:LAT], gr_sem.at[0])
    for side in range(2):
        rope = prope_in[side].astype(F32)
        for i in range(2):
            pages[4 + 2 * side + i, :, LAT:CACHE] = rope[:, i * ROPE:(i + 1) * ROPE].astype(BF16)
    token = lax.broadcasted_iota(jnp.int32, (1, TOK), 1)
    slot = token // PAGE
    owner_v = jnp.zeros((1, TOK), jnp.int32)
    first_v = jnp.zeros((1, TOK), jnp.int32)
    rows = [(meta, i) for i in range(POOL)] + [(meta_in[0], 0), (meta_in[0], 1), (meta_in[1], 2), (meta_in[1], 3)]
    for i, (row, at) in enumerate(rows):
        owner_v = jnp.where(slot == i, row[:, 1 + at:2 + at], owner_v)
        first_v = jnp.where(slot == i, row[:, 1 + POOL + at:2 + POOL + at], first_v)
    pos_v = first_v * PAGE + token % PAGE
    lane64 = lax.broadcasted_iota(jnp.int32, (HEADS, 128), 1)
    lane32 = lax.broadcasted_iota(jnp.int32, (HH, 128), 1)
    row32 = lax.broadcasted_iota(jnp.int32, (HH, 128), 0)

    def partials(members):
        page_all = pages[...].reshape(TOK, CACHE)
        queries, limits, requests = [], [], []
        for k in members:
            row = meta if k == 0 else meta_in[slots[k]]
            if k == 0:
                queries.append(q_own[pl.ds(parity * HH, HH), :])
            else:
                rope = rope_in[slots[k]].astype(F32)
                rope = jnp.concatenate([rope[:, 0:ROPE], rope[:, ROPE:2 * ROPE]], axis=0).astype(BF16)
                queries.append(jnp.concatenate([q_in[slots[k]], rope], axis=1))
            limits.append(jnp.broadcast_to(row[:, 0:1], (HH, 1)))
            requests.append(jnp.full((HH, 1), lax.rem(g + (GRP - k), GRP), jnp.int32))
        query = jnp.concatenate(queries, axis=0)
        scores = lax.dot_general(query, page_all, (((1,), (1,)), ((), ())),
                                 preferred_element_type=F32) * SCALE
        live = (pos_v < jnp.concatenate(limits, axis=0)) & (owner_v == jnp.concatenate(requests, axis=0))
        top = jnp.max(jnp.where(live, scores, NEG), axis=1, keepdims=True)
        weights = jnp.where(live, jnp.exp(scores - top), 0.0)
        total = jnp.sum(weights, axis=1, keepdims=True)
        value = jnp.dot(weights.astype(BF16), page_all[:, 0:LAT], preferred_element_type=F32)
        return {k: (top[i * HH:(i + 1) * HH], total[i * HH:(i + 1) * HH], value[i * HH:(i + 1) * HH])
                for i, k in enumerate(members)}

    def send_partial(k, part):
        top, total, value = part
        stat_out[k] = jnp.concatenate(
            [jnp.sum(jnp.where(lane32 == row32, column, 0.0), axis=0, keepdims=True) for column in (top, total)], axis=0)
        for i in range(4):
            rows = slice(i * 8, (i + 1) * 8)
            part_out[k, i] = jnp.concatenate([value[rows, 0:256], value[rows, 256:512]], axis=0).astype(BF16)
        at = min(k, 1)
        for i in range(4):
            zz = parity * 4 + i

            def away():
                peer = (lax.rem(g + (GRP - k), GRP), zz * NS + s)
                remote(stat_out.at[k], stat_in.at[k, z], ts_sem.at[at], tr_sem.at[k], peer)
                remote(part_out.at[k, i], part_in.at[k, z], ps_sem.at[at], pr_sem.at[k], peer)

            if k == 0:
                pl.when(zz != z)(away)

                @pl.when(zz == z)
                def _():
                    pltpu.make_async_copy(stat_out.at[k], stat_in.at[k, z], tr_sem.at[k]).start()
                    pltpu.make_async_copy(part_out.at[k, i], part_in.at[k, z], pr_sem.at[k]).start()
            else:
                away()

    for at, members in enumerate(((1, 7, 0), (2, 6), (4, 3, 5))):
        if at:
            take_meta(at)
        take_queries(at)
        done = partials(members)
        pl.semaphore_wait(in_sem.at[2 + at], len(groups[at]))
        for k in members:
            send_partial(k, done[k])

    odd = lax.rem(g + z // 4, 2)
    sources = [even_k + odd * (odd_k - even_k) for even_k, odd_k in ((0, 1), (2, 7), (6, 3), (4, 5))]
    mine = lane64 == lax.rem(z, 4) * 8 + lax.broadcasted_iota(jnp.int32, (HEADS, 128), 0) % 8
    tops, totals = [], []
    for k in sources:
        take(stat_in.at[k], tr_sem.at[k])
        take(part_in.at[k], pr_sem.at[k])
        for at, columns in enumerate((tops, totals)):
            spread = jnp.broadcast_to(stat_in[k, :, at:at + 1, :], (NZ, 8, 128)).reshape(HEADS, 128)
            columns.append(jnp.sum(jnp.where(mine, spread, 0.0), axis=1, keepdims=True))
    best = tops[0]
    for top in tops[1:]:
        best = jnp.maximum(best, top)
    factors = [jnp.exp(top - best) for top in tops]
    denominator = 0.0
    for factor, total in zip(factors, totals):
        denominator = denominator + factor * total
    scale = 1.0 / denominator
    factors = [factor * scale for factor in factors]
    for j in range(4):
        block = 0.0
        for k, factor in zip(sources, factors):
            both = part_in[k, :, :, j % 2 * 128:j % 2 * 128 + 128].astype(F32)
            block = block + factor * both[:, j // 2 * 8:j // 2 * 8 + 8].reshape(HEADS, 128)
        lat[j] = block

    for ss in range(NS):
        quarters = [lat[j, pl.ds(ss, NZ, stride=NS), :] for j in range(4)]
        c2_out[ss] = jnp.concatenate([jnp.concatenate(quarters[0:2], axis=1), jnp.concatenate(quarters[2:4], axis=1)], axis=0).astype(BF16)
    for k in order:
        remote(c2_out.at[lax.rem(s + k, NS)], c2_in.at[s], c2s_sem.at[0], c2r_sem.at[0], s_peer(k))
    pltpu.make_async_copy(c2_out.at[s], c2_in.at[s], c2r_sem.at[0]).start()
    vup_load.wait()
    take(c2_in, c2r_sem.at[0])

    blocks = []
    for dc in (1, 0):
        for dx in range(NX):
            at = lax.rem(x + dx, NX) * 2 + lax.rem(c + dc, 2)
            both = c2_in[at].astype(F32)
            blocks.append(jnp.concatenate([both[0:8, :], both[8:16, :]], axis=1))
    heads_in = jnp.concatenate(blocks, axis=0).astype(BF16)
    head_value = jnp.dot(heads_in, vup[...], preferred_element_type=F32).astype(BF16)

    oproj_load.wait()
    core_peer = (g, z * NS + x * 2 + (1 - c))
    for n in range(NCH):
        cols = slice(n * CHUNK, (n + 1) * CHUNK)
        product = jnp.dot(head_value, oproj[:, cols], preferred_element_type=F32)
        e1_out[n] = product[0:32].astype(BF16)
        remote(e1_out.at[n], e1_in.at[n], e1s_sem.at[0], e1r_sem.at[n], core_peer)
        own_f[n] = product[32:64]

    for n in range(NCH):
        take(e1_in.at[n], e1r_sem.at[n])
        both = own_f[n] + e1_in[n].astype(F32)
        own_f[n] = both
        for dx in (2, 1, 3):
            rows = both[dx * 8:(dx + 1) * 8]
            e2_out[n, dx] = jnp.concatenate([rows[:, 0:CHUNK // 2], rows[:, CHUNK // 2:CHUNK]], axis=0).astype(BF16)
            peer = (g, z * NS + lax.rem(x + dx, NX) * 2 + c)
            remote(e2_out.at[n, dx], e2_in.at[n, dx], e2s_sem.at[0], e2r_sem.at[n], peer)

    for n in range(NCH):
        take(e2_in.at[n, 1:NX], e2r_sem.at[n])
        for t in range(CT):
            half, col = t // (CT // 2), t % (CT // 2) * 128
            total = own_f[n, 0:8, t * 128:(t + 1) * 128]
            for dx in (1, 3, 2):
                total = total + e2_in[n, dx, :, col:col + 128].astype(F32)[half * 8:half * 8 + 8]
            e3_f[n, t * 8:(t + 1) * 8, :] = total
        for zz in range(NZ):
            e3_out[n, zz] = jnp.concatenate(
                [e3_f[n, pl.ds(zz, CT, stride=8), :], jnp.zeros((16 - CT, 128), F32)], axis=0).astype(BF16)
        for k in order:
            to = lax.rem(z + k, NZ)
            remote(e3_out.at[n, to], e3_in.at[n, k], e3s_sem.at[0], e3r_sem.at[n], z_peer(k))
    for n in range(NCH):
        take(e3_in.at[n, 1:NZ], e3r_sem.at[n])
        total = e3_out[n, z].astype(F32)
        for k in order:
            total = total + e3_in[n, k].astype(F32)
        for t in range(CT):
            row_f[:, n * CHUNK + t * 128:n * CHUNK + (t + 1) * 128] = total[t:t + 1]
    out_ref[...] = row_f[...].astype(BF16)

    take(q_in.at[0:7], qs_sem.at[0])
    take(meta_in.at[0:7], ms_sem.at[0])
    take(rope_in.at[0:7], rs_sem.at[0])
    take(pages.at[4:8, :, 0:LAT], gs_sem.at[0])
    take(prope_out, gs_sem.at[1])
    take(part_out.at[1:GRP], ps_sem.at[1])
    take(stat_in.at[1:GRP, 0:4], ts_sem.at[1])

    @pl.when(z // 4 == parity)
    def _():
        take(part_out.at[0, 0:3], ps_sem.at[0])
        take(stat_in.at[0, 0:3], ts_sem.at[0])

    @pl.when(z // 4 != parity)
    def _():
        take(part_out.at[0], ps_sem.at[0])
        take(stat_in.at[0, 0:4], ts_sem.at[0])

    take(c2_out.at[1:NS], c2s_sem.at[0])
    take(e1_out, e1s_sem.at[0])
    take(e2_out.at[:, 1:NX], e2s_sem.at[0])
    take(e3_out.at[:, 1:NZ], e3s_sem.at[0])


def body(queries, lengths, pages, slot_owner, slot_page, value_up, out_proj):
    any_spec = pl.BlockSpec(memory_space=pl.ANY)
    dma = pltpu.SemaphoreType.DMA
    return pl.pallas_call(
        kernel,
        out_shape=jax.ShapeDtypeStruct((1, D), BF16),
        in_specs=[any_spec] * 7,
        out_specs=pl.BlockSpec(memory_space=pltpu.VMEM),
        scratch_shapes=[
            pltpu.SMEM((1,), jnp.int32),
            pltpu.SMEM((POOL,), jnp.int32),
            pltpu.SMEM((POOL,), jnp.int32),
            pltpu.VMEM((HEADS, CACHE), BF16),
            pltpu.VMEM((GRP, HH, LAT), BF16),
            pltpu.VMEM((2, 16, 128), BF16),
            pltpu.VMEM((GRP, 16, 128), BF16),
            pltpu.VMEM((2, PAGE, 128), BF16),
            pltpu.VMEM((2, PAGE, 128), BF16),
            pltpu.VMEM((1, 128), jnp.int32),
            pltpu.VMEM((GRP, 1, 128), jnp.int32),
            pltpu.VMEM((2 * POOL, PAGE, CACHE), BF16),
            pltpu.VMEM((LAT, VDIM), BF16),
            pltpu.VMEM((VDIM, D), BF16),
            pltpu.VMEM((GRP, 4, 16, 256), BF16),
            pltpu.VMEM((GRP, NZ, 16, 256), BF16),
            pltpu.VMEM((GRP, 2, 128), F32),
            pltpu.VMEM((GRP, NZ, 2, 128), F32),
            pltpu.VMEM((1, D), F32),
            pltpu.VMEM((4, HEADS, 128), F32),
            pltpu.VMEM((NS, 16, 256), BF16),
            pltpu.VMEM((NS, 16, 256), BF16),
            pltpu.VMEM((NCH, 32, CHUNK), F32),
            pltpu.VMEM((NCH, 32, CHUNK), BF16),
            pltpu.VMEM((NCH, 32, CHUNK), BF16),
            pltpu.VMEM((NCH, NX, 16, CHUNK // 2), BF16),
            pltpu.VMEM((NCH, NX, 16, CHUNK // 2), BF16),
            pltpu.VMEM((NCH, CT * 8, 128), F32),
            pltpu.VMEM((NCH, NZ, 16, 128), BF16),
            pltpu.VMEM((NCH, NZ, 16, 128), BF16),
            dma((7,)), pltpu.SemaphoreType.REGULAR((5,)),
            dma((1,)), dma((3,)), dma((2,)), dma((2,)), dma((1,)), dma((3,)), dma((1,)), dma((3,)),
            dma((2,)), dma((GRP,)), dma((2,)), dma((GRP,)), dma((1,)), dma((1,)),
            dma((1,)), dma((NCH,)), dma((1,)), dma((NCH,)), dma((1,)), dma((NCH,)),
        ],
        compiler_params=pltpu.CompilerParams(
            collective_id=0, has_side_effects=True, vmem_limit_bytes=60 * 1024 * 1024),
    )(queries, lengths, pages, slot_owner, slot_page, value_up, out_proj)


def solution(mesh):
    in_specs = (
        P(("grp", "dev"), None, None),
        P(("grp", "dev")),
        P(("grp", "dev"), None, None),
        P(("grp", "dev")),
        P(("grp", "dev")),
        P("dev", None, None),
        P("dev", None),
    )
    out_specs = P(("grp", "dev"), None)
    return jax.shard_map(body, mesh=mesh, in_specs=in_specs, out_specs=out_specs, check_vma=False)
```

```python
import jax
import jax.numpy as jnp
from jax import lax
from jax.experimental import pallas as pl
from jax.experimental.pallas import tpu as pltpu
from jax.sharding import PartitionSpec as P

MESH = pl.DeviceIdType.MESH
F32 = jnp.float32
BF16 = jnp.bfloat16

ROPE = 64
NOPE = 128
SCALE = (NOPE + ROPE) ** -0.5
NEG = -1e30

GRP = 8
NZ = 8
NS = 8
NX = 4
HEADS = 64
LAT = 512
CACHE = 576
HH = HEADS // 2
PAGE = 64
POOL = 4
TOK = 2 * POOL * PAGE
VDIM = 128
D = 7168
HALF = D // 2
TILES = D // 128
NCH = 4
NX1 = 3
CHUNK = D // NCH
CT = CHUNK // 128


def pieces(value):
    high = value.astype(BF16).astype(F32)
    rest = value - high
    mid = rest.astype(BF16).astype(F32)
    return high, mid, rest - mid


def kernel(q_hbm, len_hbm, pages_hbm, owner_hbm, page_hbm, vup_hbm, oproj_hbm, out_ref,
           len_ref, owner_ref, page_ref, q_own, q_in, rope_own, rope_in, prope_out, prope_in, meta_own, meta_in, pages, vup, oproj, part_out, part_in, stat_out, stat_in,
           row_f, lat, c2_out, c2_in, own_f, e1_out, e1_in, e2_out, e2_in, e3_f, e3_out, e3_in, f1_f, f1_out, f1_in, f2_f, f2_out, f2_in,
           loc_sem, in_sem, ms_sem, mr_sem, gs_sem, gr_sem, qs_sem, qr_sem, rs_sem, rr_sem, ps_sem, pr_sem, ts_sem, tr_sem,
           c2s_sem, c2r_sem, e1s_sem, e1r_sem, e2s_sem, e2r_sem, e3s_sem, e3r_sem, f1s_sem, f1r_sem, f2s_sem, f2r_sem):
    g = lax.axis_index("grp")
    d = lax.axis_index("dev")
    z = d // NS
    s = d % NS
    x = s // 2
    c = s % 2

    def grp_peer(k):
        return (lax.rem(g + k, GRP), d)

    def z_peer(k):
        return (g, lax.rem(z + k, NZ) * NS + s)

    def s_peer(k):
        return (g, z * NS + lax.rem(s + k, NS))

    barrier = pltpu.get_barrier_semaphore()
    near = [f(k) for f in (grp_peer, z_peer) for k in (1, 7, 2, 6)] + [s_peer(k) for k in range(1, 8)]
    for peer in near:
        pl.semaphore_signal(barrier, inc=1, device_id=peer, device_id_type=MESH)

    q_load = pltpu.make_async_copy(q_hbm.at[0], q_own, loc_sem.at[0])
    q_load.start()
    number_loads = [pltpu.make_async_copy(src, dst, loc_sem.at[4 + at]) for at, (src, dst) in
                    enumerate(((len_hbm, len_ref), (owner_hbm, owner_ref), (page_hbm, page_ref)))]
    for load in number_loads:
        load.start()
    pages_load = pltpu.make_async_copy(pages_hbm, pages.at[0:POOL], loc_sem.at[1])
    pages_load.start()
    vup_load = pltpu.make_async_copy(vup_hbm.at[0], vup, loc_sem.at[2])
    vup_load.start()
    oproj_load = pltpu.make_async_copy(oproj_hbm, oproj, loc_sem.at[3])
    oproj_load.start()

    def tell(sem, peers):
        for peer in peers:
            pl.semaphore_signal(sem, inc=1, device_id=peer, device_id_type=MESH)

    def remote(src, dst, send, recv, peer):
        copy = pltpu.make_async_remote_copy(
            src_ref=src, dst_ref=dst, send_sem=send, recv_sem=recv,
            device_id=peer, device_id_type=MESH)
        copy.start()
        return copy

    def take(ref, sem):
        pltpu.make_async_copy(ref, ref, sem).wait()

    parity = lax.rem(g, 2)
    slots = {1: 0, 7: 1, 2: 2, 6: 3, 3: 4, 5: 5, 4: 6}
    groups = ((1, 7), (2, 6), (3, 5, 4))

    def send_queries(at):
        for k in groups[at]:
            remote(q_own.at[pl.ds(lax.rem(g + k, 2) * HH, HH), 0:LAT], q_in.at[slots[k]], qs_sem.at[0], qr_sem.at[at], grp_peer(k))

    def send_sides(at):
        for k in groups[at]:
            remote(meta_own, meta_in.at[slots[k]], ms_sem.at[0], mr_sem.at[at], grp_peer(k))
            remote(rope_own.at[lax.rem(g + k, 2)], rope_in.at[slots[k]], rs_sem.at[0], rr_sem.at[at], grp_peer(k))

    def take_queries(at):
        first, count = slots[groups[at][0]], len(groups[at])
        take(rope_in.at[first:first + count], rr_sem.at[at])
        take(q_in.at[first:first + count], qr_sem.at[at])

    def take_meta(at):
        first, count = slots[groups[at][0]], len(groups[at])
        take(meta_in.at[first:first + count], mr_sem.at[at])

    q_load.wait()
    pages_load.wait()
    for load in number_loads:
        load.wait()
    lane = lax.broadcasted_iota(jnp.int32, (1, 128), 1)
    meta = jnp.where(lane == 0, len_ref[0], 0)
    for i in range(POOL):
        meta = jnp.where(lane == 1 + i, owner_ref[i], meta)
        meta = jnp.where(lane == 1 + POOL + i, page_ref[i], meta)
    meta_own[...] = meta
    for half in range(2):
        rope = q_own[half * HH:(half + 1) * HH, LAT:CACHE].astype(F32)
        rope_own[half] = jnp.concatenate([rope[0:16], rope[16:32]], axis=1).astype(BF16)
    for side in range(2):
        rope = [pages[2 * side + i, :, LAT:CACHE].astype(F32) for i in range(2)]
        prope_out[side] = jnp.concatenate(rope, axis=1).astype(BF16)
    pl.semaphore_wait(barrier, 15)
    tell(in_sem.at[0], [grp_peer(2), grp_peer(6)])
    tell(in_sem.at[1], [z_peer(2), z_peer(6)])
    send_queries(0)
    send_queries(1)
    remote(pages.at[0:2, :, 0:LAT], pages.at[4:6, :, 0:LAT], gs_sem.at[0], gr_sem.at[0], grp_peer(1))
    remote(pages.at[2:4, :, 0:LAT], pages.at[6:8, :, 0:LAT], gs_sem.at[0], gr_sem.at[0], grp_peer(7))

    send_sides(0)
    remote(prope_out.at[0], prope_in.at[0], gs_sem.at[1], gr_sem.at[1], grp_peer(1))
    remote(prope_out.at[1], prope_in.at[1], gs_sem.at[1], gr_sem.at[1], grp_peer(7))
    send_sides(1)
    pl.semaphore_wait(in_sem.at[0], 2)
    send_queries(2)
    send_sides(2)
    pl.semaphore_wait(in_sem.at[1], 2)
    for at in range(3):
        tell(in_sem.at[2 + at], [grp_peer(k) for k in groups[at]])

    order = (4, 3, 5, 2, 6, 1, 7)
    take_meta(0)
    take(prope_in, gr_sem.at[1])
    take(pages.at[4:8, :, 0:LAT], gr_sem.at[0])
    for side in range(2):
        rope = prope_in[side].astype(F32)
        for i in range(2):
            pages[4 + 2 * side + i, :, LAT:CACHE] = rope[:, i * ROPE:(i + 1) * ROPE].astype(BF16)
    token = lax.broadcasted_iota(jnp.int32, (1, TOK), 1)
    slot = token // PAGE
    owner_v = jnp.zeros((1, TOK), jnp.int32)
    first_v = jnp.zeros((1, TOK), jnp.int32)
    rows = [(meta, i) for i in range(POOL)] + [(meta_in[0], 0), (meta_in[0], 1), (meta_in[1], 2), (meta_in[1], 3)]
    for i, (row, at) in enumerate(rows):
        owner_v = jnp.where(slot == i, row[:, 1 + at:2 + at], owner_v)
        first_v = jnp.where(slot == i, row[:, 1 + POOL + at:2 + POOL + at], first_v)
    pos_v = first_v * PAGE + token % PAGE
    lane64 = lax.broadcasted_iota(jnp.int32, (HEADS, 128), 1)
    lane32 = lax.broadcasted_iota(jnp.int32, (HH, 128), 1)
    row32 = lax.broadcasted_iota(jnp.int32, (HH, 128), 0)

    def partials(members):
        page_all = pages[...].reshape(TOK, CACHE)
        queries, limits, requests = [], [], []
        for k in members:
            row = meta if k == 0 else meta_in[slots[k]]
            if k == 0:
                queries.append(q_own[pl.ds(parity * HH, HH), :])
            else:
                rope = rope_in[slots[k]].astype(F32)
                rope = jnp.concatenate([rope[:, 0:ROPE], rope[:, ROPE:2 * ROPE]], axis=0).astype(BF16)
                queries.append(jnp.concatenate([q_in[slots[k]], rope], axis=1))
            limits.append(jnp.broadcast_to(row[:, 0:1], (HH, 1)))
            requests.append(jnp.full((HH, 1), lax.rem(g + (GRP - k), GRP), jnp.int32))
        query = jnp.concatenate(queries, axis=0)
        scores = lax.dot_general(query, page_all, (((1,), (1,)), ((), ())),
                                 preferred_element_type=F32) * SCALE
        live = (pos_v < jnp.concatenate(limits, axis=0)) & (owner_v == jnp.concatenate(requests, axis=0))
        top = jnp.max(jnp.where(live, scores, NEG), axis=1, keepdims=True)
        weights = jnp.where(live, jnp.exp(scores - top), 0.0)
        total = jnp.sum(weights, axis=1, keepdims=True)
        value = jnp.dot(weights.astype(BF16), page_all[:, 0:LAT], preferred_element_type=F32)
        return {k: (top[i * HH:(i + 1) * HH], total[i * HH:(i + 1) * HH], value[i * HH:(i + 1) * HH])
                for i, k in enumerate(members)}

    def send_partial(k, part):
        top, total, value = part
        stat_out[k] = jnp.concatenate(
            [jnp.sum(jnp.where(lane32 == row32, column, 0.0), axis=0, keepdims=True) for column in (top, total)], axis=0)
        for i in range(4):
            rows = slice(i * 8, (i + 1) * 8)
            part_out[k, i] = jnp.concatenate([value[rows, 0:256], value[rows, 256:512]], axis=0).astype(BF16)
        at = min(k, 1)
        for i in range(4):
            zz = parity * 4 + i

            def away():
                peer = (lax.rem(g + (GRP - k), GRP), zz * NS + s)
                remote(stat_out.at[k], stat_in.at[k, z], ts_sem.at[at], tr_sem.at[k], peer)
                remote(part_out.at[k, i], part_in.at[k, z], ps_sem.at[at], pr_sem.at[k], peer)

            if k == 0:
                pl.when(zz != z)(away)

                @pl.when(zz == z)
                def _():
                    pltpu.make_async_copy(stat_out.at[k], stat_in.at[k, z], tr_sem.at[k]).start()
                    pltpu.make_async_copy(part_out.at[k, i], part_in.at[k, z], pr_sem.at[k]).start()
            else:
                away()

    for at, members in enumerate(((1, 7, 0), (2, 6), (3, 5, 4))):
        if at:
            take_meta(at)
        take_queries(at)
        done = partials(members)
        pl.semaphore_wait(in_sem.at[2 + at], len(groups[at]))
        for k in members:
            send_partial(k, done[k])

    odd = lax.rem(g + z // 4, 2)
    sources = [even_k + odd * (odd_k - even_k) for even_k, odd_k in ((0, 1), (2, 7), (6, 3), (4, 5))]
    mine = lane64 == lax.rem(z, 4) * 8 + lax.broadcasted_iota(jnp.int32, (HEADS, 128), 0) % 8
    tops, totals = [], []
    for k in sources:
        take(stat_in.at[k], tr_sem.at[k])
        take(part_in.at[k], pr_sem.at[k])
        for at, columns in enumerate((tops, totals)):
            spread = jnp.broadcast_to(stat_in[k, :, at:at + 1, :], (NZ, 8, 128)).reshape(HEADS, 128)
            columns.append(jnp.sum(jnp.where(mine, spread, 0.0), axis=1, keepdims=True))
    best = tops[0]
    for top in tops[1:]:
        best = jnp.maximum(best, top)
    factors = [jnp.exp(top - best) for top in tops]
    denominator = 0.0
    for factor, total in zip(factors, totals):
        denominator = denominator + factor * total
    scale = 1.0 / denominator
    factors = [factor * scale for factor in factors]
    for j in range(4):
        block = 0.0
        for k, factor in zip(sources, factors):
            both = part_in[k, :, :, j % 2 * 128:j % 2 * 128 + 128].astype(F32)
            block = block + factor * both[:, j // 2 * 8:j // 2 * 8 + 8].reshape(HEADS, 128)
        lat[j] = block

    for ss in range(NS):
        quarters = [lat[j, pl.ds(ss, NZ, stride=NS), :] for j in range(4)]
        c2_out[ss] = jnp.concatenate([jnp.concatenate(quarters[0:2], axis=1), jnp.concatenate(quarters[2:4], axis=1)], axis=0).astype(BF16)
    for k in order:
        remote(c2_out.at[lax.rem(s + k, NS)], c2_in.at[s], c2s_sem.at[0], c2r_sem.at[0], s_peer(k))
    pltpu.make_async_copy(c2_out.at[s], c2_in.at[s], c2r_sem.at[0]).start()
    vup_load.wait()
    take(c2_in, c2r_sem.at[0])

    blocks = []
    for dc in (1, 0):
        for dx in range(NX):
            at = lax.rem(x + dx, NX) * 2 + lax.rem(c + dc, 2)
            both = c2_in[at].astype(F32)
            blocks.append(jnp.concatenate([both[0:8, :], both[8:16, :]], axis=1))
    heads_in = jnp.concatenate(blocks, axis=0).astype(BF16)
    head_value = jnp.dot(heads_in, vup[...], preferred_element_type=F32).astype(BF16)

    oproj_load.wait()
    core_peer = (g, z * NS + x * 2 + (1 - c))
    for n in (NX1, 0, 1, 2):
        cols = slice(n * CHUNK, (n + 1) * CHUNK)
        product = jnp.dot(head_value, oproj[:, cols], preferred_element_type=F32)
        e1_out[n] = product[0:32].astype(BF16)
        remote(e1_out.at[n], e1_in.at[n], e1s_sem.at[0], e1r_sem.at[n], core_peer)
        own_f[n] = product[32:64]

    take(e1_in.at[NX1], e1r_sem.at[NX1])
    both = own_f[NX1] + e1_in[NX1].astype(F32)
    for t in range(CT):
        f1_f[t * 32:(t + 1) * 32, :] = both[:, t * 128:(t + 1) * 128]
    f1_f[CT * 32:512, :] = jnp.zeros((512 - CT * 32, 128), F32)
    for zz in range(NZ):
        f1_out[zz] = f1_f[pl.ds(zz, 64, stride=8), :].astype(BF16)
    for k in order:
        remote(f1_out.at[lax.rem(z + k, NZ)], f1_in.at[k], f1s_sem.at[0], f1r_sem.at[0], z_peer(k))

    for n in range(NX1):
        take(e1_in.at[n], e1r_sem.at[n])
        both = own_f[n] + e1_in[n].astype(F32)
        own_f[n] = both
        for dx in (2, 1, 3):
            rows = both[dx * 8:(dx + 1) * 8]
            e2_out[n, dx] = jnp.concatenate([rows[:, 0:CHUNK // 2], rows[:, CHUNK // 2:CHUNK]], axis=0).astype(BF16)
            peer = (g, z * NS + lax.rem(x + dx, NX) * 2 + c)
            remote(e2_out.at[n, dx], e2_in.at[n, dx], e2s_sem.at[0], e2r_sem.at[n], peer)

    for n in range(NX1):
        take(e2_in.at[n, 1:NX], e2r_sem.at[n])
        for t in range(CT):
            half, col = t // (CT // 2), t % (CT // 2) * 128
            total = own_f[n, 0:8, t * 128:(t + 1) * 128]
            for dx in (1, 3, 2):
                total = total + e2_in[n, dx, :, col:col + 128].astype(F32)[half * 8:half * 8 + 8]
            e3_f[n, t * 8:(t + 1) * 8, :] = total
        for zz in range(NZ):
            e3_out[n, zz] = jnp.concatenate(
                [e3_f[n, pl.ds(zz, CT, stride=8), :], jnp.zeros((16 - CT, 128), F32)], axis=0).astype(BF16)
        for k in order:
            to = lax.rem(z + k, NZ)
            remote(e3_out.at[n, to], e3_in.at[n, k], e3s_sem.at[0], e3r_sem.at[n], z_peer(k))

    take(f1_in.at[1:NZ], f1r_sem.at[0])
    total = f1_out[z].astype(F32)
    for k in order:
        total = total + f1_in[k].astype(F32)
    f2_f[...] = total
    for dx in (2, 1, 3):
        f2_out[dx] = f2_f[pl.ds(dx, 16, stride=4), :].astype(BF16)
        peer = (g, z * NS + lax.rem(x + dx, NX) * 2 + c)
        remote(f2_out.at[dx], f2_in.at[dx], f2s_sem.at[0], f2r_sem.at[0], peer)
    f2_own = f2_f[pl.ds(0, 16, stride=4), :]

    def put(n, total):
        for t in range(CT):
            row_f[:, n * CHUNK + t * 128:n * CHUNK + (t + 1) * 128] = total[t:t + 1]

    for n in range(NX1):
        take(e3_in.at[n, 1:NZ], e3r_sem.at[n])
        total = e3_out[n, z].astype(F32)
        for k in order:
            total = total + e3_in[n, k].astype(F32)
        put(n, total)
    take(f2_in.at[1:NX], f2r_sem.at[0])
    total = f2_own
    for dx in (1, 3, 2):
        total = total + f2_in[dx].astype(F32)
    put(NX1, total)
    out_ref[...] = row_f[...].astype(BF16)

    take(q_in.at[0:7], qs_sem.at[0])
    take(meta_in.at[0:7], ms_sem.at[0])
    take(rope_in.at[0:7], rs_sem.at[0])
    take(pages.at[4:8, :, 0:LAT], gs_sem.at[0])
    take(prope_out, gs_sem.at[1])
    take(part_out.at[1:GRP], ps_sem.at[1])
    take(stat_in.at[1:GRP, 0:4], ts_sem.at[1])

    @pl.when(z // 4 == parity)
    def _():
        take(part_out.at[0, 0:3], ps_sem.at[0])
        take(stat_in.at[0, 0:3], ts_sem.at[0])

    @pl.when(z // 4 != parity)
    def _():
        take(part_out.at[0], ps_sem.at[0])
        take(stat_in.at[0, 0:4], ts_sem.at[0])

    take(c2_out.at[1:NS], c2s_sem.at[0])
    take(e1_out, e1s_sem.at[0])
    take(e2_out.at[:, 1:NX], e2s_sem.at[0])
    take(e3_out.at[:, 1:NZ], e3s_sem.at[0])
    take(f1_out.at[1:NZ], f1s_sem.at[0])
    take(f2_out.at[1:NX], f2s_sem.at[0])


def body(queries, lengths, pages, slot_owner, slot_page, value_up, out_proj):
    any_spec = pl.BlockSpec(memory_space=pl.ANY)
    dma = pltpu.SemaphoreType.DMA
    return pl.pallas_call(
        kernel,
        out_shape=jax.ShapeDtypeStruct((1, D), BF16),
        in_specs=[any_spec] * 7,
        out_specs=pl.BlockSpec(memory_space=pltpu.VMEM),
        scratch_shapes=[
            pltpu.SMEM((1,), jnp.int32),
            pltpu.SMEM((POOL,), jnp.int32),
            pltpu.SMEM((POOL,), jnp.int32),
            pltpu.VMEM((HEADS, CACHE), BF16),
            pltpu.VMEM((GRP, HH, LAT), BF16),
            pltpu.VMEM((2, 16, 128), BF16),
            pltpu.VMEM((GRP, 16, 128), BF16),
            pltpu.VMEM((2, PAGE, 128), BF16),
            pltpu.VMEM((2, PAGE, 128), BF16),
            pltpu.VMEM((1, 128), jnp.int32),
            pltpu.VMEM((GRP, 1, 128), jnp.int32),
            pltpu.VMEM((2 * POOL, PAGE, CACHE), BF16),
            pltpu.VMEM((LAT, VDIM), BF16),
            pltpu.VMEM((VDIM, D), BF16),
            pltpu.VMEM((GRP, 4, 16, 256), BF16),
            pltpu.VMEM((GRP, NZ, 16, 256), BF16),
            pltpu.VMEM((GRP, 2, 128), F32),
            pltpu.VMEM((GRP, NZ, 2, 128), F32),
            pltpu.VMEM((1, D), F32),
            pltpu.VMEM((4, HEADS, 128), F32),
            pltpu.VMEM((NS, 16, 256), BF16),
            pltpu.VMEM((NS, 16, 256), BF16),
            pltpu.VMEM((NCH, 32, CHUNK), F32),
            pltpu.VMEM((NCH, 32, CHUNK), BF16),
            pltpu.VMEM((NCH, 32, CHUNK), BF16),
            pltpu.VMEM((NX1, NX, 16, CHUNK // 2), BF16),
            pltpu.VMEM((NX1, NX, 16, CHUNK // 2), BF16),
            pltpu.VMEM((NX1, CT * 8, 128), F32),
            pltpu.VMEM((NX1, NZ, 16, 128), BF16),
            pltpu.VMEM((NX1, NZ, 16, 128), BF16),
            pltpu.VMEM((512, 128), F32),
            pltpu.VMEM((NZ, 64, 128), BF16),
            pltpu.VMEM((NZ, 64, 128), BF16),
            pltpu.VMEM((64, 128), F32),
            pltpu.VMEM((NX, 16, 128), BF16),
            pltpu.VMEM((NX, 16, 128), BF16),
            dma((7,)), pltpu.SemaphoreType.REGULAR((5,)),
            dma((1,)), dma((3,)), dma((2,)), dma((2,)), dma((1,)), dma((3,)), dma((1,)), dma((3,)),
            dma((2,)), dma((GRP,)), dma((2,)), dma((GRP,)), dma((1,)), dma((1,)),
            dma((1,)), dma((NCH,)), dma((1,)), dma((NX1,)), dma((1,)), dma((NX1,)), dma((1,)), dma((1,)), dma((1,)), dma((1,)),
        ],
        compiler_params=pltpu.CompilerParams(
            collective_id=0, has_side_effects=True, vmem_limit_bytes=60 * 1024 * 1024),
    )(queries, lengths, pages, slot_owner, slot_page, value_up, out_proj)


def solution(mesh):
    in_specs = (
        P(("grp", "dev"), None, None),
        P(("grp", "dev")),
        P(("grp", "dev"), None, None),
        P(("grp", "dev")),
        P(("grp", "dev")),
        P("dev", None, None),
        P("dev", None),
    )
    out_specs = P(("grp", "dev"), None)
    return jax.shard_map(body, mesh=mesh, in_specs=in_specs, out_specs=out_specs, check_vma=False)
```

```python
import jax
import jax.numpy as jnp
from jax import lax
from jax.experimental import pallas as pl
from jax.experimental.pallas import tpu as pltpu
from jax.sharding import PartitionSpec as P

MESH = pl.DeviceIdType.MESH
F32 = jnp.float32
BF16 = jnp.bfloat16

ROPE = 64
NOPE = 128
SCALE = (NOPE + ROPE) ** -0.5
NEG = -1e30

GRP = 8
NZ = 8
NS = 8
NX = 4
HEADS = 64
LAT = 512
CACHE = 576
HH = HEADS // 2
PAGE = 64
POOL = 4
TOK = 2 * POOL * PAGE
VDIM = 128
D = 7168
HALF = D // 2
TILES = D // 128
CHUNKS = ((0, 9), (9, 9))
LAST, LT = 18, 10


def kernel(q_hbm, len_hbm, pages_hbm, owner_hbm, page_hbm, vup_hbm, oproj_hbm, out_ref,
           len_ref, owner_ref, page_ref, q_own, q_in, rope_own, rope_in, prope_out, prope_in, meta_own, meta_in, pages, vup, oproj, part_out, part_in, stat_out, stat_in,
           row_f, lat, c2_out, c2_in, own_f, e2_out, e2_in, e3_f, e3_out, e3_in, f1_f, f1_out, f1_in, f2_f, f2_out, f2_in, sent,
           loc_sem, in_sem, ms_sem, mr_sem, gs_sem, gr_sem, qs_sem, qr_sem, rs_sem, rr_sem, ps_sem, pr_sem, ts_sem, tr_sem,
           c2s_sem, c2r_sem, vs_sem, vr_sem, ws_sem, wr_sem, e2s_sem, e2r_sem, e3s_sem, e3r_sem, f1s_sem, f1r_sem, f2s_sem, f2r_sem):
    g = lax.axis_index("grp")
    d = lax.axis_index("dev")
    z = d // NS
    s = d % NS
    x = s // 2
    c = s % 2

    def grp_peer(k):
        return (lax.rem(g + k, GRP), d)

    def z_peer(k):
        return (g, lax.rem(z + k, NZ) * NS + s)

    def s_peer(k):
        return (g, z * NS + lax.rem(s + k, NS))

    barrier = pltpu.get_barrier_semaphore()
    near = [f(k) for f in (grp_peer, z_peer) for k in (1, 7, 2, 6)] + [s_peer(k) for k in range(1, 8)]
    for peer in near:
        pl.semaphore_signal(barrier, inc=1, device_id=peer, device_id_type=MESH)

    q_load = pltpu.make_async_copy(q_hbm.at[0], q_own, loc_sem.at[0])
    q_load.start()
    number_loads = [pltpu.make_async_copy(src, dst, loc_sem.at[4 + at]) for at, (src, dst) in
                    enumerate(((len_hbm, len_ref), (owner_hbm, owner_ref), (page_hbm, page_ref)))]
    for load in number_loads:
        load.start()
    pages_load = pltpu.make_async_copy(pages_hbm, pages.at[0:POOL], loc_sem.at[1])
    pages_load.start()
    vup_load = pltpu.make_async_copy(vup_hbm.at[0], vup.at[c], loc_sem.at[2])
    vup_load.start()
    def columns(core):
        return oproj_hbm.at[:, pl.ds(pl.multiple_of(core * HALF, 128), HALF)]

    oproj_load = pltpu.make_async_copy(columns(c), oproj.at[c], loc_sem.at[3])
    oproj_load.start()

    def tell(sem, peers):
        for peer in peers:
            pl.semaphore_signal(sem, inc=1, device_id=peer, device_id_type=MESH)

    def remote(src, dst, send, recv, peer):
        copy = pltpu.make_async_remote_copy(
            src_ref=src, dst_ref=dst, send_sem=send, recv_sem=recv,
            device_id=peer, device_id_type=MESH)
        copy.start()
        return copy

    def take(ref, sem):
        pltpu.make_async_copy(ref, ref, sem).wait()

    parity = lax.rem(g, 2)
    slots = {1: 0, 7: 1, 2: 2, 6: 3, 3: 4, 5: 5, 4: 6}
    groups = ((1, 7), (2, 6), (3, 5, 4))

    def send_queries(at):
        for k in groups[at]:
            remote(q_own.at[pl.ds(lax.rem(g + k, 2) * HH, HH), 0:LAT], q_in.at[slots[k]], qs_sem.at[0], qr_sem.at[at], grp_peer(k))

    def send_sides(at):
        for k in groups[at]:
            remote(meta_own, meta_in.at[slots[k]], ms_sem.at[0], mr_sem.at[at], grp_peer(k))
            remote(rope_own.at[lax.rem(g + k, 2)], rope_in.at[slots[k]], rs_sem.at[0], rr_sem.at[at], grp_peer(k))

    def take_queries(at):
        first, count = slots[groups[at][0]], len(groups[at])
        take(rope_in.at[first:first + count], rr_sem.at[at])
        take(q_in.at[first:first + count], qr_sem.at[at])

    def take_meta(at):
        first, count = slots[groups[at][0]], len(groups[at])
        take(meta_in.at[first:first + count], mr_sem.at[at])

    q_load.wait()
    pages_load.wait()
    for load in number_loads:
        load.wait()
    lane = lax.broadcasted_iota(jnp.int32, (1, 128), 1)
    meta = jnp.where(lane == 0, len_ref[0], 0)
    for i in range(POOL):
        meta = jnp.where(lane == 1 + i, owner_ref[i], meta)
        meta = jnp.where(lane == 1 + POOL + i, page_ref[i], meta)
    meta_own[...] = meta
    for half in range(2):
        rope = q_own[half * HH:(half + 1) * HH, LAT:CACHE].astype(F32)
        rope_own[half] = jnp.concatenate([rope[0:16], rope[16:32]], axis=1).astype(BF16)
    for side in range(2):
        rope = [pages[2 * side + i, :, LAT:CACHE].astype(F32) for i in range(2)]
        prope_out[side] = jnp.concatenate(rope, axis=1).astype(BF16)
    pl.semaphore_wait(barrier, 15)
    tell(in_sem.at[0], [grp_peer(2), grp_peer(6)])
    tell(in_sem.at[1], [z_peer(2), z_peer(6)])
    send_queries(0)
    send_queries(1)
    remote(pages.at[0:2, :, 0:LAT], pages.at[4:6, :, 0:LAT], gs_sem.at[0], gr_sem.at[0], grp_peer(1))
    remote(pages.at[2:4, :, 0:LAT], pages.at[6:8, :, 0:LAT], gs_sem.at[0], gr_sem.at[0], grp_peer(7))

    send_sides(0)
    remote(prope_out.at[0], prope_in.at[0], gs_sem.at[1], gr_sem.at[1], grp_peer(1))
    remote(prope_out.at[1], prope_in.at[1], gs_sem.at[1], gr_sem.at[1], grp_peer(7))
    send_sides(1)

    core_peer = (g, z * NS + x * 2 + (1 - c))
    remote(vup_hbm.at[0], vup.at[c], vs_sem.at[0], vr_sem.at[0], core_peer)
    remote(columns(1 - c), oproj.at[c], ws_sem.at[0], wr_sem.at[0], core_peer)
    pl.semaphore_wait(in_sem.at[0], 2)
    send_queries(2)
    send_sides(2)
    pl.semaphore_wait(in_sem.at[1], 2)
    for at in range(3):
        tell(in_sem.at[2 + at], [grp_peer(k) for k in groups[at]])

    order = (4, 3, 5, 2, 6, 1, 7)
    take_meta(0)
    take(prope_in, gr_sem.at[1])
    take(pages.at[4:8, :, 0:LAT], gr_sem.at[0])
    for side in range(2):
        rope = prope_in[side].astype(F32)
        for i in range(2):
            pages[4 + 2 * side + i, :, LAT:CACHE] = rope[:, i * ROPE:(i + 1) * ROPE].astype(BF16)
    token = lax.broadcasted_iota(jnp.int32, (1, TOK), 1)
    slot = token // PAGE
    owner_v = jnp.zeros((1, TOK), jnp.int32)
    first_v = jnp.zeros((1, TOK), jnp.int32)
    rows = [(meta, i) for i in range(POOL)] + [(meta_in[0], 0), (meta_in[0], 1), (meta_in[1], 2), (meta_in[1], 3)]
    for i, (row, at) in enumerate(rows):
        owner_v = jnp.where(slot == i, row[:, 1 + at:2 + at], owner_v)
        first_v = jnp.where(slot == i, row[:, 1 + POOL + at:2 + POOL + at], first_v)
    pos_v = first_v * PAGE + token % PAGE
    lane64 = lax.broadcasted_iota(jnp.int32, (HEADS, 128), 1)
    lane32 = lax.broadcasted_iota(jnp.int32, (HH, 128), 1)
    row32 = lax.broadcasted_iota(jnp.int32, (HH, 128), 0)

    def partials(members):
        page_all = pages[...].reshape(TOK, CACHE)
        queries, limits, requests = [], [], []
        for k in members:
            row = meta if k == 0 else meta_in[slots[k]]
            if k == 0:
                queries.append(q_own[pl.ds(parity * HH, HH), :])
            else:
                rope = rope_in[slots[k]].astype(F32)
                rope = jnp.concatenate([rope[:, 0:ROPE], rope[:, ROPE:2 * ROPE]], axis=0).astype(BF16)
                queries.append(jnp.concatenate([q_in[slots[k]], rope], axis=1))
            limits.append(jnp.broadcast_to(row[:, 0:1], (HH, 1)))
            requests.append(jnp.full((HH, 1), lax.rem(g + (GRP - k), GRP), jnp.int32))
        query = jnp.concatenate(queries, axis=0)
        scores = lax.dot_general(query, page_all, (((1,), (1,)), ((), ())),
                                 preferred_element_type=F32) * SCALE
        live = (pos_v < jnp.concatenate(limits, axis=0)) & (owner_v == jnp.concatenate(requests, axis=0))
        top = jnp.max(jnp.where(live, scores, NEG), axis=1, keepdims=True)
        weights = jnp.where(live, jnp.exp(scores - top), 0.0)
        total = jnp.sum(weights, axis=1, keepdims=True)
        value = jnp.dot(weights.astype(BF16), page_all[:, 0:LAT], preferred_element_type=F32)
        return {k: (top[i * HH:(i + 1) * HH], total[i * HH:(i + 1) * HH], value[i * HH:(i + 1) * HH])
                for i, k in enumerate(members)}

    def send_partial(k, part):
        top, total, value = part
        stat_out[k] = jnp.concatenate(
            [jnp.sum(jnp.where(lane32 == row32, column, 0.0), axis=0, keepdims=True) for column in (top, total)], axis=0)
        for i in range(4):
            rows = slice(i * 8, (i + 1) * 8)
            part_out[k, i] = jnp.concatenate([value[rows, 0:256], value[rows, 256:512]], axis=0).astype(BF16)
        at = min(k, 1)
        for i in range(4):
            zz = parity * 4 + i

            def away():
                peer = (lax.rem(g + (GRP - k), GRP), zz * NS + s)
                remote(stat_out.at[k], stat_in.at[k, z], ts_sem.at[at], tr_sem.at[k], peer)
                remote(part_out.at[k, i], part_in.at[k, z], ps_sem.at[at], pr_sem.at[k], peer)

            if k == 0:
                pl.when(zz != z)(away)

                @pl.when(zz == z)
                def _():
                    pltpu.make_async_copy(stat_out.at[k], stat_in.at[k, z], tr_sem.at[k]).start()
                    pltpu.make_async_copy(part_out.at[k, i], part_in.at[k, z], pr_sem.at[k]).start()
            else:
                away()

    for at, members in enumerate(((1, 7, 0), (2, 6), (3, 5, 4))):
        if at:
            take_meta(at)
        take_queries(at)
        done = partials(members)
        pl.semaphore_wait(in_sem.at[2 + at], len(groups[at]))
        for k in members:
            send_partial(k, done[k])

    odd = lax.rem(g + z // 4, 2)
    sources = [even_k + odd * (odd_k - even_k) for even_k, odd_k in ((0, 1), (2, 7), (6, 3), (4, 5))]
    mine = lane64 == lax.rem(z, 4) * 8 + lax.broadcasted_iota(jnp.int32, (HEADS, 128), 0) % 8
    tops, totals = [], []
    for k in sources:
        take(stat_in.at[k], tr_sem.at[k])
        take(part_in.at[k], pr_sem.at[k])
        for at, columns in enumerate((tops, totals)):
            spread = jnp.broadcast_to(stat_in[k, :, at:at + 1, :], (NZ, 8, 128)).reshape(HEADS, 128)
            columns.append(jnp.sum(jnp.where(mine, spread, 0.0), axis=1, keepdims=True))
    best = tops[0]
    for top in tops[1:]:
        best = jnp.maximum(best, top)
    factors = [jnp.exp(top - best) for top in tops]
    denominator = 0.0
    for factor, total in zip(factors, totals):
        denominator = denominator + factor * total
    scale = 1.0 / denominator
    factors = [factor * scale for factor in factors]
    for j in range(4):
        block = 0.0
        for k, factor in zip(sources, factors):
            both = part_in[k, :, :, j % 2 * 128:j % 2 * 128 + 128].astype(F32)
            block = block + factor * both[:, j // 2 * 8:j // 2 * 8 + 8].reshape(HEADS, 128)
        lat[j, 0:HEADS, :] = block

    for xx in range(NX):
        for core in range(2):
            quarters = [lat[j, pl.ds(xx * 2 + core, NZ, stride=NS), :] for j in range(4)]
            c2_out[xx, core * 16:(core + 1) * 16, :] = jnp.concatenate(
                [jnp.concatenate(quarters[0:2], axis=1), jnp.concatenate(quarters[2:4], axis=1)], axis=0).astype(BF16)
    for k in order:
        to = lax.rem(s + k, NS)
        remote(c2_out.at[to // 2], c2_in.at[s], c2s_sem.at[0], c2r_sem.at[0], (g, z * NS + to))
    pltpu.make_async_copy(c2_out.at[x], c2_in.at[s], c2r_sem.at[0]).start()
    vup_load.wait()
    take(vup.at[0], vr_sem.at[0])
    take(c2_in, c2r_sem.at[0])

    blocks = [[], []]
    for dx in range(NX):
        for core in range(2):
            both = c2_in[lax.rem(x + dx, NX) * 2 + core].astype(F32)
            for head in range(2):
                blocks[head].append(jnp.concatenate([both[head * 16:head * 16 + 8], both[head * 16 + 8:head * 16 + 16]], axis=1))
    head_value = jnp.concatenate(
        [jnp.dot(jnp.concatenate(blocks[head], axis=0).astype(BF16), vup[head], preferred_element_type=F32) for head in range(2)],
        axis=1).astype(BF16)

    oproj_load.wait()
    take(oproj.at[0], wr_sem.at[0])

    def product(first, count):
        cols = slice(first * 128, (first + count) * 128)
        return jnp.dot(head_value, oproj[:, :, cols].reshape(2 * VDIM, count * 128), preferred_element_type=F32)

    for n, (first, count) in enumerate(CHUNKS):
        both = product(first, count)
        own_f[:, first * 128:(first + count) * 128] = both[0:16]
        for dx in (2, 1, 3):
            cols = slice(first * 128, (first + count) * 128)
            e2_out[dx, :, cols] = both[dx * 16:(dx + 1) * 16].astype(BF16)
            peer = (g, z * NS + lax.rem(x + dx, NX) * 2 + c)
            remote(e2_out.at[dx, :, cols], e2_in.at[dx, :, cols], e2s_sem.at[n], e2r_sem.at[n], peer)
        if n == 0:
            both = product(LAST, LT)
            for t in range(LT):
                f1_f[t * HEADS:(t + 1) * HEADS, :] = both[:, t * 128:(t + 1) * 128]
            for zz in range(NZ):
                f1_out[zz] = f1_f[pl.ds(zz, LT * 8, stride=8), :].astype(BF16)
            for k in order:
                remote(f1_out.at[lax.rem(z + k, NZ)], f1_in.at[k], f1s_sem.at[0], f1r_sem.at[0], z_peer(k))

    for n, (first, count) in enumerate(CHUNKS):
        cols = slice(first * 128, (first + count) * 128)
        take(e2_in.at[1:NX, :, cols], e2r_sem.at[n])
        total = own_f[:, cols]
        for dx in (1, 3, 2):
            total = total + e2_in[dx, :, cols].astype(F32)
        for t in range(count):
            e3_f[n, t * 16:(t + 1) * 16, :] = total[:, t * 128:(t + 1) * 128]
        for zz in range(NZ):
            for core in range(2):
                rows = e3_f[n, pl.ds(core * 8 + zz, count, stride=16), :]
                e3_out[n, zz, core] = jnp.concatenate([rows, jnp.zeros((16 - count, 128), F32)], axis=0).astype(BF16)
        for k in order:
            to = lax.rem(z + k, NZ)
            for core in range(2):
                remote(e3_out.at[n, to, core], e3_in.at[n, c, k], e3s_sem.at[n], e3r_sem.at[n], (g, to * NS + x * 2 + core))
        remote(e3_out.at[n, z, 1 - c], e3_in.at[n, c, 0], e3s_sem.at[n], e3r_sem.at[n], core_peer)
        pltpu.make_async_copy(e3_out.at[n, z, c], e3_in.at[n, c, 0], e3r_sem.at[n]).start()

    take(f1_in.at[1:NZ], f1r_sem.at[0])
    total = f1_out[z].astype(F32)
    for k in order:
        total = total + f1_in[k].astype(F32)
    f2_f[0:80, :] = total
    for dx in (2, 1, 3, 0):
        for core in range(2):
            f2_out[dx, core] = jnp.concatenate([f2_f[pl.ds(dx * 2 + core, 10, stride=8), :], jnp.zeros((6, 128), F32)], axis=0).astype(BF16)
    for dx in (2, 1, 3):
        for core in range(2):
            peer = (g, z * NS + lax.rem(x + dx, NX) * 2 + core)
            remote(f2_out.at[dx, core], f2_in.at[c, dx], f2s_sem.at[0], f2r_sem.at[0], peer)
    remote(f2_out.at[0, 1 - c], f2_in.at[c, 0], f2s_sem.at[0], f2r_sem.at[0], core_peer)
    pltpu.make_async_copy(f2_out.at[0, c], f2_in.at[c, 0], f2r_sem.at[0]).start()

    def put(core, first, count, total):
        for t in range(count):
            at = core * HALF + (first + t) * 128
            row_f[:, at:at + 128] = total[t:t + 1]

    for n, (first, count) in enumerate(CHUNKS):
        take(e3_in.at[n], e3r_sem.at[n])
        for core in range(2):
            put(core, first, count, jnp.sum(e3_in[n, core].astype(F32), axis=0))
    take(f2_in, f2r_sem.at[0])
    for core in range(2):
        put(core, LAST, LT, jnp.sum(f2_in[core].astype(F32), axis=0))
    out_ref[...] = row_f[...].astype(BF16)

    take(q_in.at[0:7], qs_sem.at[0])
    take(meta_in.at[0:7], ms_sem.at[0])
    take(rope_in.at[0:7], rs_sem.at[0])
    take(pages.at[4:8, :, 0:LAT], gs_sem.at[0])
    take(prope_out, gs_sem.at[1])
    take(part_out.at[1:GRP], ps_sem.at[1])
    take(stat_in.at[1:GRP, 0:4], ts_sem.at[1])

    @pl.when(z // 4 == parity)
    def _():
        take(part_out.at[0, 0:3], ps_sem.at[0])
        take(stat_in.at[0, 0:3], ts_sem.at[0])

    @pl.when(z // 4 != parity)
    def _():
        take(part_out.at[0], ps_sem.at[0])
        take(stat_in.at[0, 0:4], ts_sem.at[0])

    take(c2_in.at[1:NS], c2s_sem.at[0])
    take(vup.at[0], vs_sem.at[0])
    take(oproj.at[0], ws_sem.at[0])
    for n, (first, count) in enumerate(CHUNKS):
        take(e2_out.at[1:NX, :, first * 128:(first + count) * 128], e2s_sem.at[n])
        take(sent.at[0:15], e3s_sem.at[n])
    take(f1_out.at[1:NZ], f1s_sem.at[0])
    take(sent.at[0:7], f2s_sem.at[0])


def body(queries, lengths, pages, slot_owner, slot_page, value_up, out_proj):
    any_spec = pl.BlockSpec(memory_space=pl.ANY)
    dma = pltpu.SemaphoreType.DMA
    return pl.pallas_call(
        kernel,
        out_shape=jax.ShapeDtypeStruct((1, D), BF16),
        in_specs=[any_spec] * 7,
        out_specs=pl.BlockSpec(memory_space=pltpu.VMEM),
        scratch_shapes=[
            pltpu.SMEM((1,), jnp.int32),
            pltpu.SMEM((POOL,), jnp.int32),
            pltpu.SMEM((POOL,), jnp.int32),
            pltpu.VMEM((HEADS, CACHE), BF16),
            pltpu.VMEM((GRP, HH, LAT), BF16),
            pltpu.VMEM((2, 16, 128), BF16),
            pltpu.VMEM((GRP, 16, 128), BF16),
            pltpu.VMEM((2, PAGE, 128), BF16),
            pltpu.VMEM((2, PAGE, 128), BF16),
            pltpu.VMEM((1, 128), jnp.int32),
            pltpu.VMEM((GRP, 1, 128), jnp.int32),
            pltpu.VMEM((2 * POOL, PAGE, CACHE), BF16),
            pltpu.VMEM((2, LAT, VDIM), BF16),
            pltpu.VMEM((2, VDIM, HALF), BF16),
            pltpu.VMEM((GRP, 4, 16, 256), BF16),
            pltpu.VMEM((GRP, NZ, 16, 256), BF16),
            pltpu.VMEM((GRP, 2, 128), F32),
            pltpu.VMEM((GRP, NZ, 2, 128), F32),
            pltpu.VMEM((1, D), F32),
            pltpu.VMEM((4, HEADS + 8, 128), F32),
            pltpu.VMEM((NX, 32, 256), BF16),
            pltpu.VMEM((NS, 32, 256), BF16),
            pltpu.VMEM((16, LAST * 128), F32),
            pltpu.VMEM((NX, 16, LAST * 128), BF16),
            pltpu.VMEM((NX, 16, LAST * 128), BF16),
            pltpu.VMEM((2, 14 * 16 + 16, 128), F32),
            pltpu.VMEM((2, NZ, 2, 16, 128), BF16),
            pltpu.VMEM((2, 2, NZ, 16, 128), BF16),
            pltpu.VMEM((LT * HEADS + 8, 128), F32),
            pltpu.VMEM((NZ, 80, 128), BF16),
            pltpu.VMEM((NZ, 80, 128), BF16),
            pltpu.VMEM((80+8, 128), F32),
            pltpu.VMEM((NX, 2, 16, 128), BF16),
            pltpu.VMEM((2, NX, 16, 128), BF16),
            pltpu.VMEM((16, 16, 128), BF16),
            dma((7,)), pltpu.SemaphoreType.REGULAR((5,)),
            dma((1,)), dma((3,)), dma((2,)), dma((2,)), dma((1,)), dma((3,)), dma((1,)), dma((3,)),
            dma((2,)), dma((GRP,)), dma((2,)), dma((GRP,)),
            dma((1,)), dma((1,)), dma((1,)), dma((1,)), dma((1,)), dma((1,)),
            dma((2,)), dma((2,)), dma((2,)), dma((2,)), dma((1,)), dma((1,)), dma((1,)), dma((1,)),
        ],
        compiler_params=pltpu.CompilerParams(
            collective_id=0, has_side_effects=True, vmem_limit_bytes=60 * 1024 * 1024),
    )(queries, lengths, pages, slot_owner, slot_page, value_up, out_proj)


def solution(mesh):
    in_specs = (
        P(("grp", "dev"), None, None),
        P(("grp", "dev")),
        P(("grp", "dev"), None, None),
        P(("grp", "dev")),
        P(("grp", "dev")),
        P("dev", None, None),
        P("dev", None),
    )
    out_specs = P(("grp", "dev"), None)
    return jax.shard_map(body, mesh=mesh, in_specs=in_specs, out_specs=out_specs, check_vma=False)
```

```python
import jax
import jax.numpy as jnp
from jax import lax
from jax.experimental import pallas as pl
from jax.experimental.pallas import tpu as pltpu
from jax.sharding import PartitionSpec as P

MESH = pl.DeviceIdType.MESH
F32 = jnp.float32
BF16 = jnp.bfloat16

ROPE = 64
NOPE = 128
SCALE = (NOPE + ROPE) ** -0.5
NEG = -1e30

GRP = 8
NZ = 8
NS = 8
NX = 4
HEADS = 64
LAT = 512
CACHE = 576
HH = HEADS // 2
PAGE = 64
POOL = 4
TOK = 2 * POOL * PAGE
VDIM = 128
D = 7168
HALF = D // 2
TILES = D // 128
CHUNKS = ((0, 9), (9, 9))
LAST, LT = 18, 10


def kernel(q_hbm, len_hbm, pages_hbm, owner_hbm, page_hbm, vup_hbm, oproj_hbm, out_ref,
           len_ref, owner_ref, page_ref, q_own, q_in, rope_own, rope_in, prope_out, prope_in, meta_own, meta_in, pages, vup, oproj, part_out, part_in, stat_out, stat_in,
           row_f, lat, c2_out, c2_in, own_f, e2_out, e2_in, e3_f, e3_out, e3_in, f1_f, f1_out, f1_in, f2_f, f2_out, f2_in, sent,
           loc_sem, in_sem, ms_sem, mr_sem, gs_sem, gr_sem, qs_sem, qr_sem, rs_sem, rr_sem, ps_sem, pr_sem, ts_sem, tr_sem,
           c2s_sem, c2r_sem, vs_sem, vr_sem, ws_sem, wr_sem, e2s_sem, e2r_sem, e3s_sem, e3r_sem, f1s_sem, f1r_sem, f2s_sem, f2r_sem):
    g = lax.axis_index("grp")
    d = lax.axis_index("dev")
    z = d // NS
    s = d % NS
    x = s // 2
    c = s % 2

    def grp_peer(k):
        return (lax.rem(g + k, GRP), d)

    def z_peer(k):
        return (g, lax.rem(z + k, NZ) * NS + s)

    def s_peer(k):
        return (g, z * NS + lax.rem(s + k, NS))

    barrier = pltpu.get_barrier_semaphore()
    core_peer = (g, z * NS + x * 2 + (1 - c))
    near = [grp_peer(1), grp_peer(7), z_peer(1), z_peer(7), s_peer(2), s_peer(6), core_peer]
    for peer in near:
        pl.semaphore_signal(barrier, inc=1, device_id=peer, device_id_type=MESH)

    q_load = pltpu.make_async_copy(q_hbm.at[0], q_own, loc_sem.at[0])
    q_load.start()
    number_loads = [pltpu.make_async_copy(src, dst, loc_sem.at[4 + at]) for at, (src, dst) in
                    enumerate(((len_hbm, len_ref), (owner_hbm, owner_ref), (page_hbm, page_ref)))]
    for load in number_loads:
        load.start()
    pages_load = pltpu.make_async_copy(pages_hbm, pages.at[0:POOL], loc_sem.at[1])
    pages_load.start()
    vup_load = pltpu.make_async_copy(vup_hbm.at[0], vup.at[c], loc_sem.at[2])
    vup_load.start()
    def columns(core):
        return oproj_hbm.at[:, pl.ds(pl.multiple_of(core * HALF, 128), HALF)]

    oproj_load = pltpu.make_async_copy(columns(c), oproj.at[c], loc_sem.at[3])
    oproj_load.start()

    def tell(sem, peers):
        for peer in peers:
            pl.semaphore_signal(sem, inc=1, device_id=peer, device_id_type=MESH)

    def remote(src, dst, send, recv, peer):
        copy = pltpu.make_async_remote_copy(
            src_ref=src, dst_ref=dst, send_sem=send, recv_sem=recv,
            device_id=peer, device_id_type=MESH)
        copy.start()
        return copy

    def take(ref, sem):
        pltpu.make_async_copy(ref, ref, sem).wait()

    parity = lax.rem(g, 2)
    slots = {1: 0, 7: 1, 2: 2, 6: 3, 3: 4, 5: 5, 4: 6}
    groups = ((1, 7), (2, 6), (3, 5, 4))

    def send_queries(at):
        for k in groups[at]:
            remote(q_own.at[pl.ds(lax.rem(g + k, 2) * HH, HH), 0:LAT], q_in.at[slots[k]], qs_sem.at[0], qr_sem.at[at], grp_peer(k))

    def send_sides(at):
        for k in groups[at]:
            remote(meta_own, meta_in.at[slots[k]], ms_sem.at[0], mr_sem.at[at], grp_peer(k))
            remote(rope_own.at[lax.rem(g + k, 2)], rope_in.at[slots[k]], rs_sem.at[0], rr_sem.at[at], grp_peer(k))

    def take_queries(at):
        first, count = slots[groups[at][0]], len(groups[at])
        take(rope_in.at[first:first + count], rr_sem.at[at])
        take(q_in.at[first:first + count], qr_sem.at[at])

    def take_meta(at):
        first, count = slots[groups[at][0]], len(groups[at])
        take(meta_in.at[first:first + count], mr_sem.at[at])

    q_load.wait()
    pages_load.wait()
    for load in number_loads:
        load.wait()
    lane = lax.broadcasted_iota(jnp.int32, (1, 128), 1)
    meta = jnp.where(lane == 0, len_ref[0], 0)
    for i in range(POOL):
        meta = jnp.where(lane == 1 + i, owner_ref[i], meta)
        meta = jnp.where(lane == 1 + POOL + i, page_ref[i], meta)
    meta_own[...] = meta
    for half in range(2):
        rope = q_own[half * HH:(half + 1) * HH, LAT:CACHE].astype(F32)
        rope_own[half] = jnp.concatenate([rope[0:16], rope[16:32]], axis=1).astype(BF16)
    for side in range(2):
        rope = [pages[2 * side + i, :, LAT:CACHE].astype(F32) for i in range(2)]
        prope_out[side] = jnp.concatenate(rope, axis=1).astype(BF16)

    pl.semaphore_wait(barrier, 7)
    tell(in_sem.at[0], [grp_peer(1), grp_peer(7)])
    tell(in_sem.at[1], [z_peer(1), z_peer(7)])
    tell(in_sem.at[6], [s_peer(2), s_peer(6), core_peer])
    send_queries(0)
    send_sides(0)
    remote(pages.at[0:2, :, 0:LAT], pages.at[4:6, :, 0:LAT], gs_sem.at[0], gr_sem.at[0], grp_peer(1))
    remote(pages.at[2:4, :, 0:LAT], pages.at[6:8, :, 0:LAT], gs_sem.at[0], gr_sem.at[0], grp_peer(7))
    remote(prope_out.at[0], prope_in.at[0], gs_sem.at[1], gr_sem.at[1], grp_peer(1))
    remote(prope_out.at[1], prope_in.at[1], gs_sem.at[1], gr_sem.at[1], grp_peer(7))
    remote(vup_hbm.at[0], vup.at[c], vs_sem.at[0], vr_sem.at[0], core_peer)
    remote(columns(1 - c), oproj.at[c], ws_sem.at[0], wr_sem.at[0], core_peer)
    pl.semaphore_wait(in_sem.at[0], 2)
    tell(in_sem.at[5], [grp_peer(2), grp_peer(6)])
    send_queries(1)
    send_sides(1)
    pl.semaphore_wait(in_sem.at[1], 2)
    tell(in_sem.at[7], [z_peer(2), z_peer(6)])
    pl.semaphore_wait(in_sem.at[6], 3)
    tell(in_sem.at[8], [s_peer(2), s_peer(6)])
    pl.semaphore_wait(in_sem.at[5], 2)
    send_queries(2)
    send_sides(2)
    pl.semaphore_wait(in_sem.at[7], 2)
    for at in range(3):
        tell(in_sem.at[2 + at], [grp_peer(k) for k in groups[at]])

    order = (4, 3, 5, 2, 6, 1, 7)
    take_meta(0)
    take(prope_in, gr_sem.at[1])
    take(pages.at[4:8, :, 0:LAT], gr_sem.at[0])
    for side in range(2):
        rope = prope_in[side].astype(F32)
        for i in range(2):
            pages[4 + 2 * side + i, :, LAT:CACHE] = rope[:, i * ROPE:(i + 1) * ROPE].astype(BF16)
    token = lax.broadcasted_iota(jnp.int32, (1, TOK), 1)
    slot = token // PAGE
    owner_v = jnp.zeros((1, TOK), jnp.int32)
    first_v = jnp.zeros((1, TOK), jnp.int32)
    rows = [(meta, i) for i in range(POOL)] + [(meta_in[0], 0), (meta_in[0], 1), (meta_in[1], 2), (meta_in[1], 3)]
    for i, (row, at) in enumerate(rows):
        owner_v = jnp.where(slot == i, row[:, 1 + at:2 + at], owner_v)
        first_v = jnp.where(slot == i, row[:, 1 + POOL + at:2 + POOL + at], first_v)
    pos_v = first_v * PAGE + token % PAGE
    lane64 = lax.broadcasted_iota(jnp.int32, (HEADS, 128), 1)
    lane32 = lax.broadcasted_iota(jnp.int32, (HH, 128), 1)
    row32 = lax.broadcasted_iota(jnp.int32, (HH, 128), 0)

    def partials(members):
        page_all = pages[...].reshape(TOK, CACHE)
        queries, limits, requests = [], [], []
        for k in members:
            row = meta if k == 0 else meta_in[slots[k]]
            if k == 0:
                queries.append(q_own[pl.ds(parity * HH, HH), :])
            else:
                rope = rope_in[slots[k]].astype(F32)
                rope = jnp.concatenate([rope[:, 0:ROPE], rope[:, ROPE:2 * ROPE]], axis=0).astype(BF16)
                queries.append(jnp.concatenate([q_in[slots[k]], rope], axis=1))
            limits.append(jnp.broadcast_to(row[:, 0:1], (HH, 1)))
            requests.append(jnp.full((HH, 1), lax.rem(g + (GRP - k), GRP), jnp.int32))
        query = jnp.concatenate(queries, axis=0)
        scores = lax.dot_general(query, page_all, (((1,), (1,)), ((), ())),
                                 preferred_element_type=F32) * SCALE
        live = (pos_v < jnp.concatenate(limits, axis=0)) & (owner_v == jnp.concatenate(requests, axis=0))
        top = jnp.max(jnp.where(live, scores, NEG), axis=1, keepdims=True)
        weights = jnp.where(live, jnp.exp(scores - top), 0.0)
        total = jnp.sum(weights, axis=1, keepdims=True)
        value = jnp.dot(weights.astype(BF16), page_all[:, 0:LAT], preferred_element_type=F32)
        return {k: (top[i * HH:(i + 1) * HH], total[i * HH:(i + 1) * HH], value[i * HH:(i + 1) * HH])
                for i, k in enumerate(members)}

    def send_partial(k, part):
        top, total, value = part
        stat_out[k] = jnp.concatenate(
            [jnp.sum(jnp.where(lane32 == row32, column, 0.0), axis=0, keepdims=True) for column in (top, total)], axis=0)
        for i in range(4):
            rows = slice(i * 8, (i + 1) * 8)
            part_out[k, i] = jnp.concatenate([value[rows, 0:256], value[rows, 256:512]], axis=0).astype(BF16)
        at = min(k, 1)
        for i in range(4):
            zz = parity * 4 + i

            def away():
                peer = (lax.rem(g + (GRP - k), GRP), zz * NS + s)
                remote(stat_out.at[k], stat_in.at[k, z], ts_sem.at[at], tr_sem.at[k], peer)
                remote(part_out.at[k, i], part_in.at[k, z], ps_sem.at[at], pr_sem.at[k], peer)

            if k == 0:
                pl.when(zz != z)(away)

                @pl.when(zz == z)
                def _():
                    pltpu.make_async_copy(stat_out.at[k], stat_in.at[k, z], tr_sem.at[k]).start()
                    pltpu.make_async_copy(part_out.at[k, i], part_in.at[k, z], pr_sem.at[k]).start()
            else:
                away()

    for at, members in enumerate(((1, 7, 0), (2, 6), (3, 5, 4))):
        if at:
            take_meta(at)
        take_queries(at)
        done = partials(members)
        pl.semaphore_wait(in_sem.at[2 + at], len(groups[at]))
        for k in members:
            send_partial(k, done[k])

    odd = lax.rem(g + z // 4, 2)
    sources = [even_k + odd * (odd_k - even_k) for even_k, odd_k in ((0, 1), (2, 7), (6, 3), (4, 5))]
    mine = lane64 == lax.rem(z, 4) * 8 + lax.broadcasted_iota(jnp.int32, (HEADS, 128), 0) % 8
    tops, totals = [], []
    for k in sources:
        take(stat_in.at[k], tr_sem.at[k])
        take(part_in.at[k], pr_sem.at[k])
        for at, columns in enumerate((tops, totals)):
            spread = jnp.broadcast_to(stat_in[k, :, at:at + 1, :], (NZ, 8, 128)).reshape(HEADS, 128)
            columns.append(jnp.sum(jnp.where(mine, spread, 0.0), axis=1, keepdims=True))
    best = tops[0]
    for top in tops[1:]:
        best = jnp.maximum(best, top)
    factors = [jnp.exp(top - best) for top in tops]
    denominator = 0.0
    for factor, total in zip(factors, totals):
        denominator = denominator + factor * total
    scale = 1.0 / denominator
    factors = [factor * scale for factor in factors]
    for j in range(4):
        block = 0.0
        for k, factor in zip(sources, factors):
            both = part_in[k, :, :, j % 2 * 128:j % 2 * 128 + 128].astype(F32)
            block = block + factor * both[:, j // 2 * 8:j // 2 * 8 + 8].reshape(HEADS, 128)
        lat[j, 0:HEADS, :] = block

    for xx in range(NX):
        for core in range(2):
            quarters = [lat[j, pl.ds(xx * 2 + core, NZ, stride=NS), :] for j in range(4)]
            c2_out[xx, core * 16:(core + 1) * 16, :] = jnp.concatenate(
                [jnp.concatenate(quarters[0:2], axis=1), jnp.concatenate(quarters[2:4], axis=1)], axis=0).astype(BF16)
    pl.semaphore_wait(in_sem.at[8], 2)
    for k in order:
        to = lax.rem(s + k, NS)
        remote(c2_out.at[to // 2], c2_in.at[s], c2s_sem.at[0], c2r_sem.at[0], (g, z * NS + to))
    pltpu.make_async_copy(c2_out.at[x], c2_in.at[s], c2r_sem.at[0]).start()
    vup_load.wait()
    take(vup.at[0], vr_sem.at[0])
    take(c2_in, c2r_sem.at[0])

    blocks = [[], []]
    for dx in range(NX):
        for core in range(2):
            both = c2_in[lax.rem(x + dx, NX) * 2 + core].astype(F32)
            for head in range(2):
                blocks[head].append(jnp.concatenate([both[head * 16:head * 16 + 8], both[head * 16 + 8:head * 16 + 16]], axis=1))
    head_value = jnp.concatenate(
        [jnp.dot(jnp.concatenate(blocks[head], axis=0).astype(BF16), vup[head], preferred_element_type=F32) for head in range(2)],
        axis=1).astype(BF16)

    oproj_load.wait()
    take(oproj.at[0], wr_sem.at[0])

    def product(first, count):
        cols = slice(first * 128, (first + count) * 128)
        return jnp.dot(head_value, oproj[:, :, cols].reshape(2 * VDIM, count * 128), preferred_element_type=F32)

    for n, (first, count) in enumerate(CHUNKS):
        both = product(first, count)
        own_f[:, first * 128:(first + count) * 128] = both[0:16]
        for dx in (2, 1, 3):
            cols = slice(first * 128, (first + count) * 128)
            e2_out[dx, :, cols] = both[dx * 16:(dx + 1) * 16].astype(BF16)
            peer = (g, z * NS + lax.rem(x + dx, NX) * 2 + c)
            remote(e2_out.at[dx, :, cols], e2_in.at[dx, :, cols], e2s_sem.at[n], e2r_sem.at[n], peer)
        if n == 0:
            both = product(LAST, LT)
            for t in range(LT):
                f1_f[t * HEADS:(t + 1) * HEADS, :] = both[:, t * 128:(t + 1) * 128]
            for zz in range(NZ):
                f1_out[zz] = f1_f[pl.ds(zz, LT * 8, stride=8), :].astype(BF16)
            for k in order:
                remote(f1_out.at[lax.rem(z + k, NZ)], f1_in.at[k], f1s_sem.at[0], f1r_sem.at[0], z_peer(k))

    for n, (first, count) in enumerate(CHUNKS):
        cols = slice(first * 128, (first + count) * 128)
        take(e2_in.at[1:NX, :, cols], e2r_sem.at[n])
        total = own_f[:, cols]
        for dx in (1, 3, 2):
            total = total + e2_in[dx, :, cols].astype(F32)
        for t in range(count):
            e3_f[n, t * 16:(t + 1) * 16, :] = total[:, t * 128:(t + 1) * 128]
        for zz in range(NZ):
            for core in range(2):
                rows = e3_f[n, pl.ds(core * 8 + zz, count, stride=16), :]
                e3_out[n, zz, core] = jnp.concatenate([rows, jnp.zeros((16 - count, 128), F32)], axis=0).astype(BF16)
        for k in order:
            to = lax.rem(z + k, NZ)
            for core in range(2):
                remote(e3_out.at[n, to, core], e3_in.at[n, c, k], e3s_sem.at[n], e3r_sem.at[n], (g, to * NS + x * 2 + core))
        remote(e3_out.at[n, z, 1 - c], e3_in.at[n, c, 0], e3s_sem.at[n], e3r_sem.at[n], core_peer)
        pltpu.make_async_copy(e3_out.at[n, z, c], e3_in.at[n, c, 0], e3r_sem.at[n]).start()

    take(f1_in.at[1:NZ], f1r_sem.at[0])
    total = f1_out[z].astype(F32)
    for k in order:
        total = total + f1_in[k].astype(F32)
    f2_f[0:80, :] = total
    for dx in (2, 1, 3, 0):
        for core in range(2):
            f2_out[dx, core] = jnp.concatenate([f2_f[pl.ds(dx * 2 + core, 10, stride=8), :], jnp.zeros((6, 128), F32)], axis=0).astype(BF16)
    for dx in (2, 1, 3):
        for core in range(2):
            peer = (g, z * NS + lax.rem(x + dx, NX) * 2 + core)
            remote(f2_out.at[dx, core], f2_in.at[c, dx], f2s_sem.at[0], f2r_sem.at[0], peer)
    remote(f2_out.at[0, 1 - c], f2_in.at[c, 0], f2s_sem.at[0], f2r_sem.at[0], core_peer)
    pltpu.make_async_copy(f2_out.at[0, c], f2_in.at[c, 0], f2r_sem.at[0]).start()

    def put(core, first, count, total):
        for t in range(count):
            at = core * HALF + (first + t) * 128
            row_f[:, at:at + 128] = total[t:t + 1]

    for n, (first, count) in enumerate(CHUNKS):
        take(e3_in.at[n], e3r_sem.at[n])
        for core in range(2):
            put(core, first, count, jnp.sum(e3_in[n, core].astype(F32), axis=0))
    take(f2_in, f2r_sem.at[0])
    for core in range(2):
        put(core, LAST, LT, jnp.sum(f2_in[core].astype(F32), axis=0))
    out_ref[...] = row_f[...].astype(BF16)

    take(q_in.at[0:7], qs_sem.at[0])
    take(meta_in.at[0:7], ms_sem.at[0])
    take(rope_in.at[0:7], rs_sem.at[0])
    take(pages.at[4:8, :, 0:LAT], gs_sem.at[0])
    take(prope_out, gs_sem.at[1])
    take(part_out.at[1:GRP], ps_sem.at[1])
    take(stat_in.at[1:GRP, 0:4], ts_sem.at[1])

    @pl.when(z // 4 == parity)
    def _():
        take(part_out.at[0, 0:3], ps_sem.at[0])
        take(stat_in.at[0, 0:3], ts_sem.at[0])

    @pl.when(z // 4 != parity)
    def _():
        take(part_out.at[0], ps_sem.at[0])
        take(stat_in.at[0, 0:4], ts_sem.at[0])

    take(c2_in.at[1:NS], c2s_sem.at[0])
    take(vup.at[0], vs_sem.at[0])
    take(oproj.at[0], ws_sem.at[0])
    for n, (first, count) in enumerate(CHUNKS):
        take(e2_out.at[1:NX, :, first * 128:(first + count) * 128], e2s_sem.at[n])
        take(sent.at[0:15], e3s_sem.at[n])
    take(f1_out.at[1:NZ], f1s_sem.at[0])
    take(sent.at[0:7], f2s_sem.at[0])


def body(queries, lengths, pages, slot_owner, slot_page, value_up, out_proj):
    any_spec = pl.BlockSpec(memory_space=pl.ANY)
    dma = pltpu.SemaphoreType.DMA
    return pl.pallas_call(
        kernel,
        out_shape=jax.ShapeDtypeStruct((1, D), BF16),
        in_specs=[any_spec] * 7,
        out_specs=pl.BlockSpec(memory_space=pltpu.VMEM),
        scratch_shapes=[
            pltpu.SMEM((1,), jnp.int32),
            pltpu.SMEM((POOL,), jnp.int32),
            pltpu.SMEM((POOL,), jnp.int32),
            pltpu.VMEM((HEADS, CACHE), BF16),
            pltpu.VMEM((GRP, HH, LAT), BF16),
            pltpu.VMEM((2, 16, 128), BF16),
            pltpu.VMEM((GRP, 16, 128), BF16),
            pltpu.VMEM((2, PAGE, 128), BF16),
            pltpu.VMEM((2, PAGE, 128), BF16),
            pltpu.VMEM((1, 128), jnp.int32),
            pltpu.VMEM((GRP, 1, 128), jnp.int32),
            pltpu.VMEM((2 * POOL, PAGE, CACHE), BF16),
            pltpu.VMEM((2, LAT, VDIM), BF16),
            pltpu.VMEM((2, VDIM, HALF), BF16),
            pltpu.VMEM((GRP, 4, 16, 256), BF16),
            pltpu.VMEM((GRP, NZ, 16, 256), BF16),
            pltpu.VMEM((GRP, 2, 128), F32),
            pltpu.VMEM((GRP, NZ, 2, 128), F32),
            pltpu.VMEM((1, D), F32),
            pltpu.VMEM((4, HEADS + 8, 128), F32),
            pltpu.VMEM((NX, 32, 256), BF16),
            pltpu.VMEM((NS, 32, 256), BF16),
            pltpu.VMEM((16, LAST * 128), F32),
            pltpu.VMEM((NX, 16, LAST * 128), BF16),
            pltpu.VMEM((NX, 16, LAST * 128), BF16),
            pltpu.VMEM((2, 14 * 16 + 16, 128), F32),
            pltpu.VMEM((2, NZ, 2, 16, 128), BF16),
            pltpu.VMEM((2, 2, NZ, 16, 128), BF16),
            pltpu.VMEM((LT * HEADS + 8, 128), F32),
            pltpu.VMEM((NZ, 80, 128), BF16),
            pltpu.VMEM((NZ, 80, 128), BF16),
            pltpu.VMEM((80+8, 128), F32),
            pltpu.VMEM((NX, 2, 16, 128), BF16),
            pltpu.VMEM((2, NX, 16, 128), BF16),
            pltpu.VMEM((16, 16, 128), BF16),
            dma((7,)), pltpu.SemaphoreType.REGULAR((9,)),
            dma((1,)), dma((3,)), dma((2,)), dma((2,)), dma((1,)), dma((3,)), dma((1,)), dma((3,)),
            dma((2,)), dma((GRP,)), dma((2,)), dma((GRP,)),
            dma((1,)), dma((1,)), dma((1,)), dma((1,)), dma((1,)), dma((1,)),
            dma((2,)), dma((2,)), dma((2,)), dma((2,)), dma((1,)), dma((1,)), dma((1,)), dma((1,)),
        ],
        compiler_params=pltpu.CompilerParams(
            collective_id=0, has_side_effects=True, vmem_limit_bytes=60 * 1024 * 1024),
    )(queries, lengths, pages, slot_owner, slot_page, value_up, out_proj)


def solution(mesh):
    in_specs = (
        P(("grp", "dev"), None, None),
        P(("grp", "dev")),
        P(("grp", "dev"), None, None),
        P(("grp", "dev")),
        P(("grp", "dev")),
        P("dev", None, None),
        P("dev", None),
    )
    out_specs = P(("grp", "dev"), None)
    return jax.shard_map(body, mesh=mesh, in_specs=in_specs, out_specs=out_specs, check_vma=False)
```

```python
import jax
import jax.numpy as jnp
from jax import lax
from jax.experimental import pallas as pl
from jax.experimental.pallas import tpu as pltpu
from jax.sharding import PartitionSpec as P

MESH = pl.DeviceIdType.MESH
F32 = jnp.float32
BF16 = jnp.bfloat16

ROPE = 64
NOPE = 128
SCALE = (NOPE + ROPE) ** -0.5
NEG = -1e30

GRP = 8
NZ = 8
NS = 8
NX = 4
HEADS = 64
LAT = 512
CACHE = 576
HH = HEADS // 2
PAGE = 64
POOL = 4
TOK = 2 * POOL * PAGE
VDIM = 128
D = 7168
HALF = D // 2
TILES = D // 128
CHUNKS = ((0, 9), (9, 9))
LAST, LT = 18, 10


def kernel(q_hbm, len_hbm, pages_hbm, owner_hbm, page_hbm, vup_hbm, oproj_hbm, out_ref,
           len_ref, owner_ref, page_ref, q_own, q_in, rope_own, rope_in, prope_out, prope_in, meta_own, meta_in, pages, vup, oproj, part_out, part_in, stat_out, stat_in,
           row_f, lat, c2_out, c2_in, own_f, e2_out, e2_in, e3_f, e3_out, e3_in, f1_f, f1_out, f1_in, f2_f, f2_out, f2_in, sent,
           loc_sem, in_sem, ms_sem, mr_sem, gs_sem, gr_sem, qs_sem, qr_sem, rs_sem, rr_sem, ps_sem, pr_sem, ts_sem, tr_sem,
           c2s_sem, c2r_sem, vs_sem, vr_sem, ws_sem, wr_sem, e2s_sem, e2r_sem, e3s_sem, e3r_sem, f1s_sem, f1r_sem, f2s_sem, f2r_sem):
    g = lax.axis_index("grp")
    d = lax.axis_index("dev")
    z = d // NS
    s = d % NS
    x = s // 2
    c = s % 2

    def grp_peer(k):
        return (lax.rem(g + k, GRP), d)

    def z_peer(k):
        return (g, lax.rem(z + k, NZ) * NS + s)

    def s_peer(k):
        return (g, z * NS + lax.rem(s + k, NS))

    barrier = pltpu.get_barrier_semaphore()
    core_peer = (g, z * NS + x * 2 + (1 - c))
    near = [grp_peer(1), grp_peer(7), z_peer(1), z_peer(7), s_peer(2), s_peer(6), core_peer]
    for peer in near:
        pl.semaphore_signal(barrier, inc=1, device_id=peer, device_id_type=MESH)

    q_load = pltpu.make_async_copy(q_hbm.at[0], q_own, loc_sem.at[0])
    q_load.start()
    number_loads = [pltpu.make_async_copy(src, dst, loc_sem.at[4 + at]) for at, (src, dst) in
                    enumerate(((len_hbm, len_ref), (owner_hbm, owner_ref), (page_hbm, page_ref)))]
    for load in number_loads:
        load.start()
    pages_load = pltpu.make_async_copy(pages_hbm, pages.at[0:POOL], loc_sem.at[1])
    pages_load.start()
    vup_load = pltpu.make_async_copy(vup_hbm.at[0], vup.at[c], loc_sem.at[2])
    vup_load.start()
    def columns(core):
        return oproj_hbm.at[:, pl.ds(pl.multiple_of(core * HALF, 128), HALF)]

    oproj_load = pltpu.make_async_copy(columns(c), oproj.at[c], loc_sem.at[3])
    oproj_load.start()

    def tell(sem, peers):
        for peer in peers:
            pl.semaphore_signal(sem, inc=1, device_id=peer, device_id_type=MESH)

    def remote(src, dst, send, recv, peer):
        copy = pltpu.make_async_remote_copy(
            src_ref=src, dst_ref=dst, send_sem=send, recv_sem=recv,
            device_id=peer, device_id_type=MESH)
        copy.start()
        return copy

    def take(ref, sem):
        pltpu.make_async_copy(ref, ref, sem).wait()

    parity = lax.rem(g, 2)
    slots = {1: 0, 7: 1, 2: 2, 6: 3, 3: 4, 5: 5, 4: 6}
    groups = ((1, 7), (2, 6), (3, 5, 4))

    def send_queries(at):
        for k in groups[at]:
            remote(q_own.at[pl.ds(lax.rem(g + k, 2) * HH, HH), 0:LAT], q_in.at[slots[k]], qs_sem.at[0], qr_sem.at[at], grp_peer(k))

    def send_sides(at):
        for k in groups[at]:
            remote(meta_own, meta_in.at[slots[k]], ms_sem.at[0], mr_sem.at[at], grp_peer(k))
            remote(rope_own.at[lax.rem(g + k, 2)], rope_in.at[slots[k]], rs_sem.at[0], rr_sem.at[at], grp_peer(k))

    def take_queries(at):
        first, count = slots[groups[at][0]], len(groups[at])
        take(rope_in.at[first:first + count], rr_sem.at[at])
        take(q_in.at[first:first + count], qr_sem.at[at])

    def take_meta(at):
        first, count = slots[groups[at][0]], len(groups[at])
        take(meta_in.at[first:first + count], mr_sem.at[at])

    q_load.wait()
    pages_load.wait()
    for load in number_loads:
        load.wait()
    lane = lax.broadcasted_iota(jnp.int32, (1, 128), 1)
    meta = jnp.where(lane == 0, len_ref[0], 0)
    for i in range(POOL):
        meta = jnp.where(lane == 1 + i, owner_ref[i], meta)
        meta = jnp.where(lane == 1 + POOL + i, page_ref[i], meta)
    meta_own[...] = meta
    for half in range(2):
        rope = q_own[half * HH:(half + 1) * HH, LAT:CACHE].astype(F32)
        rope_own[half] = jnp.concatenate([rope[0:16], rope[16:32]], axis=1).astype(BF16)
    for side in range(2):
        rope = [pages[2 * side + i, :, LAT:CACHE].astype(F32) for i in range(2)]
        prope_out[side] = jnp.concatenate(rope, axis=1).astype(BF16)

    pl.semaphore_wait(barrier, 7)
    tell(in_sem.at[0], [grp_peer(1), grp_peer(7)])
    tell(in_sem.at[1], [z_peer(1), z_peer(7)])
    tell(in_sem.at[6], [s_peer(2), s_peer(6), core_peer])
    send_queries(0)
    send_sides(0)
    remote(pages.at[0:2, :, 0:LAT], pages.at[4:6, :, 0:LAT], gs_sem.at[0], gr_sem.at[0], grp_peer(1))
    remote(pages.at[2:4, :, 0:LAT], pages.at[6:8, :, 0:LAT], gs_sem.at[0], gr_sem.at[0], grp_peer(7))
    remote(prope_out.at[0], prope_in.at[0], gs_sem.at[1], gr_sem.at[1], grp_peer(1))
    remote(prope_out.at[1], prope_in.at[1], gs_sem.at[1], gr_sem.at[1], grp_peer(7))
    remote(vup_hbm.at[0], vup.at[c], vs_sem.at[0], vr_sem.at[0], core_peer)
    remote(columns(1 - c), oproj.at[c], ws_sem.at[0], wr_sem.at[0], core_peer)
    pl.semaphore_wait(in_sem.at[0], 2)
    tell(in_sem.at[5], [grp_peer(2), grp_peer(6)])
    send_queries(1)
    send_sides(1)
    pl.semaphore_wait(in_sem.at[1], 2)
    tell(in_sem.at[7], [z_peer(2), z_peer(6)])
    pl.semaphore_wait(in_sem.at[6], 3)
    tell(in_sem.at[8], [s_peer(2), s_peer(6)])
    pl.semaphore_wait(in_sem.at[5], 2)
    send_queries(2)
    send_sides(2)
    pl.semaphore_wait(in_sem.at[7], 2)
    for at in range(3):
        tell(in_sem.at[2 + at], [grp_peer(k) for k in groups[at]])

    order = (4, 3, 5, 2, 6, 1, 7)
    take_meta(0)
    take(prope_in, gr_sem.at[1])
    take(pages.at[4:8, :, 0:LAT], gr_sem.at[0])
    for side in range(2):
        rope = prope_in[side].astype(F32)
        for i in range(2):
            pages[4 + 2 * side + i, :, LAT:CACHE] = rope[:, i * ROPE:(i + 1) * ROPE].astype(BF16)
    token = lax.broadcasted_iota(jnp.int32, (1, TOK), 1)
    slot = token // PAGE
    owner_v = jnp.zeros((1, TOK), jnp.int32)
    first_v = jnp.zeros((1, TOK), jnp.int32)
    rows = [(meta, i) for i in range(POOL)] + [(meta_in[0], 0), (meta_in[0], 1), (meta_in[1], 2), (meta_in[1], 3)]
    for i, (row, at) in enumerate(rows):
        owner_v = jnp.where(slot == i, row[:, 1 + at:2 + at], owner_v)
        first_v = jnp.where(slot == i, row[:, 1 + POOL + at:2 + POOL + at], first_v)
    pos_v = first_v * PAGE + token % PAGE
    lane64 = lax.broadcasted_iota(jnp.int32, (HEADS, 128), 1)
    lane32 = lax.broadcasted_iota(jnp.int32, (HH, 128), 1)
    row32 = lax.broadcasted_iota(jnp.int32, (HH, 128), 0)

    def partials(members):
        page_all = pages[...].reshape(TOK, CACHE)
        queries, limits, requests = [], [], []
        for k in members:
            row = meta if k == 0 else meta_in[slots[k]]
            if k == 0:
                queries.append(q_own[pl.ds(parity * HH, HH), :])
            else:
                rope = rope_in[slots[k]].astype(F32)
                rope = jnp.concatenate([rope[:, 0:ROPE], rope[:, ROPE:2 * ROPE]], axis=0).astype(BF16)
                queries.append(jnp.concatenate([q_in[slots[k]], rope], axis=1))
            limits.append(jnp.broadcast_to(row[:, 0:1], (HH, 1)))
            requests.append(jnp.full((HH, 1), lax.rem(g + (GRP - k), GRP), jnp.int32))
        query = jnp.concatenate(queries, axis=0)
        scores = lax.dot_general(query, page_all, (((1,), (1,)), ((), ())),
                                 preferred_element_type=F32) * SCALE
        live = (pos_v < jnp.concatenate(limits, axis=0)) & (owner_v == jnp.concatenate(requests, axis=0))
        top = jnp.max(jnp.where(live, scores, NEG), axis=1, keepdims=True)
        weights = jnp.where(live, jnp.exp(scores - top), 0.0)
        total = jnp.sum(weights, axis=1, keepdims=True)
        value = jnp.dot(weights.astype(BF16), page_all[:, 0:LAT], preferred_element_type=F32)
        return {k: (top[i * HH:(i + 1) * HH], total[i * HH:(i + 1) * HH], value[i * HH:(i + 1) * HH])
                for i, k in enumerate(members)}

    def send_partial(k, part):
        top, total, value = part
        stat_out[k] = jnp.concatenate(
            [jnp.sum(jnp.where(lane32 == row32, column, 0.0), axis=0, keepdims=True) for column in (top, total)], axis=0)
        for i in range(4):
            rows = slice(i * 8, (i + 1) * 8)
            part_out[k, i] = jnp.concatenate([value[rows, 0:256], value[rows, 256:512]], axis=0).astype(BF16)
        at = min(k, 1)
        for i in range(4):
            zz = parity * 4 + i

            def away():
                peer = (lax.rem(g + (GRP - k), GRP), zz * NS + s)
                remote(stat_out.at[k], stat_in.at[k, z], ts_sem.at[at], tr_sem.at[k], peer)
                remote(part_out.at[k, i], part_in.at[k, z], ps_sem.at[at], pr_sem.at[k], peer)

            if k == 0:
                pl.when(zz != z)(away)

                @pl.when(zz == z)
                def _():
                    pltpu.make_async_copy(stat_out.at[k], stat_in.at[k, z], tr_sem.at[k]).start()
                    pltpu.make_async_copy(part_out.at[k, i], part_in.at[k, z], pr_sem.at[k]).start()
            else:
                away()

    for at, members in enumerate(((1, 7, 0), (2, 6), (3, 5, 4))):
        if at:
            take_meta(at)
        take_queries(at)
        done = partials(members)
        pl.semaphore_wait(in_sem.at[2 + at], len(groups[at]))
        for k in members:
            send_partial(k, done[k])

    odd = lax.rem(g + z // 4, 2)
    sources = [even_k + odd * (odd_k - even_k) for even_k, odd_k in ((0, 1), (2, 7), (6, 3), (4, 5))]
    mine = lane64 == lax.rem(z, 4) * 8 + lax.broadcasted_iota(jnp.int32, (HEADS, 128), 0) % 8
    state = None
    for at, k in enumerate(sources):
        take(stat_in.at[k], tr_sem.at[k])
        take(part_in.at[k], pr_sem.at[k])
        top, total = [jnp.sum(jnp.where(mine, jnp.broadcast_to(stat_in[k, :, i:i + 1, :], (NZ, 8, 128)).reshape(HEADS, 128), 0.0),
                              axis=1, keepdims=True) for i in range(2)]
        if at == 0:
            old_factor, factor = None, 1.0
            state = (top, total)
        else:
            best = jnp.maximum(state[0], top)
            old_factor, factor = jnp.exp(state[0] - best), jnp.exp(top - best)
            state = (best, old_factor * state[1] + factor * total)
            if at == 3:
                scale = 1.0 / state[1]
                old_factor, factor = old_factor * scale, factor * scale
        for j in range(4):
            both = part_in[k, :, :, j % 2 * 128:j % 2 * 128 + 128].astype(F32)
            block = both[:, j // 2 * 8:j // 2 * 8 + 8].reshape(HEADS, 128)
            lat[j, 0:HEADS, :] = block if at == 0 else old_factor * lat[j, 0:HEADS, :] + factor * block

    for xx in range(NX):
        for core in range(2):
            quarters = [lat[j, pl.ds(xx * 2 + core, NZ, stride=NS), :] for j in range(4)]
            c2_out[xx, core * 16:(core + 1) * 16, :] = jnp.concatenate(
                [jnp.concatenate(quarters[0:2], axis=1), jnp.concatenate(quarters[2:4], axis=1)], axis=0).astype(BF16)
    pl.semaphore_wait(in_sem.at[8], 2)
    for k in order:
        to = lax.rem(s + k, NS)
        remote(c2_out.at[to // 2], c2_in.at[s], c2s_sem.at[0], c2r_sem.at[0], (g, z * NS + to))
    pltpu.make_async_copy(c2_out.at[x], c2_in.at[s], c2r_sem.at[0]).start()
    vup_load.wait()
    take(vup.at[0], vr_sem.at[0])
    take(c2_in, c2r_sem.at[0])

    blocks = [[], []]
    for dx in range(NX):
        for core in range(2):
            both = c2_in[lax.rem(x + dx, NX) * 2 + core].astype(F32)
            for head in range(2):
                blocks[head].append(jnp.concatenate([both[head * 16:head * 16 + 8], both[head * 16 + 8:head * 16 + 16]], axis=1))
    head_value = jnp.concatenate(
        [jnp.dot(jnp.concatenate(blocks[head], axis=0).astype(BF16), vup[head], preferred_element_type=F32) for head in range(2)],
        axis=1).astype(BF16)

    oproj_load.wait()
    take(oproj.at[0], wr_sem.at[0])

    def product(first, count):
        cols = slice(first * 128, (first + count) * 128)
        return jnp.dot(head_value, oproj[:, :, cols].reshape(2 * VDIM, count * 128), preferred_element_type=F32)

    for n, (first, count) in enumerate(CHUNKS):
        both = product(first, count)
        own_f[:, first * 128:(first + count) * 128] = both[0:16]
        for dx in (2, 1, 3):
            cols = slice(first * 128, (first + count) * 128)
            e2_out[dx, :, cols] = both[dx * 16:(dx + 1) * 16].astype(BF16)
            peer = (g, z * NS + lax.rem(x + dx, NX) * 2 + c)
            remote(e2_out.at[dx, :, cols], e2_in.at[dx, :, cols], e2s_sem.at[n], e2r_sem.at[n], peer)
        if n == 0:
            both = product(LAST, LT)
            for t in range(LT):
                f1_f[t * HEADS:(t + 1) * HEADS, :] = both[:, t * 128:(t + 1) * 128]
            for zz in range(NZ):
                f1_out[zz] = f1_f[pl.ds(zz, LT * 8, stride=8), :].astype(BF16)
            for k in order:
                remote(f1_out.at[lax.rem(z + k, NZ)], f1_in.at[k], f1s_sem.at[0], f1r_sem.at[0], z_peer(k))

    for n, (first, count) in enumerate(CHUNKS):
        cols = slice(first * 128, (first + count) * 128)
        take(e2_in.at[1:NX, :, cols], e2r_sem.at[n])
        total = own_f[:, cols]
        for dx in (1, 3, 2):
            total = total + e2_in[dx, :, cols].astype(F32)
        for t in range(count):
            e3_f[n, t * 16:(t + 1) * 16, :] = total[:, t * 128:(t + 1) * 128]
        for zz in range(NZ):
            for core in range(2):
                rows = e3_f[n, pl.ds(core * 8 + zz, count, stride=16), :]
                e3_out[n, zz, core] = jnp.concatenate([rows, jnp.zeros((16 - count, 128), F32)], axis=0).astype(BF16)
        for k in order:
            to = lax.rem(z + k, NZ)
            for core in range(2):
                remote(e3_out.at[n, to, core], e3_in.at[n, c, k], e3s_sem.at[n], e3r_sem.at[n], (g, to * NS + x * 2 + core))
        remote(e3_out.at[n, z, 1 - c], e3_in.at[n, c, 0], e3s_sem.at[n], e3r_sem.at[n], core_peer)
        pltpu.make_async_copy(e3_out.at[n, z, c], e3_in.at[n, c, 0], e3r_sem.at[n]).start()

    take(f1_in.at[1:NZ], f1r_sem.at[0])
    total = f1_out[z].astype(F32)
    for k in order:
        total = total + f1_in[k].astype(F32)
    f2_f[0:80, :] = total
    for dx in (2, 1, 3, 0):
        for core in range(2):
            f2_out[dx, core] = jnp.concatenate([f2_f[pl.ds(dx * 2 + core, 10, stride=8), :], jnp.zeros((6, 128), F32)], axis=0).astype(BF16)
    for dx in (2, 1, 3):
        for core in range(2):
            peer = (g, z * NS + lax.rem(x + dx, NX) * 2 + core)
            remote(f2_out.at[dx, core], f2_in.at[c, dx], f2s_sem.at[0], f2r_sem.at[0], peer)
    remote(f2_out.at[0, 1 - c], f2_in.at[c, 0], f2s_sem.at[0], f2r_sem.at[0], core_peer)
    pltpu.make_async_copy(f2_out.at[0, c], f2_in.at[c, 0], f2r_sem.at[0]).start()

    def put(core, first, count, total):
        for t in range(count):
            at = core * HALF + (first + t) * 128
            row_f[:, at:at + 128] = total[t:t + 1]

    for n, (first, count) in enumerate(CHUNKS):
        take(e3_in.at[n], e3r_sem.at[n])
        for core in range(2):
            put(core, first, count, jnp.sum(e3_in[n, core].astype(F32), axis=0))
    take(f2_in, f2r_sem.at[0])
    for core in range(2):
        put(core, LAST, LT, jnp.sum(f2_in[core].astype(F32), axis=0))
    out_ref[...] = row_f[...].astype(BF16)

    take(q_in.at[0:7], qs_sem.at[0])
    take(meta_in.at[0:7], ms_sem.at[0])
    take(rope_in.at[0:7], rs_sem.at[0])
    take(pages.at[4:8, :, 0:LAT], gs_sem.at[0])
    take(prope_out, gs_sem.at[1])
    take(part_out.at[1:GRP], ps_sem.at[1])
    take(stat_in.at[1:GRP, 0:4], ts_sem.at[1])

    @pl.when(z // 4 == parity)
    def _():
        take(part_out.at[0, 0:3], ps_sem.at[0])
        take(stat_in.at[0, 0:3], ts_sem.at[0])

    @pl.when(z // 4 != parity)
    def _():
        take(part_out.at[0], ps_sem.at[0])
        take(stat_in.at[0, 0:4], ts_sem.at[0])

    take(c2_in.at[1:NS], c2s_sem.at[0])
    take(vup.at[0], vs_sem.at[0])
    take(oproj.at[0], ws_sem.at[0])
    for n, (first, count) in enumerate(CHUNKS):
        take(e2_out.at[1:NX, :, first * 128:(first + count) * 128], e2s_sem.at[n])
        take(sent.at[0:15], e3s_sem.at[n])
    take(f1_out.at[1:NZ], f1s_sem.at[0])
    take(sent.at[0:7], f2s_sem.at[0])


def body(queries, lengths, pages, slot_owner, slot_page, value_up, out_proj):
    any_spec = pl.BlockSpec(memory_space=pl.ANY)
    dma = pltpu.SemaphoreType.DMA
    return pl.pallas_call(
        kernel,
        out_shape=jax.ShapeDtypeStruct((1, D), BF16),
        in_specs=[any_spec] * 7,
        out_specs=pl.BlockSpec(memory_space=pltpu.VMEM),
        scratch_shapes=[
            pltpu.SMEM((1,), jnp.int32),
            pltpu.SMEM((POOL,), jnp.int32),
            pltpu.SMEM((POOL,), jnp.int32),
            pltpu.VMEM((HEADS, CACHE), BF16),
            pltpu.VMEM((GRP, HH, LAT), BF16),
            pltpu.VMEM((2, 16, 128), BF16),
            pltpu.VMEM((GRP, 16, 128), BF16),
            pltpu.VMEM((2, PAGE, 128), BF16),
            pltpu.VMEM((2, PAGE, 128), BF16),
            pltpu.VMEM((1, 128), jnp.int32),
            pltpu.VMEM((GRP, 1, 128), jnp.int32),
            pltpu.VMEM((2 * POOL, PAGE, CACHE), BF16),
            pltpu.VMEM((2, LAT, VDIM), BF16),
            pltpu.VMEM((2, VDIM, HALF), BF16),
            pltpu.VMEM((GRP, 4, 16, 256), BF16),
            pltpu.VMEM((GRP, NZ, 16, 256), BF16),
            pltpu.VMEM((GRP, 2, 128), F32),
            pltpu.VMEM((GRP, NZ, 2, 128), F32),
            pltpu.VMEM((1, D), F32),
            pltpu.VMEM((4, HEADS + 8, 128), F32),
            pltpu.VMEM((NX, 32, 256), BF16),
            pltpu.VMEM((NS, 32, 256), BF16),
            pltpu.VMEM((16, LAST * 128), F32),
            pltpu.VMEM((NX, 16, LAST * 128), BF16),
            pltpu.VMEM((NX, 16, LAST * 128), BF16),
            pltpu.VMEM((2, 14 * 16 + 16, 128), F32),
            pltpu.VMEM((2, NZ, 2, 16, 128), BF16),
            pltpu.VMEM((2, 2, NZ, 16, 128), BF16),
            pltpu.VMEM((LT * HEADS + 8, 128), F32),
            pltpu.VMEM((NZ, 80, 128), BF16),
            pltpu.VMEM((NZ, 80, 128), BF16),
            pltpu.VMEM((80+8, 128), F32),
            pltpu.VMEM((NX, 2, 16, 128), BF16),
            pltpu.VMEM((2, NX, 16, 128), BF16),
            pltpu.VMEM((16, 16, 128), BF16),
            dma((7,)), pltpu.SemaphoreType.REGULAR((9,)),
            dma((1,)), dma((3,)), dma((2,)), dma((2,)), dma((1,)), dma((3,)), dma((1,)), dma((3,)),
            dma((2,)), dma((GRP,)), dma((2,)), dma((GRP,)),
            dma((1,)), dma((1,)), dma((1,)), dma((1,)), dma((1,)), dma((1,)),
            dma((2,)), dma((2,)), dma((2,)), dma((2,)), dma((1,)), dma((1,)), dma((1,)), dma((1,)),
        ],
        compiler_params=pltpu.CompilerParams(
            collective_id=0, has_side_effects=True, vmem_limit_bytes=60 * 1024 * 1024),
    )(queries, lengths, pages, slot_owner, slot_page, value_up, out_proj)


def solution(mesh):
    in_specs = (
        P(("grp", "dev"), None, None),
        P(("grp", "dev")),
        P(("grp", "dev"), None, None),
        P(("grp", "dev")),
        P(("grp", "dev")),
        P("dev", None, None),
        P("dev", None),
    )
    out_specs = P(("grp", "dev"), None)
    return jax.shard_map(body, mesh=mesh, in_specs=in_specs, out_specs=out_specs, check_vma=False)
```
